32 devices in a mesh: gx: 8 (over y, x, core), gy: 4 (over z).
Axes of the slice: x: 2, y: 2, z: 4, core: 2. Of those that a mesh axis runs over, the one named last changes fastest.
Arguments:
- water_head: float32 [256, 128, 128], P('gx', 'gy'), may hold values from -4 to 4
- conductivity: float32 [256, 128, 128], P('gx', 'gy'), may hold values from 1 to 8
- recharge: float32 [256, 128, 128], P('gx', 'gy'), may hold values from -4 to 4
Outputs:
- next_head: float32 [256, 128, 128], P('gx', 'gy')
The draws below stay inside these ranges and needn't reach their ends.
All inputs are finite; a program needn't handle non-finite values.
Results may differ from the reference program's by a relative error of at most 0.008.
Values sent between devices are 32-bit elements; how exact they have to be, the bound alone decides.
A program may use at most 64 MiB of HBM per device.

```python
import math
import jax
import jax.numpy as jnp
from jax import lax

COEF_Z = 8
COEF_X = 5120
COEF_Y = 5120
NX = 256
NY = 128
NZ = 128


def modal_pattern(key):
    subkeys = jax.random.split(key, 5)
    waves_first = jax.random.randint(subkeys[0], (4,), 1, 9)
    waves_second = jax.random.randint(subkeys[1], (4,), 1, 9)
    waves_third = jax.random.randint(subkeys[2], (4,), 0, 4)
    phases = jax.random.uniform(subkeys[3], (4, 3), jnp.float32, -math.pi, math.pi)
    amplitudes = jax.random.uniform(subkeys[4], (4,), jnp.float32, -0.5, 0.5)
    coord_first = (jnp.arange(NX, dtype=jnp.float32) + 0.5) / NX
    coord_second = (jnp.arange(NY, dtype=jnp.float32) + 0.5) / NY
    coord_third = (jnp.arange(NZ, dtype=jnp.float32) + 0.5) / NZ
    pattern = jnp.zeros((NX, NY, NZ), jnp.float32)
    for term_index in range(4):
        along_first = jnp.cos(2.0 * math.pi * waves_first[term_index].astype(jnp.float32) * coord_first + phases[term_index, 0])
        along_second = jnp.cos(2.0 * math.pi * waves_second[term_index].astype(jnp.float32) * coord_second + phases[term_index, 1])
        along_third = jnp.cos(math.pi * waves_third[term_index].astype(jnp.float32) * coord_third + phases[term_index, 2])
        pattern = pattern + amplitudes[term_index] * along_first[:, None, None] * along_second[None, :, None] * along_third[None, None, :]
    return pattern


def cellwise_noise(key):
    return 0.5 * jnp.clip(jax.random.normal(key, (NX, NY, NZ), jnp.float32), -4.0, 4.0)


def draw_water_head(key, part):
    return modal_pattern(jax.random.fold_in(key, 11)) + cellwise_noise(jax.random.fold_in(key, 12))


def draw_recharge(key, part):
    return modal_pattern(jax.random.fold_in(key, 21)) + cellwise_noise(jax.random.fold_in(key, 22))


def steps_of(stream_key, extent, pieces, low, top_value):
    level, own = 1.0, jax.random.fold_in(stream_key, 6)
    for dim, shards_of in pieces:
        steps = jnp.exp(jax.random.uniform(jax.random.fold_in(own, dim), (shards_of,), jnp.float32, low / len(pieces), top_value / len(pieces)))
        level = level * jnp.repeat(steps, extent[dim] // shards_of).reshape([-1 if axis == dim else 1 for axis in range(len(extent))])
    return level


def setup_inputs(seed: int = 0) -> dict:
    keys = jax.random.split(jax.random.key(seed), 4)
    water_head = draw_water_head(jax.random.fold_in(keys[3], 71), 0)
    conductivity = jnp.clip(jnp.exp(math.log(8.0) - 2.0794415 * jax.random.uniform(keys[1], (NX, NY, NZ), jnp.float32) ** steps_of(keys[1], (NX, NY, NZ), ((0, 8), (1, 4)), -0.2, 0.2)), 1.0, 8.0)
    recharge = draw_recharge(jax.random.fold_in(keys[3], 71), 0)
    return dict(water_head=water_head, conductivity=conductivity, recharge=recharge)


def harmonic(one_side, other_side):
    return 2.0 * one_side * other_side / (one_side + other_side)

def line_solve(link_west, link_east, values):
    beneath = (-link_west).at[..., 0].set(0.0)
    overhead = (-link_east).at[..., -1].set(0.0)
    diagonal = 1.0 + link_west + link_east
    return lax.linalg.tridiagonal_solve(beneath, diagonal, overhead, values[..., None])[..., 0]

def reference(water_head, conductivity, recharge):

    def plane_delta(plane):
        below_index = jnp.maximum(plane - 1, 0).astype(jnp.int32)
        above_index = jnp.minimum(plane + 1, NZ - 1).astype(jnp.int32)
        heads_here = lax.dynamic_index_in_dim(water_head, plane, 2, keepdims=False)
        heads_below = lax.dynamic_index_in_dim(water_head, below_index, 2, keepdims=False)
        heads_above = lax.dynamic_index_in_dim(water_head, above_index, 2, keepdims=False)
        conduct_here = lax.dynamic_index_in_dim(conductivity, plane, 2, keepdims=False)
        conduct_below = lax.dynamic_index_in_dim(conductivity, below_index, 2, keepdims=False)
        conduct_above = lax.dynamic_index_in_dim(conductivity, above_index, 2, keepdims=False)
        source_here = lax.dynamic_index_in_dim(recharge, plane, 2, keepdims=False)
        heads_pad = jnp.pad(heads_here, 1)
        conduct_pad = jnp.pad(conduct_here, 1)
        heads_ew = heads_pad[:, 1:-1]
        conduct_ew = conduct_pad[:, 1:-1]
        east_face = harmonic(conduct_ew[1:-1], conduct_ew[2:])
        west_face = harmonic(conduct_ew[:-2], conduct_ew[1:-1])
        flow_east = east_face * (heads_ew[2:] - heads_ew[1:-1]) - west_face * (heads_ew[1:-1] - heads_ew[:-2])
        heads_ns = heads_pad[1:-1]
        conduct_ns = conduct_pad[1:-1]
        north_face = harmonic(conduct_ns[:, 1:-1], conduct_ns[:, 2:])
        south_face = harmonic(conduct_ns[:, :-2], conduct_ns[:, 1:-1])
        flow_north = north_face * (heads_ns[:, 2:] - heads_ns[:, 1:-1]) - south_face * (heads_ns[:, 1:-1] - heads_ns[:, :-2])
        upper_face = jnp.where(plane < NZ - 1, harmonic(conduct_here, conduct_above), 0.0)
        under_face = jnp.where(plane > 0, harmonic(conduct_below, conduct_here), 0.0)
        flow_depth = upper_face * (heads_above - heads_here) - under_face * (heads_here - heads_below)
        forcing = COEF_X * flow_east + COEF_Y * flow_north + COEF_Z * flow_depth + source_here
        first_delta = line_solve((0.5 * COEF_X * west_face).T, (0.5 * COEF_X * east_face).T, forcing.T).T
        second_delta = line_solve(0.5 * COEF_Y * south_face, 0.5 * COEF_Y * north_face, first_delta)
        return second_delta
    planes = lax.map(plane_delta, jnp.arange(NZ, dtype=jnp.int32))

    def row_result(row_index):
        second_row = lax.dynamic_index_in_dim(planes, row_index, 1, keepdims=False).T
        conduct_row = lax.dynamic_index_in_dim(conductivity, row_index, 0, keepdims=False)
        heads_row = lax.dynamic_index_in_dim(water_head, row_index, 0, keepdims=False)
        conduct_ud = jnp.pad(conduct_row, ((0, 0), (1, 1)))
        upper_face = harmonic(conduct_ud[:, 1:-1], conduct_ud[:, 2:])
        under_face = harmonic(conduct_ud[:, :-2], conduct_ud[:, 1:-1])
        third_delta = line_solve(0.5 * COEF_Z * under_face, 0.5 * COEF_Z * upper_face, second_row)
        return heads_row + third_delta
    return lax.map(row_result, jnp.arange(NX, dtype=jnp.int32))
```

```python
import functools

import jax
import jax.numpy as jnp
from jax import lax
from jax.experimental import pallas as pl
from jax.experimental.pallas import tpu as pltpu
from jax.sharding import PartitionSpec as P

COEF_Z = 8
COEF_X = 5120
COEF_Y = 5120
ROWS = 8
MESH = pl.DeviceIdType.MESH


def link(coef, one_side, other_side):
    return coef * one_side * other_side / (one_side + other_side)


def steps(count, unroll, body, carry):
    def lap(block, carry):
        for u in range(unroll):
            carry = body(block * unroll + u, carry)
        return carry

    return lax.fori_loop(0, count // unroll, lap, carry)


def plane(i, size):
    start = i * size
    return pl.ds(start if isinstance(i, int) else pl.multiple_of(start, size), size)


def factor_segment(links, cells, rows, fwd, bwd, gains):
    def body(i, carry):
        s_f, g_f, s_b, g_b = carry
        j = cells - 1 - i
        here, there = plane(i, rows), plane(j, rows)
        w, e = links[here], links[plane(i + 1, rows)]
        t = 1.0 + w * s_f
        p = 1.0 / (t + e)
        s_f, wp = t * p, w * p
        g_f = g_f * wp
        fwd[0][here], fwd[1][here], fwd[2][here], fwd[3][here] = p, wp, e * p, g_f
        w, e = links[there], links[plane(j + 1, rows)]
        t = 1.0 + e * s_b
        p = 1.0 / (t + w)
        s_b, ep = t * p, e * p
        g_b = g_b * ep
        bwd[0][there], bwd[1][there], bwd[2][there], bwd[3][there] = p, ep, w * p, g_b
        return s_f, g_f, s_b, g_b

    ones = jnp.ones((rows, 128), jnp.float32)
    _, g_f, _, g_b = steps(cells, 4, body, (ones, ones, ones, ones))
    gains[0] = bwd[2][plane(0, rows)]
    gains[1] = g_b
    gains[2] = g_f
    gains[3] = fwd[2][plane(cells - 1, rows)]


def sweep_values(load, cells, rows, fwd, bwd, ends):
    def body(i, carry):
        y_f, y_b = carry
        j = cells - 1 - i
        here, there = plane(i, rows), plane(j, rows)
        y_f = load(i) * fwd[0][here] + fwd[1][here] * y_f
        fwd[4][here] = y_f
        y_b = load(j) * bwd[0][there] + bwd[1][there] * y_b
        bwd[4][there] = y_b
        return y_f, y_b

    zeros = jnp.zeros((rows, 128), jnp.float32)
    y_f, y_b = steps(cells, 4, body, (zeros, zeros))
    ends[0] = y_b
    ends[1] = y_f


def back_substitute(before, after, cells, rows, fwd, bwd, target):
    def body(i, carry):
        low, high = carry
        j = cells - 1 - i
        here, there = plane(i, rows), plane(j, rows)
        low = (bwd[4][here] + bwd[3][here] * after) + bwd[2][here] * low
        target[here] = low
        high = (fwd[4][there] + fwd[3][there] * before) + fwd[2][there] * high
        target[there] = high
        return low, high

    steps(cells // 2, 4, body, (before, after))


class Reduced:
    def __init__(self, axis, rows, refs):
        self.axis, self.count, self.me = axis, lax.axis_size(axis), lax.axis_index(axis)
        self.owners = min(self.count, rows // ROWS)
        self.rows = rows // self.owners
        self.stride = self.count // self.owners
        self.mine = lax.rem(self.me, self.stride) == 0
        self.group = self.me // self.stride
        (self.gains, self.ends, self.all_gains, self.all_ends, self.relation, self.reply, self.sides) = refs[:7]
        (self.gain_send, self.gain_recv, self.end_send, self.end_recv, self.reply_send, self.reply_recv) = refs[7:]

    def copy(self, src, dst, send, recv, to):
        return pltpu.make_async_remote_copy(
            src_ref=src, dst_ref=dst, send_sem=send, recv_sem=recv,
            device_id={self.axis: to}, device_id_type=MESH,
        )

    def to_owner(self, o, source, everyone, send, recv):
        return self.copy(
            source.at[:, pl.ds(o * self.rows, self.rows), :], everyone.at[self.me],
            send.at[o], recv.at[self.me], o * self.stride,
        )

    def spread(self, source, everyone, send, recv):
        for o in range(self.owners):

            @pl.when(self.me != o * self.stride)
            def _():
                self.to_owner(o, source, everyone, send, recv).start()

            @pl.when(self.me == o * self.stride)
            def _():
                everyone[o * self.stride] = source[:, o * self.rows : (o + 1) * self.rows, :]

    def send_gains(self):
        self.spread(self.gains, self.all_gains, self.gain_send, self.gain_recv)

    def send_ends(self):
        self.spread(self.ends, self.all_ends, self.end_send, self.end_recv)

    def arrived(self, everyone, recv):
        for d in range(1, self.count):
            k = lax.rem(self.me + d, self.count)
            self.copy(everyone.at[k], everyone.at[k], recv.at[k], recv.at[k], k).wait_recv()

    def factor(self):
        @pl.when(self.mine)
        def _():
            self.arrived(self.all_gains, self.gain_recv)
            gain = jnp.zeros((self.rows, 128), jnp.float32)
            for k in range(self.count):
                head_west, head_east = self.all_gains[k, 0], self.all_gains[k, 1]
                tail_west, tail_east = self.all_gains[k, 2], self.all_gains[k, 3]
                scale = 1.0 / (1.0 - head_west * gain)
                beta, gamma = head_east * scale, tail_west * gain
                self.relation[k, 0], self.relation[k, 1] = scale, beta
                self.relation[k, 2], self.relation[k, 3] = gamma, gain
                gain = tail_east + gamma * beta

    def reply_copy(self, k):
        return self.copy(
            self.reply.at[k], self.sides.at[self.group],
            self.reply_send.at[k], self.reply_recv.at[self.group], k,
        )

    def solve(self):
        @pl.when(self.mine)
        def _():
            self.arrived(self.all_ends, self.end_recv)
            value = jnp.zeros((self.rows, 128), jnp.float32)
            alphas, values = [], []
            for k in range(self.count):
                values.append(value)
                scale, gamma = self.relation[k, 0], self.relation[k, 2]
                head_west, tail_west = self.all_gains[k, 0], self.all_gains[k, 2]
                alpha = (self.all_ends[k, 0] + head_west * value) * scale
                value = (self.all_ends[k, 1] + tail_west * value) + gamma * alpha
                alphas.append(alpha)
            after = jnp.zeros((self.rows, 128), jnp.float32)
            for k in reversed(range(self.count)):
                self.reply[k, 1] = after
                after = alphas[k] + self.relation[k, 1] * after
                self.reply[k, 0] = values[k] + self.relation[k, 3] * after
            for d in range(1, self.count):
                self.reply_copy(lax.rem(self.me + d, self.count)).start()
            self.sides[self.group] = self.reply[self.me]

    def result(self):
        for o in range(self.owners):

            @pl.when(self.me != o * self.stride)
            def _():
                self.copy(
                    self.sides.at[o], self.sides.at[o], self.reply_recv.at[o], self.reply_recv.at[o],
                    o * self.stride,
                ).wait_recv()

        whole = (self.owners * self.rows, 128)
        return self.sides[:, 0].reshape(whole), self.sides[:, 1].reshape(whole)

    def drain(self):
        for o in range(self.owners):

            @pl.when(self.me != o * self.stride)
            def _():
                self.to_owner(o, self.gains, self.all_gains, self.gain_send, self.gain_recv).wait_send()
                self.to_owner(o, self.ends, self.all_ends, self.end_send, self.end_recv).wait_send()

        @pl.when(self.mine)
        def _():
            for d in range(1, self.count):
                self.reply_copy(lax.rem(self.me + d, self.count)).wait_send()


def reduced_scratch(count, rows):
    owners = min(count, rows // ROWS)
    part = rows // owners
    dma = pltpu.SemaphoreType.DMA
    return [
        pltpu.VMEM((4, rows, 128), jnp.float32),
        pltpu.VMEM((2, rows, 128), jnp.float32),
        pltpu.VMEM((count, 4, part, 128), jnp.float32),
        pltpu.VMEM((count, 2, part, 128), jnp.float32),
        pltpu.VMEM((count, 4, part, 128), jnp.float32),
        pltpu.VMEM((count, 2, part, 128), jnp.float32),
        pltpu.VMEM((owners, 2, part, 128), jnp.float32),
        dma((owners,)), dma((count,)), dma((owners,)), dma((count,)), dma((count,)), dma((owners,)),
    ]


def kernel(X, Y, h, c, q, out, *scratch):
    Z = 128
    chunks = X * Y // 128
    (stage_x, stage_y, halo_x, halo_y, halo_send, halo_recv, force, link_x, link_y, link_z) = scratch[:10]
    fwd_x, bwd_x, fwd_y, bwd_y = scratch[10:15], scratch[15:20], scratch[20:25], scratch[25:30]
    first, second, up_z, piv_z, lag_z, lead_z, mid_z, val_z = scratch[30:38]
    along_x = Reduced("gx", Y, scratch[38:51])
    along_y = Reduced("gy", X, scratch[51:64])
    nx, ny, me_x, me_y = along_x.count, along_y.count, along_x.me, along_y.me

    barrier = pltpu.get_barrier_semaphore()
    for d in range(1, nx):
        pl.semaphore_signal(barrier, inc=1, device_id={"gx": lax.rem(me_x + d, nx)}, device_id_type=MESH)
    for d in range(1, ny):
        pl.semaphore_signal(barrier, inc=1, device_id={"gy": lax.rem(me_y + d, ny)}, device_id_type=MESH)

    def column(j):
        return pl.ds(j, X, stride=Y)

    for side, (i, j) in enumerate(((0, 0), (X - 1, Y - 1))):
        stage_x[side, 0], stage_x[side, 1] = h[plane(i, Y)], c[plane(i, Y)]
        stage_y[side, 0], stage_y[side, 1] = h[column(j), :], c[column(j), :]
    pl.semaphore_wait(barrier, nx - 1 + ny - 1)

    halos = []
    for a, (axis, me, count, stage, halo) in enumerate(
        (("gx", me_x, nx, stage_x, halo_x), ("gy", me_y, ny, stage_y, halo_y))
    ):
        for side in (0, 1):
            to = me - 1 if side == 0 else me + 1
            inside = me > 0 if side == 0 else me < count - 1
            send = pltpu.make_async_remote_copy(
                src_ref=stage.at[side], dst_ref=halo.at[1 - side],
                send_sem=halo_send.at[2 * a + side], recv_sem=halo_recv.at[2 * a + 1 - side],
                device_id={axis: to}, device_id_type=MESH,
            )
            take = pltpu.make_async_remote_copy(
                src_ref=stage.at[side], dst_ref=halo.at[side],
                send_sem=halo_send.at[2 * a + side], recv_sem=halo_recv.at[2 * a + side],
                device_id={axis: to}, device_id_type=MESH,
            )
            halos.append((inside, send, take))

            @pl.when(inside)
            def _():
                send.start()

            @pl.when(jnp.logical_not(inside))
            def _():
                halo[side] = jnp.zeros((2,) + halo.shape[2:], jnp.float32)

    inner = lax.broadcasted_iota(jnp.int32, (X, 128), 1) < Z - 1

    def depth_and_second(j, carry):
        head, cond, flux = carry
        up = jnp.where(inner, link(COEF_Z, cond, pltpu.roll(cond, Z - 1, 1)), 0.0)
        link_z[plane(j, X)] = up
        rise = up * (pltpu.roll(head, Z - 1, 1) - head)
        ahead = jnp.minimum(j + 1, Y - 1)
        head_next, cond_next = h[column(ahead), :], c[column(ahead), :]
        north = link(COEF_Y, cond, cond_next)
        link_y[plane(j + 1, X)] = north
        flux_next = north * (head_next - head)
        force[column(j), :] = 2.0 * ((rise - pltpu.roll(rise, 1, 1)) + (flux_next - flux))
        return head_next, cond_next, flux_next

    steps(Y, 2, depth_and_second, (h[column(0), :], c[column(0), :], jnp.zeros((X, 128), jnp.float32)))

    def along_first(i, carry):
        head, cond, flux = carry
        here, ahead = plane(i, Y), plane(jnp.minimum(i + 1, X - 1), Y)
        head_next, cond_next = h[ahead], c[ahead]
        east = link(COEF_X, cond, cond_next)
        link_x[plane(i + 1, Y)] = east
        flux_next = east * (head_next - head)
        force[here] = force[here] + (2.0 * (flux_next - flux) + q[here])
        return head_next, cond_next, flux_next

    steps(X, 2, along_first, (h[plane(0, Y)], c[plane(0, Y)], jnp.zeros((Y, 128), jnp.float32)))

    for inside, _, take in halos:

        @pl.when(inside)
        def _():
            take.wait_recv()

    low = link(COEF_X, halo_x[0, 1], c[plane(0, Y)])
    high = link(COEF_X, halo_x[1, 1], c[plane(X - 1, Y)])
    link_x[plane(0, Y)], link_x[plane(X, Y)] = low, high
    force[plane(0, Y)] += 2.0 * (low * (halo_x[0, 0] - h[plane(0, Y)]))
    force[plane(X - 1, Y)] += 2.0 * (high * (halo_x[1, 0] - h[plane(X - 1, Y)]))
    low = link(COEF_Y, halo_y[0, 1], c[column(0), :])
    high = link(COEF_Y, halo_y[1, 1], c[column(Y - 1), :])
    link_y[plane(0, X)], link_y[plane(Y, X)] = low, high
    force[column(0), :] += 2.0 * (low * (halo_y[0, 0] - h[column(0), :]))
    force[column(Y - 1), :] += 2.0 * (high * (halo_y[1, 0] - h[column(Y - 1), :]))

    factor_segment(link_x, X, Y, fwd_x, bwd_x, along_x.gains)
    along_x.send_gains()
    sweep_values(lambda i: force[plane(i, Y)], X, Y, fwd_x, bwd_x, along_x.ends)
    along_x.send_ends()

    factor_segment(link_y, Y, X, fwd_y, bwd_y, along_y.gains)
    along_y.send_gains()

    along_x.factor()
    along_x.solve()

    def turn_links(k, carry):
        up_z[pl.ds(k, Z, stride=chunks), :] = link_z[plane(k, 128)].T
        return carry

    steps(chunks, 2, turn_links, 0)
    half = Z // 2

    def factor_z(i, carry):
        s_f, w, s_b, e = carry
        here, there = plane(i, chunks), plane(Z - 1 - i, chunks)
        ahead = up_z[here]
        t = 1.0 + w * s_f
        p = 1.0 / (t + ahead)
        s_f = t * p
        piv_z[here], lag_z[here], lead_z[here] = p, w * p, ahead * p
        behind = up_z[plane(Z - 2 - i, chunks)]
        t = 1.0 + e * s_b
        p = 1.0 / (t + behind)
        s_b = t * p
        piv_z[there], lag_z[there], lead_z[there] = p, e * p, behind * p
        return s_f, ahead, s_b, behind

    ones, zeros = (jnp.full((chunks, 128), v, jnp.float32) for v in (1.0, 0.0))
    s_f, _, s_b, _ = steps(half, 4, factor_z, (ones, zeros, ones, zeros))
    mid_z[...] = 1.0 / (s_f + s_b * lead_z[plane(half - 1, chunks)])

    before, after = along_x.result()
    back_substitute(before, after, X, Y, fwd_x, bwd_x, first)

    sweep_values(lambda j: first[column(j), :], Y, X, fwd_y, bwd_y, along_y.ends)
    along_y.send_ends()
    along_y.factor()
    along_y.solve()
    before, after = along_y.result()
    back_substitute(before, after, Y, X, fwd_y, bwd_y, second)

    def turn_values(k, carry):
        val_z[pl.ds(k, Z, stride=chunks), :] = second[plane(k, 128)].T
        return carry

    steps(chunks, 2, turn_values, 0)

    def sweep_z(i, carry):
        y_f, y_b = carry
        here, there = plane(i, chunks), plane(Z - 1 - i, chunks)
        y_f = val_z[here] * piv_z[here] + lag_z[here] * y_f
        y_b = val_z[there] * piv_z[there] + lag_z[there] * y_b
        val_z[here], val_z[there] = y_f, y_b
        return y_f, y_b

    y_f, y_b = steps(half, 8, sweep_z, (zeros, zeros))
    below = (y_f + lead_z[plane(half - 1, chunks)] * y_b) * mid_z[...]
    above = y_b + lead_z[plane(half, chunks)] * below

    def back_z(i, carry):
        low, high = carry
        here, there = plane(half - 1 - i, chunks), plane(half + i, chunks)
        val_z[here], val_z[there] = low, high
        nearer, farther = plane(jnp.maximum(half - 2 - i, 0), chunks), plane(jnp.minimum(half + 1 + i, Z - 1), chunks)
        low = val_z[nearer] + lead_z[nearer] * low
        high = val_z[farther] + lead_z[farther] * high
        return low, high

    steps(half, 8, back_z, (below, above))

    per_chunk = 128 // X

    def write(k, carry):
        lines = val_z[pl.ds(k, Z, stride=chunks), :].T
        for part in range(per_chunk):
            at = column(k * per_chunk + part)
            out[at, :] = h[at, :] + lines[part * X : (part + 1) * X]
        return carry

    steps(chunks, 2, write, 0)

    for inside, send, _ in halos:

        @pl.when(inside)
        def _():
            send.wait_send()

    along_x.drain()
    along_y.drain()


def per_device(water_head, conductivity, recharge):
    X, Y, Z = water_head.shape
    nx, ny = lax.axis_size("gx"), lax.axis_size("gy")
    chunks = X * Y // 128

    def vmem(*shape):
        return pltpu.VMEM(shape, jnp.float32)

    cells = X * Y
    scratch = [
        vmem(2, 2, Y, Z), vmem(2, 2, X, Z), vmem(2, 2, Y, Z), vmem(2, 2, X, Z),
        pltpu.SemaphoreType.DMA((4,)), pltpu.SemaphoreType.DMA((4,)),
        vmem(cells, Z), vmem(cells + Y, Z), vmem(cells + X, Z), vmem(cells, Z),
    ]
    scratch += [vmem(cells, Z) for _ in range(20)]
    scratch += [vmem(cells, Z) for _ in range(6)] + [vmem(chunks, 128), vmem(cells, Z)]
    scratch += reduced_scratch(nx, Y) + reduced_scratch(ny, X)
    flat = [array.reshape(cells, Z) for array in (water_head, conductivity, recharge)]
    result = pl.pallas_call(
        functools.partial(kernel, X, Y),
        out_shape=jax.ShapeDtypeStruct((cells, Z), jnp.float32),
        in_specs=[pl.BlockSpec(memory_space=pltpu.VMEM)] * 3,
        out_specs=pl.BlockSpec(memory_space=pltpu.VMEM),
        scratch_shapes=scratch,
        compiler_params=pltpu.CompilerParams(
            collective_id=0, has_side_effects=True, vmem_limit_bytes=56 * 2**20
        ),
    )(*flat)
    return result.reshape(X, Y, Z)


def solution(mesh):
    placed = (P("gx", "gy", None), P("gx", "gy", None), P("gx", "gy", None))
    return jax.shard_map(
        per_device, mesh=mesh, in_specs=placed, out_specs=P("gx", "gy", None), check_vma=False
    )
```

```python
import functools

import jax
import jax.numpy as jnp
from jax import lax
from jax.experimental import pallas as pl
from jax.experimental.pallas import tpu as pltpu
from jax.sharding import PartitionSpec as P

COEF_Z = 8
COEF_X = 5120
COEF_Y = 5120
ROWS = 8
MESH = pl.DeviceIdType.MESH


def link(coef, one_side, other_side):
    return (coef * one_side * other_side) * pl.reciprocal(one_side + other_side)


def steps(count, unroll, body, carry):
    def lap(block, carry):
        for u in range(unroll):
            carry = body(block * unroll + u, carry)
        return carry

    return lax.fori_loop(0, count // unroll, lap, carry)


def plane(i, size):
    start = i * size
    return pl.ds(start if isinstance(i, int) else pl.multiple_of(start, size), size)


def factor_segment(links, cells, rows, fwd_p, bwd_p, near, far, gains):
    def body(keep, i, carry):
        s_f, g_f, s_b, g_b = carry
        j = cells - 1 - i
        here, there = plane(i, rows), plane(j, rows)
        w, e = links[here], links[plane(i + 1, rows)]
        t = 1.0 + w * s_f
        p = pl.reciprocal(t + e)
        s_f = t * p
        g_f = g_f * (w * p)
        fwd_p[here] = p
        if keep:
            near[here], far[here] = e * p, g_f
        w, e = links[there], links[plane(j + 1, rows)]
        t = 1.0 + e * s_b
        p = pl.reciprocal(t + w)
        s_b = t * p
        g_b = g_b * (e * p)
        bwd_p[there] = p
        if keep:
            near[there], far[there] = w * p, g_b
        return s_f, g_f, s_b, g_b

    half = cells // 2
    ones = jnp.ones((rows, 128), jnp.float32)
    carry = steps(half, 4, functools.partial(body, False), (ones, ones, ones, ones))
    _, g_f, _, g_b = steps(half, 4, lambda i, carry: body(True, i + half, carry), carry)
    gains[0] = near[plane(0, rows)]
    gains[1] = g_b
    gains[2] = g_f
    gains[3] = near[plane(cells - 1, rows)]


def sweep_values(rhs, links, cells, rows, fwd_p, bwd_p, value, ends):
    def body(keep, i, carry):
        y_f, y_b = carry
        j = cells - 1 - i
        here, there = plane(i, rows), plane(j, rows)
        y_f = (rhs[here] + links[here] * y_f) * fwd_p[here]
        y_b = (rhs[there] + links[plane(j + 1, rows)] * y_b) * bwd_p[there]
        if keep:
            value[here], value[there] = y_f, y_b
        return y_f, y_b

    half = cells // 2
    zeros = jnp.zeros((rows, 128), jnp.float32)
    carry = steps(half, 4, functools.partial(body, False), (zeros, zeros))
    y_f, y_b = steps(half, 4, lambda i, carry: body(True, i + half, carry), carry)
    ends[0] = y_b
    ends[1] = y_f


def back_substitute(before, after, cells, rows, near, far, value, store):
    def body(i, carry):
        low, high = carry
        j = cells - 1 - i
        here, there = plane(i, rows), plane(j, rows)
        low = (value[here] + far[here] * after) + near[here] * low
        store(i, low)
        high = (value[there] + far[there] * before) + near[there] * high
        store(j, high)
        return low, high

    steps(cells // 2, 4, body, (before, after))


class Reduced:
    def __init__(self, axis, rows, refs):
        self.axis, self.count, self.me = axis, lax.axis_size(axis), lax.axis_index(axis)
        self.owners = min(self.count, rows // ROWS)
        self.rows = rows // self.owners
        self.stride = self.count // self.owners
        self.mine = lax.rem(self.me, self.stride) == 0
        self.group = self.me // self.stride
        (self.gains, self.ends, self.all_gains, self.all_ends, self.relation, self.reply, self.sides) = refs[:7]
        (self.gain_send, self.gain_recv, self.end_send, self.end_recv, self.reply_send, self.reply_recv) = refs[7:]

    def copy(self, src, dst, send, recv, to):
        return pltpu.make_async_remote_copy(
            src_ref=src, dst_ref=dst, send_sem=send, recv_sem=recv,
            device_id={self.axis: to}, device_id_type=MESH,
        )

    def to_owner(self, o, source, everyone, send, recv):
        return self.copy(
            source.at[:, pl.ds(o * self.rows, self.rows), :], everyone.at[self.me],
            send.at[o], recv.at[self.me], o * self.stride,
        )

    def spread(self, source, everyone, send, recv):
        for o in range(self.owners):

            @pl.when(self.me != o * self.stride)
            def _():
                self.to_owner(o, source, everyone, send, recv).start()

            @pl.when(self.me == o * self.stride)
            def _():
                everyone[o * self.stride] = source[:, o * self.rows : (o + 1) * self.rows, :]

    def send_gains(self):
        self.spread(self.gains, self.all_gains, self.gain_send, self.gain_recv)

    def send_ends(self):
        self.spread(self.ends, self.all_ends, self.end_send, self.end_recv)

    def arrived(self, everyone, recv):
        for d in range(1, self.count):
            k = lax.rem(self.me + d, self.count)
            self.copy(everyone.at[k], everyone.at[k], recv.at[k], recv.at[k], k).wait_recv()

    def factor(self):
        @pl.when(self.mine)
        def _():
            self.arrived(self.all_gains, self.gain_recv)
            gain = jnp.zeros((self.rows, 128), jnp.float32)
            for k in range(self.count):
                head_west, head_east = self.all_gains[k, 0], self.all_gains[k, 1]
                tail_west, tail_east = self.all_gains[k, 2], self.all_gains[k, 3]
                scale = pl.reciprocal(1.0 - head_west * gain)
                beta, gamma = head_east * scale, tail_west * gain
                self.relation[k, 0], self.relation[k, 1] = scale, beta
                self.relation[k, 2], self.relation[k, 3] = gamma, gain
                gain = tail_east + gamma * beta

    def reply_copy(self, k):
        return self.copy(
            self.reply.at[k], self.sides.at[self.group],
            self.reply_send.at[k], self.reply_recv.at[self.group], k,
        )

    def solve(self):
        @pl.when(self.mine)
        def _():
            self.arrived(self.all_ends, self.end_recv)
            value = jnp.zeros((self.rows, 128), jnp.float32)
            alphas, values = [], []
            for k in range(self.count):
                values.append(value)
                scale, gamma = self.relation[k, 0], self.relation[k, 2]
                head_west, tail_west = self.all_gains[k, 0], self.all_gains[k, 2]
                alpha = (self.all_ends[k, 0] + head_west * value) * scale
                value = (self.all_ends[k, 1] + tail_west * value) + gamma * alpha
                alphas.append(alpha)
            after = jnp.zeros((self.rows, 128), jnp.float32)
            for k in reversed(range(self.count)):
                self.reply[k, 1] = after
                after = alphas[k] + self.relation[k, 1] * after
                self.reply[k, 0] = values[k] + self.relation[k, 3] * after
            for d in range(1, self.count):
                self.reply_copy(lax.rem(self.me + d, self.count)).start()
            self.sides[self.group] = self.reply[self.me]

    def result(self):
        for o in range(self.owners):

            @pl.when(self.me != o * self.stride)
            def _():
                self.copy(
                    self.sides.at[o], self.sides.at[o], self.reply_recv.at[o], self.reply_recv.at[o],
                    o * self.stride,
                ).wait_recv()

        whole = (self.owners * self.rows, 128)
        return self.sides[:, 0].reshape(whole), self.sides[:, 1].reshape(whole)

    def drain(self):
        for o in range(self.owners):

            @pl.when(self.me != o * self.stride)
            def _():
                self.to_owner(o, self.gains, self.all_gains, self.gain_send, self.gain_recv).wait_send()
                self.to_owner(o, self.ends, self.all_ends, self.end_send, self.end_recv).wait_send()

        @pl.when(self.mine)
        def _():
            for d in range(1, self.count):
                self.reply_copy(lax.rem(self.me + d, self.count)).wait_send()


def reduced_scratch(count, rows):
    owners = min(count, rows // ROWS)
    part = rows // owners
    dma = pltpu.SemaphoreType.DMA
    return [
        pltpu.VMEM((4, rows, 128), jnp.float32),
        pltpu.VMEM((2, rows, 128), jnp.float32),
        pltpu.VMEM((count, 4, part, 128), jnp.float32),
        pltpu.VMEM((count, 2, part, 128), jnp.float32),
        pltpu.VMEM((count, 4, part, 128), jnp.float32),
        pltpu.VMEM((count, 2, part, 128), jnp.float32),
        pltpu.VMEM((owners, 2, part, 128), jnp.float32),
        dma((owners,)), dma((count,)), dma((owners,)), dma((count,)), dma((count,)), dma((owners,)),
    ]


def kernel(X, Y, h, c, q, out, *scratch):
    Z = 128
    chunks = X * Y // 128
    (stage_x, stage_y, halo_x, halo_y, halo_send, halo_recv, force, link_x, link_y, link_z) = scratch[:10]
    fwd_x, bwd_x, near_x, far_x, value_x, fwd_y, bwd_y, near_y, far_y, value_y = scratch[10:20]
    first, second, up_z, piv_z, lag_z, lead_z, val_z = scratch[20:27]
    along_x = Reduced("gx", Y, scratch[27:40])
    along_y = Reduced("gy", X, scratch[40:53])
    nx, ny, me_x, me_y = along_x.count, along_y.count, along_x.me, along_y.me

    barrier = pltpu.get_barrier_semaphore()
    for d in range(1, nx):
        pl.semaphore_signal(barrier, inc=1, device_id={"gx": lax.rem(me_x + d, nx)}, device_id_type=MESH)
    for d in range(1, ny):
        pl.semaphore_signal(barrier, inc=1, device_id={"gy": lax.rem(me_y + d, ny)}, device_id_type=MESH)

    def column(j):
        return pl.ds(j, X, stride=Y)

    for side, (i, j) in enumerate(((0, 0), (X - 1, Y - 1))):
        stage_x[side, 0], stage_x[side, 1] = h[plane(i, Y)], c[plane(i, Y)]
        stage_y[side, 0], stage_y[side, 1] = h[column(j), :], c[column(j), :]

    def along_first(i, carry):
        head, cond, flux = carry
        here, ahead = plane(i, Y), plane(jnp.minimum(i + 1, X - 1), Y)
        head_next, cond_next = h[ahead], c[ahead]
        east = link(COEF_X, cond, cond_next)
        link_x[plane(i + 1, Y)] = east
        flux_next = east * (head_next - head)
        force[here] = 2.0 * (flux_next - flux) + q[here]
        return head_next, cond_next, flux_next

    steps(X, 2, along_first, (h[plane(0, Y)], c[plane(0, Y)], jnp.zeros((Y, 128), jnp.float32)))
    pl.semaphore_wait(barrier, nx - 1 + ny - 1)

    halos = []
    for a, (axis, me, count, stage, halo) in enumerate(
        (("gx", me_x, nx, stage_x, halo_x), ("gy", me_y, ny, stage_y, halo_y))
    ):
        for side in (0, 1):
            to = me - 1 if side == 0 else me + 1
            inside = me > 0 if side == 0 else me < count - 1
            send = pltpu.make_async_remote_copy(
                src_ref=stage.at[side], dst_ref=halo.at[1 - side],
                send_sem=halo_send.at[2 * a + side], recv_sem=halo_recv.at[2 * a + 1 - side],
                device_id={axis: to}, device_id_type=MESH,
            )
            take = pltpu.make_async_remote_copy(
                src_ref=stage.at[side], dst_ref=halo.at[side],
                send_sem=halo_send.at[2 * a + side], recv_sem=halo_recv.at[2 * a + side],
                device_id={axis: to}, device_id_type=MESH,
            )
            halos.append((inside, send, take))

            @pl.when(inside)
            def _():
                send.start()

            @pl.when(jnp.logical_not(inside))
            def _():
                halo[side] = jnp.zeros((2,) + halo.shape[2:], jnp.float32)

    inner = lax.broadcasted_iota(jnp.int32, (X, 128), 1) < Z - 1

    def depth_and_second(j, carry):
        head, cond, flux = carry
        up = jnp.where(inner, link(COEF_Z, cond, pltpu.roll(cond, Z - 1, 1)), 0.0)
        link_z[plane(j, X)] = up
        rise = up * (pltpu.roll(head, Z - 1, 1) - head)
        ahead = jnp.minimum(j + 1, Y - 1)
        head_next, cond_next = h[column(ahead), :], c[column(ahead), :]
        north = link(COEF_Y, cond, cond_next)
        link_y[plane(j + 1, X)] = north
        flux_next = north * (head_next - head)
        force[column(j), :] += 2.0 * ((rise - pltpu.roll(rise, 1, 1)) + (flux_next - flux))
        return head_next, cond_next, flux_next

    steps(Y, 2, depth_and_second, (h[column(0), :], c[column(0), :], jnp.zeros((X, 128), jnp.float32)))

    for inside, _, take in halos:

        @pl.when(inside)
        def _():
            take.wait_recv()

    low = link(COEF_X, halo_x[0, 1], c[plane(0, Y)])
    high = link(COEF_X, halo_x[1, 1], c[plane(X - 1, Y)])
    link_x[plane(0, Y)], link_x[plane(X, Y)] = low, high
    force[plane(0, Y)] += 2.0 * (low * (halo_x[0, 0] - h[plane(0, Y)]))
    force[plane(X - 1, Y)] += 2.0 * (high * (halo_x[1, 0] - h[plane(X - 1, Y)]))
    low = link(COEF_Y, halo_y[0, 1], c[column(0), :])
    high = link(COEF_Y, halo_y[1, 1], c[column(Y - 1), :])
    link_y[plane(0, X)], link_y[plane(Y, X)] = low, high
    force[column(0), :] += 2.0 * (low * (halo_y[0, 0] - h[column(0), :]))
    force[column(Y - 1), :] += 2.0 * (high * (halo_y[1, 0] - h[column(Y - 1), :]))

    factor_segment(link_x, X, Y, fwd_x, bwd_x, near_x, far_x, along_x.gains)
    along_x.send_gains()
    sweep_values(force, link_x, X, Y, fwd_x, bwd_x, value_x, along_x.ends)
    along_x.send_ends()

    factor_segment(link_y, Y, X, fwd_y, bwd_y, near_y, far_y, along_y.gains)
    along_y.send_gains()

    along_x.factor()
    along_x.solve()

    def turn_links(k, carry):
        up_z[pl.ds(k, Z, stride=chunks), :] = link_z[plane(k, 128)].T
        return carry

    steps(chunks, 2, turn_links, 0)
    half = Z // 2

    def factor_z(i, carry):
        s_f, w, s_b, e = carry
        here, there = plane(i, chunks), plane(Z - 1 - i, chunks)
        ahead = up_z[here]
        t = 1.0 + w * s_f
        p = pl.reciprocal(t + ahead)
        s_f = t * p
        piv_z[here], lag_z[here], lead_z[here] = p, w * p, ahead * p
        behind = up_z[plane(Z - 2 - i, chunks)]
        t = 1.0 + e * s_b
        p = pl.reciprocal(t + behind)
        s_b = t * p
        piv_z[there], lag_z[there], lead_z[there] = p, e * p, behind * p
        return s_f, ahead, s_b, behind

    def factor_part(start, stop, carry):
        return steps(stop - start, 4, lambda i, carry: factor_z(i + start, carry), carry)

    ones, zeros = (jnp.full((chunks, 128), v, jnp.float32) for v in (1.0, 0.0))
    carry = factor_part(0, 16, (ones, zeros, ones, zeros))

    before, after = along_x.result()

    def store_first(i, cells):
        first[pl.ds(i, Y, stride=X), :] = cells

    back_substitute(before, after, X, Y, near_x, far_x, value_x, store_first)

    sweep_values(first, link_y, Y, X, fwd_y, bwd_y, value_y, along_y.ends)
    along_y.send_ends()
    along_y.factor()
    carry = factor_part(16, 40, carry)
    along_y.solve()
    s_f, _, s_b, _ = factor_part(40, half, carry)
    middle = pl.reciprocal(s_f + s_b * lead_z[plane(half - 1, chunks)])
    before, after = along_y.result()

    def store_second(j, cells):
        second[plane(j, X)] = cells

    back_substitute(before, after, Y, X, near_y, far_y, value_y, store_second)

    def turn_values(k, carry):
        val_z[pl.ds(k, Z, stride=chunks), :] = second[plane(k, 128)].T
        return carry

    steps(chunks, 2, turn_values, 0)

    def sweep_z(i, carry):
        y_f, y_b = carry
        here, there = plane(i, chunks), plane(Z - 1 - i, chunks)
        y_f = val_z[here] * piv_z[here] + lag_z[here] * y_f
        y_b = val_z[there] * piv_z[there] + lag_z[there] * y_b
        val_z[here], val_z[there] = y_f, y_b
        return y_f, y_b

    y_f, y_b = steps(half, 8, sweep_z, (zeros, zeros))
    below = (y_f + lead_z[plane(half - 1, chunks)] * y_b) * middle
    above = y_b + lead_z[plane(half, chunks)] * below

    def back_z(i, carry):
        low, high = carry
        here, there = plane(half - 1 - i, chunks), plane(half + i, chunks)
        val_z[here], val_z[there] = low, high
        nearer, farther = plane(jnp.maximum(half - 2 - i, 0), chunks), plane(jnp.minimum(half + 1 + i, Z - 1), chunks)
        low = val_z[nearer] + lead_z[nearer] * low
        high = val_z[farther] + lead_z[farther] * high
        return low, high

    steps(half, 8, back_z, (below, above))

    per_chunk = 128 // X

    def write(k, carry):
        lines = val_z[pl.ds(k, Z, stride=chunks), :].T
        for part in range(per_chunk):
            at = column(k * per_chunk + part)
            out[at, :] = h[at, :] + lines[part * X : (part + 1) * X]
        return carry

    steps(chunks, 2, write, 0)

    for inside, send, _ in halos:

        @pl.when(inside)
        def _():
            send.wait_send()

    along_x.drain()
    along_y.drain()


def per_device(water_head, conductivity, recharge):
    X, Y, Z = water_head.shape
    nx, ny = lax.axis_size("gx"), lax.axis_size("gy")

    def vmem(*shape):
        return pltpu.VMEM(shape, jnp.float32)

    cells = X * Y
    scratch = [
        vmem(2, 2, Y, Z), vmem(2, 2, X, Z), vmem(2, 2, Y, Z), vmem(2, 2, X, Z),
        pltpu.SemaphoreType.DMA((4,)), pltpu.SemaphoreType.DMA((4,)),
        vmem(cells, Z), vmem(cells + Y, Z), vmem(cells + X, Z), vmem(cells, Z),
    ]
    scratch += [vmem(cells, Z) for _ in range(17)]
    scratch += reduced_scratch(nx, Y) + reduced_scratch(ny, X)
    flat = [array.reshape(cells, Z) for array in (water_head, conductivity, recharge)]
    result = pl.pallas_call(
        functools.partial(kernel, X, Y),
        out_shape=jax.ShapeDtypeStruct((cells, Z), jnp.float32),
        in_specs=[pl.BlockSpec(memory_space=pltpu.VMEM)] * 3,
        out_specs=pl.BlockSpec(memory_space=pltpu.VMEM),
        scratch_shapes=scratch,
        compiler_params=pltpu.CompilerParams(
            collective_id=0, has_side_effects=True, vmem_limit_bytes=56 * 2**20
        ),
    )(*flat)
    return result.reshape(X, Y, Z)


def solution(mesh):
    placed = (P("gx", "gy", None), P("gx", "gy", None), P("gx", "gy", None))
    return jax.shard_map(
        per_device, mesh=mesh, in_specs=placed, out_specs=P("gx", "gy", None), check_vma=False
    )
```

```python
import functools

import jax
import jax.numpy as jnp
from jax import lax
from jax.experimental import pallas as pl
from jax.experimental.pallas import tpu as pltpu
from jax.sharding import PartitionSpec as P

COEF_Z = 8
COEF_X = 5120
COEF_Y = 5120
ROWS = 8
MESH = pl.DeviceIdType.MESH


def inverse(x):
    return pl.reciprocal(x, approx=True, full_range=False)


def link(coef, one_side, other_side):
    return (coef * one_side * other_side) * inverse(one_side + other_side)


def steps(count, unroll, body, carry):
    def lap(block, carry):
        for u in range(unroll):
            carry = body(block * unroll + u, carry)
        return carry

    return lax.fori_loop(0, count // unroll, lap, carry)


def plane(i, size):
    start = i * size
    return pl.ds(start if isinstance(i, int) else pl.multiple_of(start, size), size)


def factor_segment(links, cells, rows, fwd_p, bwd_p, near, far, gains, carry=None):
    def body(keep, i, carry):
        s_f, g_f, s_b, g_b = carry
        j = cells - 1 - i
        here, there = plane(i, rows), plane(j, rows)
        w, e = links[here], links[plane(i + 1, rows)]
        t = 1.0 + w * s_f
        p = inverse(t + e)
        s_f = t * p
        g_f = g_f * (w * p)
        fwd_p[here] = p
        if keep:
            near[here], far[here] = e * p, g_f
        w, e = links[there], links[plane(j + 1, rows)]
        t = 1.0 + e * s_b
        p = inverse(t + w)
        s_b = t * p
        g_b = g_b * (e * p)
        bwd_p[there] = p
        if keep:
            near[there], far[there] = w * p, g_b
        return s_f, g_f, s_b, g_b

    half = cells // 2
    if carry is None:
        ones = jnp.ones((rows, 128), jnp.float32)
        return steps(half, 4, functools.partial(body, False), (ones, ones, ones, ones))
    _, g_f, _, g_b = steps(half, 4, lambda i, carry: body(True, i + half, carry), carry)
    gains[0] = near[plane(0, rows)]
    gains[1] = g_b
    gains[2] = g_f
    gains[3] = near[plane(cells - 1, rows)]


def sweep_values(rhs, links, cells, rows, fwd_p, bwd_p, value, ends):
    def body(keep, i, carry):
        y_f, y_b = carry
        j = cells - 1 - i
        here, there = plane(i, rows), plane(j, rows)
        y_f = (rhs[here] + links[here] * y_f) * fwd_p[here]
        y_b = (rhs[there] + links[plane(j + 1, rows)] * y_b) * bwd_p[there]
        if keep:
            value[here], value[there] = y_f, y_b
        return y_f, y_b

    half = cells // 2
    zeros = jnp.zeros((rows, 128), jnp.float32)
    carry = steps(half, 4, functools.partial(body, False), (zeros, zeros))
    y_f, y_b = steps(half, 4, lambda i, carry: body(True, i + half, carry), carry)
    ends[0] = y_b
    ends[1] = y_f


def back_substitute(before, after, cells, rows, near, far, value, unroll, store):
    def lap(block, carry):
        low, high = carry
        lows, highs = [], []
        for u in range(unroll):
            i = block * unroll + u
            here, there = plane(i, rows), plane(cells - 1 - i, rows)
            low = (value[here] + far[here] * after) + near[here] * low
            high = (value[there] + far[there] * before) + near[there] * high
            lows.append(low)
            highs.append(high)
        store(block, lows, highs)
        return low, high

    lax.fori_loop(0, cells // 2 // unroll, lap, (before, after))


class Reduced:
    def __init__(self, axis, rows, refs):
        self.axis, self.count, self.me = axis, lax.axis_size(axis), lax.axis_index(axis)
        self.owners = min(self.count, rows // ROWS)
        self.rows = rows // self.owners
        self.stride = self.count // self.owners
        self.mine = lax.rem(self.me, self.stride) == 0
        self.group = self.me // self.stride
        (self.gains, self.ends, self.all_gains, self.all_ends, self.relation, self.reply, self.sides) = refs[:7]
        (self.gain_send, self.gain_recv, self.end_send, self.end_recv, self.reply_send, self.reply_recv) = refs[7:]

    def copy(self, src, dst, send, recv, to):
        return pltpu.make_async_remote_copy(
            src_ref=src, dst_ref=dst, send_sem=send, recv_sem=recv,
            device_id={self.axis: to}, device_id_type=MESH,
        )

    def to_owner(self, o, source, everyone, send, recv):
        return self.copy(
            source.at[:, pl.ds(o * self.rows, self.rows), :], everyone.at[self.me],
            send.at[o], recv.at[self.me], o * self.stride,
        )

    def spread(self, source, everyone, send, recv):
        for o in range(self.owners):

            @pl.when(self.me != o * self.stride)
            def _():
                self.to_owner(o, source, everyone, send, recv).start()

            @pl.when(self.me == o * self.stride)
            def _():
                everyone[o * self.stride] = source[:, o * self.rows : (o + 1) * self.rows, :]

    def send_gains(self):
        self.spread(self.gains, self.all_gains, self.gain_send, self.gain_recv)

    def send_ends(self):
        self.spread(self.ends, self.all_ends, self.end_send, self.end_recv)

    def arrived(self, everyone, recv):
        for d in range(1, self.count):
            k = lax.rem(self.me + d, self.count)
            self.copy(everyone.at[k], everyone.at[k], recv.at[k], recv.at[k], k).wait_recv()

    def factor(self):
        @pl.when(self.mine)
        def _():
            self.arrived(self.all_gains, self.gain_recv)
            gain = jnp.zeros((self.rows, 128), jnp.float32)
            for k in range(self.count):
                head_west, head_east = self.all_gains[k, 0], self.all_gains[k, 1]
                tail_west, tail_east = self.all_gains[k, 2], self.all_gains[k, 3]
                scale = inverse(1.0 - head_west * gain)
                beta, gamma = head_east * scale, tail_west * gain
                self.relation[k, 0], self.relation[k, 1] = scale, beta
                self.relation[k, 2], self.relation[k, 3] = gamma, gain
                gain = tail_east + gamma * beta

    def reply_copy(self, k):
        return self.copy(
            self.reply.at[k], self.sides.at[self.group],
            self.reply_send.at[k], self.reply_recv.at[self.group], k,
        )

    def solve(self):
        @pl.when(self.mine)
        def _():
            self.arrived(self.all_ends, self.end_recv)
            value = jnp.zeros((self.rows, 128), jnp.float32)
            alphas, values = [], []
            for k in range(self.count):
                values.append(value)
                scale, gamma = self.relation[k, 0], self.relation[k, 2]
                head_west, tail_west = self.all_gains[k, 0], self.all_gains[k, 2]
                alpha = (self.all_ends[k, 0] + head_west * value) * scale
                value = (self.all_ends[k, 1] + tail_west * value) + gamma * alpha
                alphas.append(alpha)
            after = jnp.zeros((self.rows, 128), jnp.float32)
            for k in reversed(range(self.count)):
                self.reply[k, 1] = after
                after = alphas[k] + self.relation[k, 1] * after
                self.reply[k, 0] = values[k] + self.relation[k, 3] * after
            for d in range(1, self.count):
                self.reply_copy(lax.rem(self.me + d, self.count)).start()
            self.sides[self.group] = self.reply[self.me]

    def result(self):
        for o in range(self.owners):

            @pl.when(self.me != o * self.stride)
            def _():
                self.copy(
                    self.sides.at[o], self.sides.at[o], self.reply_recv.at[o], self.reply_recv.at[o],
                    o * self.stride,
                ).wait_recv()

        whole = (self.owners * self.rows, 128)
        return self.sides[:, 0].reshape(whole), self.sides[:, 1].reshape(whole)

    def drain(self):
        for o in range(self.owners):

            @pl.when(self.me != o * self.stride)
            def _():
                self.to_owner(o, self.gains, self.all_gains, self.gain_send, self.gain_recv).wait_send()
                self.to_owner(o, self.ends, self.all_ends, self.end_send, self.end_recv).wait_send()

        @pl.when(self.mine)
        def _():
            for d in range(1, self.count):
                self.reply_copy(lax.rem(self.me + d, self.count)).wait_send()


def reduced_scratch(count, rows):
    owners = min(count, rows // ROWS)
    part = rows // owners
    dma = pltpu.SemaphoreType.DMA
    return [
        pltpu.VMEM((4, rows, 128), jnp.float32),
        pltpu.VMEM((2, rows, 128), jnp.float32),
        pltpu.VMEM((count, 4, part, 128), jnp.float32),
        pltpu.VMEM((count, 2, part, 128), jnp.float32),
        pltpu.VMEM((count, 4, part, 128), jnp.float32),
        pltpu.VMEM((count, 2, part, 128), jnp.float32),
        pltpu.VMEM((owners, 2, part, 128), jnp.float32),
        dma((owners,)), dma((count,)), dma((owners,)), dma((count,)), dma((count,)), dma((owners,)),
    ]


def kernel(X, Y, h_in, c_in, q_in, out, *scratch):
    Z = 128
    chunks = X * Y // 128
    (stage_x, stage_y, halo_x, halo_y, halo_send, halo_recv, force, link_x, link_y, link_z) = scratch[:10]
    fwd_x, bwd_x, near_x, far_x, value_x, fwd_y, bwd_y, near_y, far_y, value_y = scratch[10:20]
    first, up_z, piv_z, lag_z, lead_z, val_z, h, c, q, load_sem = scratch[20:30]
    along_x = Reduced("gx", Y, scratch[30:43])
    along_y = Reduced("gy", X, scratch[43:56])
    nx, ny, me_x, me_y = along_x.count, along_y.count, along_x.me, along_y.me

    loads = [
        pltpu.make_async_copy(src, dst, load_sem.at[k])
        for k, (src, dst) in enumerate(((h_in, h), (c_in, c), (q_in, q)))
    ]
    for load in loads:
        load.start()
    barrier = pltpu.get_barrier_semaphore()
    for d in range(1, nx):
        pl.semaphore_signal(barrier, inc=1, device_id={"gx": lax.rem(me_x + d, nx)}, device_id_type=MESH)
    for d in range(1, ny):
        pl.semaphore_signal(barrier, inc=1, device_id={"gy": lax.rem(me_y + d, ny)}, device_id_type=MESH)

    loads[0].wait()
    loads[1].wait()

    def column(j):
        return pl.ds(j, X, stride=Y)

    for side, (i, j) in enumerate(((0, 0), (X - 1, Y - 1))):
        stage_x[side, 0], stage_x[side, 1] = h[plane(i, Y)], c[plane(i, Y)]
        stage_y[side, 0], stage_y[side, 1] = h[column(j), :], c[column(j), :]

    loads[2].wait()

    def along_first(i, carry):
        head, cond, flux = carry
        here, ahead = plane(i, Y), plane(jnp.minimum(i + 1, X - 1), Y)
        head_next, cond_next = h[ahead], c[ahead]
        east = link(COEF_X, cond, cond_next)
        link_x[plane(i + 1, Y)] = east
        flux_next = east * (head_next - head)
        force[here] = 2.0 * (flux_next - flux) + q[here]
        return head_next, cond_next, flux_next

    steps(X, 2, along_first, (h[plane(0, Y)], c[plane(0, Y)], jnp.zeros((Y, 128), jnp.float32)))
    pl.semaphore_wait(barrier, nx - 1 + ny - 1)

    halos = []
    for a, (axis, me, count, stage, halo) in enumerate(
        (("gx", me_x, nx, stage_x, halo_x), ("gy", me_y, ny, stage_y, halo_y))
    ):
        for side in (0, 1):
            to = me - 1 if side == 0 else me + 1
            inside = me > 0 if side == 0 else me < count - 1
            send = pltpu.make_async_remote_copy(
                src_ref=stage.at[side], dst_ref=halo.at[1 - side],
                send_sem=halo_send.at[2 * a + side], recv_sem=halo_recv.at[2 * a + 1 - side],
                device_id={axis: to}, device_id_type=MESH,
            )
            take = pltpu.make_async_remote_copy(
                src_ref=stage.at[side], dst_ref=halo.at[side],
                send_sem=halo_send.at[2 * a + side], recv_sem=halo_recv.at[2 * a + side],
                device_id={axis: to}, device_id_type=MESH,
            )
            halos.append((inside, send, take))

            @pl.when(inside)
            def _():
                send.start()

            @pl.when(jnp.logical_not(inside))
            def _():
                halo[side] = jnp.zeros((2,) + halo.shape[2:], jnp.float32)

    inner = lax.broadcasted_iota(jnp.int32, (X, 128), 1) < Z - 1

    def depth_and_second(j, carry):
        head, cond, flux = carry
        up = jnp.where(inner, link(COEF_Z, cond, pltpu.roll(cond, Z - 1, 1)), 0.0)
        link_z[plane(j, X)] = up
        rise = up * (pltpu.roll(head, Z - 1, 1) - head)
        ahead = jnp.minimum(j + 1, Y - 1)
        head_next, cond_next = h[column(ahead), :], c[column(ahead), :]
        north = link(COEF_Y, cond, cond_next)
        link_y[plane(j + 1, X)] = north
        flux_next = north * (head_next - head)
        force[column(j), :] += 2.0 * ((rise - pltpu.roll(rise, 1, 1)) + (flux_next - flux))
        return head_next, cond_next, flux_next

    steps(Y, 2, depth_and_second, (h[column(0), :], c[column(0), :], jnp.zeros((X, 128), jnp.float32)))

    for inside, _, take in halos:

        @pl.when(inside)
        def _():
            take.wait_recv()

    low = link(COEF_X, halo_x[0, 1], c[plane(0, Y)])
    high = link(COEF_X, halo_x[1, 1], c[plane(X - 1, Y)])
    link_x[plane(0, Y)], link_x[plane(X, Y)] = low, high
    force[plane(0, Y)] += 2.0 * (low * (halo_x[0, 0] - h[plane(0, Y)]))
    force[plane(X - 1, Y)] += 2.0 * (high * (halo_x[1, 0] - h[plane(X - 1, Y)]))
    low = link(COEF_Y, halo_y[0, 1], c[column(0), :])
    high = link(COEF_Y, halo_y[1, 1], c[column(Y - 1), :])
    link_y[plane(0, X)], link_y[plane(Y, X)] = low, high
    force[column(0), :] += 2.0 * (low * (halo_y[0, 0] - h[column(0), :]))
    force[column(Y - 1), :] += 2.0 * (high * (halo_y[1, 0] - h[column(Y - 1), :]))

    segment_x = (link_x, X, Y, fwd_x, bwd_x, near_x, far_x, along_x.gains)
    factor_segment(*segment_x, factor_segment(*segment_x))
    along_x.send_gains()
    sweep_values(force, link_x, X, Y, fwd_x, bwd_x, value_x, along_x.ends)
    along_x.send_ends()

    segment_y = (link_y, Y, X, fwd_y, bwd_y, near_y, far_y, along_y.gains)
    along_x.factor()
    halfway = factor_segment(*segment_y)
    along_x.solve()
    factor_segment(*segment_y, halfway)
    along_y.send_gains()

    before, after = along_x.result()

    def store_first(block, lows, highs):
        for u in range(4):
            i = block * 4 + u
            first[pl.ds(i, Y, stride=X), :] = lows[u]
            first[pl.ds(X - 1 - i, Y, stride=X), :] = highs[u]

    back_substitute(before, after, X, Y, near_x, far_x, value_x, 4, store_first)

    sweep_values(first, link_y, Y, X, fwd_y, bwd_y, value_y, along_y.ends)
    along_y.send_ends()
    along_y.factor()

    def turn_links(k, carry):
        up_z[pl.ds(k, Z, stride=chunks), :] = link_z[plane(k, 128)].T
        return carry

    steps(chunks, 2, turn_links, 0)
    half = Z // 2

    def factor_z(i, carry):
        s_f, w, s_b, e = carry
        here, there = plane(i, chunks), plane(Z - 1 - i, chunks)
        ahead = up_z[here]
        t = 1.0 + w * s_f
        p = inverse(t + ahead)
        s_f = t * p
        piv_z[here], lag_z[here], lead_z[here] = p, w * p, ahead * p
        behind = up_z[plane(Z - 2 - i, chunks)]
        t = 1.0 + e * s_b
        p = inverse(t + behind)
        s_b = t * p
        piv_z[there], lag_z[there], lead_z[there] = p, e * p, behind * p
        return s_f, ahead, s_b, behind

    def factor_part(start, stop, carry):
        return steps(stop - start, 4, lambda i, carry: factor_z(i + start, carry), carry)

    ones, zeros = (jnp.full((chunks, 128), v, jnp.float32) for v in (1.0, 0.0))
    carry = factor_part(0, 16, (ones, zeros, ones, zeros))
    along_y.solve()
    s_f, _, s_b, _ = factor_part(16, half, carry)
    middle = inverse(s_f + s_b * lead_z[plane(half - 1, chunks)])
    before, after = along_y.result()
    per_chunk = 128 // X

    def store_second(block, lows, highs):
        val_z[pl.ds(block, Z, stride=chunks), :] = jnp.concatenate(lows, 0).T
        val_z[pl.ds(chunks - 1 - block, Z, stride=chunks), :] = jnp.concatenate(highs[::-1], 0).T

    back_substitute(before, after, Y, X, near_y, far_y, value_y, per_chunk, store_second)

    def sweep_z(i, carry):
        y_f, y_b = carry
        here, there = plane(i, chunks), plane(Z - 1 - i, chunks)
        y_f = val_z[here] * piv_z[here] + lag_z[here] * y_f
        y_b = val_z[there] * piv_z[there] + lag_z[there] * y_b
        val_z[here], val_z[there] = y_f, y_b
        return y_f, y_b

    y_f, y_b = steps(half, 8, sweep_z, (zeros, zeros))
    below = (y_f + lead_z[plane(half - 1, chunks)] * y_b) * middle
    above = y_b + lead_z[plane(half, chunks)] * below

    def back_z(i, carry):
        low, high = carry
        here, there = plane(half - 1 - i, chunks), plane(half + i, chunks)
        out[here], out[there] = low, high
        nearer, farther = plane(jnp.maximum(half - 2 - i, 0), chunks), plane(jnp.minimum(half + 1 + i, Z - 1), chunks)
        low = val_z[nearer] + lead_z[nearer] * low
        high = val_z[farther] + lead_z[farther] * high
        return low, high

    steps(half, 8, back_z, (below, above))

    for inside, send, _ in halos:

        @pl.when(inside)
        def _():
            send.wait_send()

    along_x.drain()
    along_y.drain()


def finish(X, Y, delta, h, out):
    chunks, per_chunk = X * Y // 128, 128 // X

    def write(k, carry):
        lines = delta[pl.ds(k, 128, stride=chunks), :].T
        for part in range(per_chunk):
            at = pl.ds(k * per_chunk + part, X, stride=Y)
            out[at, :] = h[at, :] + lines[part * X : (part + 1) * X]
        return carry

    steps(chunks, 2, write, 0)


def per_device(water_head, conductivity, recharge):
    X, Y, Z = water_head.shape
    nx, ny = lax.axis_size("gx"), lax.axis_size("gy")

    def vmem(*shape):
        return pltpu.VMEM(shape, jnp.float32)

    cells = X * Y
    scratch = [
        vmem(2, 2, Y, Z), vmem(2, 2, X, Z), vmem(2, 2, Y, Z), vmem(2, 2, X, Z),
        pltpu.SemaphoreType.DMA((4,)), pltpu.SemaphoreType.DMA((4,)),
        vmem(cells, Z), vmem(cells + Y, Z), vmem(cells + X, Z), vmem(cells, Z),
    ]
    scratch += [vmem(cells, Z) for _ in range(19)] + [pltpu.SemaphoreType.DMA((3,))]
    scratch += reduced_scratch(nx, Y) + reduced_scratch(ny, X)
    flat = [array.reshape(cells, Z) for array in (water_head, conductivity, recharge)]
    delta = pl.pallas_call(
        functools.partial(kernel, X, Y),
        out_shape=jax.ShapeDtypeStruct((cells, Z), jnp.float32),
        in_specs=[pl.BlockSpec(memory_space=pl.ANY)] * 3,
        out_specs=pl.BlockSpec(memory_space=pltpu.VMEM),
        scratch_shapes=scratch,
        compiler_params=pltpu.CompilerParams(
            collective_id=0, has_side_effects=True, vmem_limit_bytes=56 * 2**20
        ),
    )(*flat)
    result = pl.pallas_call(
        functools.partial(finish, X, Y),
        out_shape=jax.ShapeDtypeStruct((cells, Z), jnp.float32),
        in_specs=[pl.BlockSpec(memory_space=pltpu.VMEM)] * 2,
        out_specs=pl.BlockSpec(memory_space=pltpu.VMEM),
        compiler_params=pltpu.CompilerParams(vmem_limit_bytes=16 * 2**20),
    )(delta, flat[0])
    return result.reshape(X, Y, Z)


def solution(mesh):
    placed = (P("gx", "gy", None), P("gx", "gy", None), P("gx", "gy", None))
    return jax.shard_map(
        per_device, mesh=mesh, in_specs=placed, out_specs=P("gx", "gy", None), check_vma=False
    )
```

```python
import functools

import jax
import jax.numpy as jnp
from jax import lax
from jax.experimental import pallas as pl
from jax.experimental.pallas import tpu as pltpu
from jax.sharding import PartitionSpec as P

COEF_Z = 8
COEF_X = 5120
COEF_Y = 5120
ROWS = 8
PARTS = 4
MESH = pl.DeviceIdType.MESH


def inverse(x):
    return pl.reciprocal(x, approx=True, full_range=False)


def link(coef, one_side, other_side):
    return (coef * one_side * other_side) * inverse(one_side + other_side)


def steps(count, unroll, body, carry):
    def lap(block, carry):
        for u in range(unroll):
            carry = body(block * unroll + u, carry)
        return carry

    return lax.fori_loop(0, count // unroll, lap, carry)


def plane(i, size):
    start = i * size
    return pl.ds(start if isinstance(i, int) else pl.multiple_of(start, size), size)


def factor_segment(links, cells, rows, fwd_p, bwd_p, near, far, gains, carry=None):
    def body(keep, i, carry):
        s_f, g_f, s_b, g_b = carry
        j = cells - 1 - i
        here, there = plane(i, rows), plane(j, rows)
        w, e = links[here], links[plane(i + 1, rows)]
        t = 1.0 + w * s_f
        p = inverse(t + e)
        s_f = t * p
        g_f = g_f * (w * p)
        fwd_p[here] = p
        if keep:
            near[here], far[here] = e * p, g_f
        w, e = links[there], links[plane(j + 1, rows)]
        t = 1.0 + e * s_b
        p = inverse(t + w)
        s_b = t * p
        g_b = g_b * (e * p)
        bwd_p[there] = p
        if keep:
            near[there], far[there] = w * p, g_b
        return s_f, g_f, s_b, g_b

    half = cells // 2
    if carry is None:
        ones = jnp.ones((rows, 128), jnp.float32)
        return steps(half, 4, functools.partial(body, False), (ones, ones, ones, ones))
    _, g_f, _, g_b = steps(half, 4, lambda i, carry: body(True, i + half, carry), carry)
    gains[0] = near[plane(0, rows)]
    gains[1] = g_b
    gains[2] = g_f
    gains[3] = near[plane(cells - 1, rows)]


def sweep_values(rhs, links, cells, rows, fwd_p, bwd_p, value, ends):
    def body(keep, i, carry):
        y_f, y_b = carry
        j = cells - 1 - i
        here, there = plane(i, rows), plane(j, rows)
        y_f = (rhs[here] + links[here] * y_f) * fwd_p[here]
        y_b = (rhs[there] + links[plane(j + 1, rows)] * y_b) * bwd_p[there]
        if keep:
            value[here], value[there] = y_f, y_b
        return y_f, y_b

    half = cells // 2
    zeros = jnp.zeros((rows, 128), jnp.float32)
    carry = steps(half, 8, functools.partial(body, False), (zeros, zeros))
    y_f, y_b = steps(half, 8, lambda i, carry: body(True, i + half, carry), carry)
    ends[0] = y_b
    ends[1] = y_f


def back_substitute(before, after, cells, rows, near, far, value, unroll, store):
    def lap(block, carry):
        low, high = carry
        lows, highs = [], []
        for u in range(unroll):
            i = block * unroll + u
            here, there = plane(i, rows), plane(cells - 1 - i, rows)
            low = (value[here] + far[here] * after) + near[here] * low
            high = (value[there] + far[there] * before) + near[there] * high
            lows.append(low)
            highs.append(high)
        store(block, lows, highs)
        return low, high

    lax.fori_loop(0, cells // 2 // unroll, lap, (before, after))


class Reduced:
    def __init__(self, axis, rows, refs):
        self.axis, self.count, self.me = axis, lax.axis_size(axis), lax.axis_index(axis)
        self.owners = min(self.count, rows // ROWS)
        self.rows = rows // self.owners
        self.stride = self.count // self.owners
        self.mine = lax.rem(self.me, self.stride) == 0
        self.group = self.me // self.stride
        (self.gains, self.ends, self.all_gains, self.all_ends, self.relation, self.reply, self.sides) = refs[:7]
        (self.gain_send, self.gain_recv, self.end_send, self.end_recv, self.reply_send, self.reply_recv) = refs[7:]

    def copy(self, src, dst, send, recv, to):
        return pltpu.make_async_remote_copy(
            src_ref=src, dst_ref=dst, send_sem=send, recv_sem=recv,
            device_id={self.axis: to}, device_id_type=MESH,
        )

    def to_owner(self, o, source, everyone, send, recv):
        return self.copy(
            source.at[:, pl.ds(o * self.rows, self.rows), :], everyone.at[self.me],
            send.at[o], recv.at[self.me], o * self.stride,
        )

    def spread(self, source, everyone, send, recv):
        for o in range(self.owners):

            @pl.when(self.me != o * self.stride)
            def _():
                self.to_owner(o, source, everyone, send, recv).start()

            @pl.when(self.me == o * self.stride)
            def _():
                everyone[o * self.stride] = source[:, o * self.rows : (o + 1) * self.rows, :]

    def send_gains(self):
        self.spread(self.gains, self.all_gains, self.gain_send, self.gain_recv)

    def send_ends(self):
        self.spread(self.ends, self.all_ends, self.end_send, self.end_recv)

    def arrived(self, everyone, recv):
        for d in range(1, self.count):
            k = lax.rem(self.me + d, self.count)
            self.copy(everyone.at[k], everyone.at[k], recv.at[k], recv.at[k], k).wait_recv()

    def factor(self):
        @pl.when(self.mine)
        def _():
            self.arrived(self.all_gains, self.gain_recv)
            gain = jnp.zeros((self.rows, 128), jnp.float32)
            for k in range(self.count):
                head_west, head_east = self.all_gains[k, 0], self.all_gains[k, 1]
                tail_west, tail_east = self.all_gains[k, 2], self.all_gains[k, 3]
                scale = inverse(1.0 - head_west * gain)
                beta, gamma = head_east * scale, tail_west * gain
                self.relation[k, 0], self.relation[k, 1] = scale, beta
                self.relation[k, 2], self.relation[k, 3] = gamma, gain
                gain = tail_east + gamma * beta

    def reply_copy(self, k):
        return self.copy(
            self.reply.at[k], self.sides.at[self.group],
            self.reply_send.at[k], self.reply_recv.at[self.group], k,
        )

    def solve(self):
        @pl.when(self.mine)
        def _():
            self.arrived(self.all_ends, self.end_recv)
            value = jnp.zeros((self.rows, 128), jnp.float32)
            alphas, values = [], []
            for k in range(self.count):
                values.append(value)
                scale, gamma = self.relation[k, 0], self.relation[k, 2]
                head_west, tail_west = self.all_gains[k, 0], self.all_gains[k, 2]
                alpha = (self.all_ends[k, 0] + head_west * value) * scale
                value = (self.all_ends[k, 1] + tail_west * value) + gamma * alpha
                alphas.append(alpha)
            after = jnp.zeros((self.rows, 128), jnp.float32)
            for k in reversed(range(self.count)):
                self.reply[k, 1] = after
                after = alphas[k] + self.relation[k, 1] * after
                self.reply[k, 0] = values[k] + self.relation[k, 3] * after
            for d in range(1, self.count):
                self.reply_copy(lax.rem(self.me + d, self.count)).start()
            self.sides[self.group] = self.reply[self.me]

    def result(self):
        for o in range(self.owners):

            @pl.when(self.me != o * self.stride)
            def _():
                self.copy(
                    self.sides.at[o], self.sides.at[o], self.reply_recv.at[o], self.reply_recv.at[o],
                    o * self.stride,
                ).wait_recv()

        whole = (self.owners * self.rows, 128)
        return self.sides[:, 0].reshape(whole), self.sides[:, 1].reshape(whole)

    def drain(self):
        for o in range(self.owners):

            @pl.when(self.me != o * self.stride)
            def _():
                self.to_owner(o, self.gains, self.all_gains, self.gain_send, self.gain_recv).wait_send()
                self.to_owner(o, self.ends, self.all_ends, self.end_send, self.end_recv).wait_send()

        @pl.when(self.mine)
        def _():
            for d in range(1, self.count):
                self.reply_copy(lax.rem(self.me + d, self.count)).wait_send()


def reduced_scratch(count, rows):
    owners = min(count, rows // ROWS)
    part = rows // owners
    dma = pltpu.SemaphoreType.DMA
    return [
        pltpu.VMEM((4, rows, 128), jnp.float32),
        pltpu.VMEM((2, rows, 128), jnp.float32),
        pltpu.VMEM((count, 4, part, 128), jnp.float32),
        pltpu.VMEM((count, 2, part, 128), jnp.float32),
        pltpu.VMEM((count, 4, part, 128), jnp.float32),
        pltpu.VMEM((count, 2, part, 128), jnp.float32),
        pltpu.VMEM((owners, 2, part, 128), jnp.float32),
        dma((owners,)), dma((count,)), dma((owners,)), dma((count,)), dma((count,)), dma((owners,)),
    ]


def kernel(X, Y, h_in, c_in, q_in, out, *scratch):
    Z = 128
    chunks = X * Y // 128
    (stage_x, stage_y, halo_x, halo_y, halo_send, halo_recv, force, link_x, link_y, link_z) = scratch[:10]
    fwd_x, bwd_x, near_x, far_x, value_x, fwd_y, bwd_y, near_y, far_y, value_y = scratch[10:20]
    first, up_z, piv_z, lag_z, lead_z, val_z, low_z, delta, h, c, q, load_sem, delta_sem = scratch[20:33]
    along_x = Reduced("gx", Y, scratch[33:46])
    along_y = Reduced("gy", X, scratch[46:59])
    nx, ny, me_x, me_y = along_x.count, along_y.count, along_x.me, along_y.me

    part = X * Y // PARTS
    loads = [
        pltpu.make_async_copy(src.at[pl.ds(m * part, part)], dst.at[pl.ds(m * part, part)], load_sem.at[k, m])
        for k, (src, dst) in enumerate(((h_in, h), (c_in, c), (q_in, q)))
        for m in range(PARTS)
    ]
    for load in loads:
        load.start()
    barrier = pltpu.get_barrier_semaphore()
    for d in range(1, nx):
        pl.semaphore_signal(barrier, inc=1, device_id={"gx": lax.rem(me_x + d, nx)}, device_id_type=MESH)
    for d in range(1, ny):
        pl.semaphore_signal(barrier, inc=1, device_id={"gy": lax.rem(me_y + d, ny)}, device_id_type=MESH)

    for load in loads[: 2 * PARTS]:
        load.wait()

    def column(j):
        return pl.ds(j, X, stride=Y)

    for side, (i, j) in enumerate(((0, 0), (X - 1, Y - 1))):
        stage_x[side, 0], stage_x[side, 1] = h[plane(i, Y)], c[plane(i, Y)]
        stage_y[side, 0], stage_y[side, 1] = h[column(j), :], c[column(j), :]

    for load in loads[2 * PARTS :]:
        load.wait()

    def along_first(i, carry):
        head, cond, flux = carry
        here, ahead = plane(i, Y), plane(jnp.minimum(i + 1, X - 1), Y)
        head_next, cond_next = h[ahead], c[ahead]
        east = link(COEF_X, cond, cond_next)
        link_x[plane(i + 1, Y)] = east
        flux_next = east * (head_next - head)
        force[here] = 2.0 * (flux_next - flux) + q[here]
        return head_next, cond_next, flux_next

    steps(X, 4, along_first, (h[plane(0, Y)], c[plane(0, Y)], jnp.zeros((Y, 128), jnp.float32)))
    pl.semaphore_wait(barrier, nx - 1 + ny - 1)

    halos = []
    for a, (axis, me, count, stage, halo) in enumerate(
        (("gx", me_x, nx, stage_x, halo_x), ("gy", me_y, ny, stage_y, halo_y))
    ):
        for side in (0, 1):
            to = me - 1 if side == 0 else me + 1
            inside = me > 0 if side == 0 else me < count - 1
            send = pltpu.make_async_remote_copy(
                src_ref=stage.at[side], dst_ref=halo.at[1 - side],
                send_sem=halo_send.at[2 * a + side], recv_sem=halo_recv.at[2 * a + 1 - side],
                device_id={axis: to}, device_id_type=MESH,
            )
            take = pltpu.make_async_remote_copy(
                src_ref=stage.at[side], dst_ref=halo.at[side],
                send_sem=halo_send.at[2 * a + side], recv_sem=halo_recv.at[2 * a + side],
                device_id={axis: to}, device_id_type=MESH,
            )
            halos.append((inside, send, take))

            @pl.when(inside)
            def _():
                send.start()

            @pl.when(jnp.logical_not(inside))
            def _():
                halo[side] = jnp.zeros((2,) + halo.shape[2:], jnp.float32)

    inner = lax.broadcasted_iota(jnp.int32, (X, 128), 1) < Z - 1

    def depth_and_second(j, carry):
        head, cond, flux = carry
        up = jnp.where(inner, link(COEF_Z, cond, pltpu.roll(cond, Z - 1, 1)), 0.0)
        link_z[plane(j, X)] = up
        rise = up * (pltpu.roll(head, Z - 1, 1) - head)
        ahead = jnp.minimum(j + 1, Y - 1)
        head_next, cond_next = h[column(ahead), :], c[column(ahead), :]
        north = link(COEF_Y, cond, cond_next)
        link_y[plane(j + 1, X)] = north
        flux_next = north * (head_next - head)
        force[column(j), :] += 2.0 * ((rise - pltpu.roll(rise, 1, 1)) + (flux_next - flux))
        return head_next, cond_next, flux_next

    steps(Y, 4, depth_and_second, (h[column(0), :], c[column(0), :], jnp.zeros((X, 128), jnp.float32)))

    for inside, _, take in halos:

        @pl.when(inside)
        def _():
            take.wait_recv()

    low = link(COEF_X, halo_x[0, 1], c[plane(0, Y)])
    high = link(COEF_X, halo_x[1, 1], c[plane(X - 1, Y)])
    link_x[plane(0, Y)], link_x[plane(X, Y)] = low, high
    force[plane(0, Y)] += 2.0 * (low * (halo_x[0, 0] - h[plane(0, Y)]))
    force[plane(X - 1, Y)] += 2.0 * (high * (halo_x[1, 0] - h[plane(X - 1, Y)]))
    low = link(COEF_Y, halo_y[0, 1], c[column(0), :])
    high = link(COEF_Y, halo_y[1, 1], c[column(Y - 1), :])
    link_y[plane(0, X)], link_y[plane(Y, X)] = low, high
    force[column(0), :] += 2.0 * (low * (halo_y[0, 0] - h[column(0), :]))
    force[column(Y - 1), :] += 2.0 * (high * (halo_y[1, 0] - h[column(Y - 1), :]))

    segment_x = (link_x, X, Y, fwd_x, bwd_x, near_x, far_x, along_x.gains)
    factor_segment(*segment_x, factor_segment(*segment_x))
    along_x.send_gains()
    sweep_values(force, link_x, X, Y, fwd_x, bwd_x, value_x, along_x.ends)
    along_x.send_ends()

    segment_y = (link_y, Y, X, fwd_y, bwd_y, near_y, far_y, along_y.gains)
    along_x.factor()
    halfway = factor_segment(*segment_y)
    along_x.solve()
    factor_segment(*segment_y, halfway)
    along_y.send_gains()

    before, after = along_x.result()

    def store_first(block, lows, highs):
        for u in range(4):
            i = block * 4 + u
            first[pl.ds(i, Y, stride=X), :] = lows[u]
            first[pl.ds(X - 1 - i, Y, stride=X), :] = highs[u]

    back_substitute(before, after, X, Y, near_x, far_x, value_x, 4, store_first)

    sweep_values(first, link_y, Y, X, fwd_y, bwd_y, value_y, along_y.ends)
    along_y.send_ends()
    along_y.factor()

    def turn_links(k, carry):
        up_z[pl.ds(k, Z, stride=chunks), :] = link_z[plane(k, 128)].T
        return carry

    steps(chunks, 2, turn_links, 0)
    half = Z // 2

    def factor_z(i, carry):
        s_f, w, s_b, e = carry
        here, there = plane(i, chunks), plane(Z - 1 - i, chunks)
        ahead = up_z[here]
        t = 1.0 + w * s_f
        p = inverse(t + ahead)
        s_f = t * p
        piv_z[here], lag_z[here], lead_z[here] = p, w * p, ahead * p
        behind = up_z[plane(Z - 2 - i, chunks)]
        t = 1.0 + e * s_b
        p = inverse(t + behind)
        s_b = t * p
        piv_z[there], lag_z[there], lead_z[there] = p, e * p, behind * p
        return s_f, ahead, s_b, behind

    def factor_part(start, stop, carry):
        return steps(stop - start, 4, lambda i, carry: factor_z(i + start, carry), carry)

    ones, zeros = (jnp.full((chunks, 128), v, jnp.float32) for v in (1.0, 0.0))
    carry = factor_part(0, 16, (ones, zeros, ones, zeros))
    along_y.solve()
    s_f, _, s_b, _ = factor_part(16, half, carry)
    middle = inverse(s_f + s_b * lead_z[plane(half - 1, chunks)])
    before, after = along_y.result()
    per_chunk = 128 // X

    def store_second(block, lows, highs):
        val_z[pl.ds(block, Z, stride=chunks), :] = jnp.concatenate(lows, 0).T
        val_z[pl.ds(chunks - 1 - block, Z, stride=chunks), :] = jnp.concatenate(highs[::-1], 0).T

    back_substitute(before, after, Y, X, near_y, far_y, value_y, per_chunk, store_second)

    def sweep_z(i, carry):
        y_f, y_b = carry
        here, there = plane(i, chunks), plane(Z - 1 - i, chunks)
        y_f = val_z[here] * piv_z[here] + lag_z[here] * y_f
        y_b = val_z[there] * piv_z[there] + lag_z[there] * y_b
        low_z[here], low_z[there] = y_f, y_b
        return y_f, y_b

    y_f, y_b = steps(half, 16, sweep_z, (zeros, zeros))
    below = (y_f + lead_z[plane(half - 1, chunks)] * y_b) * middle
    above = y_b + lead_z[plane(half, chunks)] * below

    def back_z(i, carry):
        low, high = carry
        delta[pl.ds(half - 1 - i, chunks, stride=Z), :] = low
        delta[pl.ds(half + i, chunks, stride=Z), :] = high
        nearer, farther = plane(jnp.maximum(half - 2 - i, 0), chunks), plane(jnp.minimum(half + 1 + i, Z - 1), chunks)
        low = low_z[nearer] + lead_z[nearer] * low
        high = low_z[farther] + lead_z[farther] * high
        return low, high

    steps(half, 16, back_z, (below, above))

    gives = [
        pltpu.make_async_copy(delta.at[pl.ds(k * Z, Z)], out.at[pl.ds(k * Z, Z)], delta_sem.at[k])
        for k in range(chunks)
    ]
    for give in gives:
        give.start()

    for inside, send, _ in halos:

        @pl.when(inside)
        def _():
            send.wait_send()

    along_x.drain()
    along_y.drain()
    for give in gives:
        give.wait()


def finish(X, Y, delta_in, h, out, delta, total, load_sem, give_sem):
    Z, chunks, per_chunk = 128, X * Y // 128, 128 // X
    loads = [
        pltpu.make_async_copy(delta_in.at[pl.ds(k * Z, Z)], delta.at[pl.ds(k * Z, Z)], load_sem.at[k])
        for k in range(chunks)
    ]
    for load in loads:
        load.start()
    gives = []
    for k in range(chunks):
        loads[k].wait()
        lines = delta[k * Z : (k + 1) * Z].T
        for part in range(per_chunk):
            at = pl.ds(k * per_chunk + part, X, stride=Y)
            total[at, :] = h[at, :] + lines[part * X : (part + 1) * X]
        done = (k + 1) * per_chunk
        if done % 8 == 0:
            tile = pl.ds(done - 8, 8)
            gives.append(
                pltpu.make_async_copy(
                    total.reshape(X, Y, Z).at[:, tile, :], out.at[:, tile, :], give_sem.at[len(gives)]
                )
            )
            gives[-1].start()
    for give in gives:
        give.wait()


def per_device(water_head, conductivity, recharge):
    X, Y, Z = water_head.shape
    nx, ny = lax.axis_size("gx"), lax.axis_size("gy")

    def vmem(*shape):
        return pltpu.VMEM(shape, jnp.float32)

    cells = X * Y
    chunks = cells // 128
    scratch = [
        vmem(2, 2, Y, Z), vmem(2, 2, X, Z), vmem(2, 2, Y, Z), vmem(2, 2, X, Z),
        pltpu.SemaphoreType.DMA((4,)), pltpu.SemaphoreType.DMA((4,)),
        vmem(cells, Z), vmem(cells + Y, Z), vmem(cells + X, Z), vmem(cells, Z),
    ]
    scratch += [vmem(cells, Z) for _ in range(21)] + [pltpu.SemaphoreType.DMA((3, PARTS)), pltpu.SemaphoreType.DMA((chunks,))]
    scratch += reduced_scratch(nx, Y) + reduced_scratch(ny, X)
    flat = [array.reshape(cells, Z) for array in (water_head, conductivity, recharge)]
    delta = pl.pallas_call(
        functools.partial(kernel, X, Y),
        out_shape=jax.ShapeDtypeStruct((cells, Z), jnp.float32),
        in_specs=[pl.BlockSpec(memory_space=pl.ANY)] * 3,
        out_specs=pl.BlockSpec(memory_space=pl.ANY),
        scratch_shapes=scratch,
        compiler_params=pltpu.CompilerParams(
            collective_id=0, has_side_effects=True, vmem_limit_bytes=56 * 2**20
        ),
    )(*flat)
    return pl.pallas_call(
        functools.partial(finish, X, Y),
        out_shape=jax.ShapeDtypeStruct((X, Y, Z), jnp.float32),
        in_specs=[pl.BlockSpec(memory_space=pltpu.HBM), pl.BlockSpec(memory_space=pltpu.VMEM)],
        out_specs=pl.BlockSpec(memory_space=pl.ANY),
        scratch_shapes=[
            vmem(cells, Z), vmem(cells, Z),
            pltpu.SemaphoreType.DMA((chunks,)), pltpu.SemaphoreType.DMA((Y // 8,)),
        ],
        compiler_params=pltpu.CompilerParams(vmem_limit_bytes=16 * 2**20),
    )(delta, flat[0])


def solution(mesh):
    placed = (P("gx", "gy", None), P("gx", "gy", None), P("gx", "gy", None))
    return jax.shard_map(
        per_device, mesh=mesh, in_specs=placed, out_specs=P("gx", "gy", None), check_vma=False
    )
```

```python
import functools

import jax
import jax.numpy as jnp
from jax import lax
from jax.experimental import pallas as pl
from jax.experimental.pallas import tpu as pltpu
from jax.sharding import PartitionSpec as P

COEF_Z = 8
COEF_X = 5120
COEF_Y = 5120
ROWS = 8
PARTS = 4
MESH = pl.DeviceIdType.MESH


def inverse(x):
    return pl.reciprocal(x, approx=True, full_range=False)


def link(coef, one_side, other_side):
    return (coef * one_side * other_side) * inverse(one_side + other_side)


def blocks(start, stop, size, body, carry):
    return lax.fori_loop(start // size, stop // size, lambda block, carry: body(block * size, carry), carry)


def plane(i, size):
    start = i * size
    return pl.ds(start if isinstance(i, int) else pl.multiple_of(start, size), size)


def pivots(links, share):
    result = []
    for behind, ahead in zip(links[:-1], links[1:]):
        if not result:
            top = 1.0 + behind * share
            bottom = top + ahead
            scale = inverse(bottom)
            result.append(scale)
        else:
            top = bottom + behind * top
            below, bottom = bottom, top + ahead * bottom
            scale = inverse(bottom)
            result.append(below * scale)
    return result, top * scale


def factor_segment(links, cells, rows, fwd_p, bwd_p, near, far, gains, carry=None):
    size = 4

    def body(keep, i, carry):
        states, stores = [], []
        for (s, g), (p_ref, first, way) in zip(carry, ((fwd_p, i, 1), (bwd_p, cells - 1 - i, -1))):
            edge = first + (way < 0)
            beside = [links[plane(edge + way * u, rows)] for u in range(size + 1)]
            parts, s = pivots(beside, s)
            for u, p in enumerate(parts):
                at = plane(first + way * u, rows)
                g = g * (beside[u] * p)
                stores.append((p_ref, at, p))
                if keep:
                    stores += [(near, at, beside[u + 1] * p), (far, at, g)]
            states.append((s, g))
        for ref, at, value in stores:
            ref[at] = value
        return tuple(states)

    half = cells // 2
    if carry is None:
        ones = jnp.ones((rows, 128), jnp.float32)
        return blocks(0, half, size, functools.partial(body, False), ((ones, ones), (ones, ones)))
    (_, g_f), (_, g_b) = blocks(half, cells, size, functools.partial(body, True), carry)
    gains[0] = near[plane(0, rows)]
    gains[1] = g_b
    gains[2] = g_f
    gains[3] = near[plane(cells - 1, rows)]


def sweep_values(rhs, links, cells, rows, fwd_p, bwd_p, value, ends):
    size = 4

    def body(keep, i, carry):
        y_f, y_b = carry
        stores = []
        for u in range(size):
            j = cells - 1 - i - u
            here, there = plane(i + u, rows), plane(j, rows)
            p_f, p_b = fwd_p[here], bwd_p[there]
            y_f = rhs[here] * p_f + (links[here] * p_f) * y_f
            y_b = rhs[there] * p_b + (links[plane(j + 1, rows)] * p_b) * y_b
            stores += [(here, y_f), (there, y_b)]
        if keep:
            for at, y in stores:
                value[at] = y
        return y_f, y_b

    half = cells // 2
    zeros = jnp.zeros((rows, 128), jnp.float32)
    carry = blocks(0, half, size, functools.partial(body, False), (zeros, zeros))
    y_f, y_b = blocks(half, cells, size, functools.partial(body, True), carry)
    ends[0] = y_b
    ends[1] = y_f


def back_substitute(before, after, cells, rows, near, far, value, unroll, store):
    def lap(block, carry):
        low, high = carry
        lows, highs = [], []
        for u in range(unroll):
            i = block * unroll + u
            here, there = plane(i, rows), plane(cells - 1 - i, rows)
            low = (value[here] + far[here] * after) + near[here] * low
            high = (value[there] + far[there] * before) + near[there] * high
            lows.append(low)
            highs.append(high)
        store(block, lows, highs)
        return low, high

    lax.fori_loop(0, cells // 2 // unroll, lap, (before, after))


class Reduced:
    def __init__(self, axis, rows, refs):
        self.axis, self.count, self.me = axis, lax.axis_size(axis), lax.axis_index(axis)
        self.owners = min(self.count, rows // ROWS)
        self.rows = rows // self.owners
        self.stride = self.count // self.owners
        self.mine = lax.rem(self.me, self.stride) == 0
        self.group = self.me // self.stride
        (self.gains, self.ends, self.all_gains, self.all_ends, self.relation, self.reply, self.sides) = refs[:7]
        (self.gain_send, self.gain_recv, self.end_send, self.end_recv, self.reply_send, self.reply_recv) = refs[7:]

    def copy(self, src, dst, send, recv, to):
        return pltpu.make_async_remote_copy(
            src_ref=src, dst_ref=dst, send_sem=send, recv_sem=recv,
            device_id={self.axis: to}, device_id_type=MESH,
        )

    def to_owner(self, o, source, everyone, send, recv):
        return self.copy(
            source.at[:, pl.ds(o * self.rows, self.rows), :], everyone.at[self.me],
            send.at[o], recv.at[self.me], o * self.stride,
        )

    def spread(self, source, everyone, send, recv):
        for o in range(self.owners):

            @pl.when(self.me != o * self.stride)
            def _():
                self.to_owner(o, source, everyone, send, recv).start()

            @pl.when(self.me == o * self.stride)
            def _():
                everyone[o * self.stride] = source[:, o * self.rows : (o + 1) * self.rows, :]

    def send_gains(self):
        self.spread(self.gains, self.all_gains, self.gain_send, self.gain_recv)

    def send_ends(self):
        self.spread(self.ends, self.all_ends, self.end_send, self.end_recv)

    def arrived(self, everyone, recv):
        for d in range(1, self.count):
            k = lax.rem(self.me + d, self.count)
            self.copy(everyone.at[k], everyone.at[k], recv.at[k], recv.at[k], k).wait_recv()

    def factor(self):
        @pl.when(self.mine)
        def _():
            self.arrived(self.all_gains, self.gain_recv)
            gain = jnp.zeros((self.rows, 128), jnp.float32)
            for k in range(self.count):
                head_west, head_east = self.all_gains[k, 0], self.all_gains[k, 1]
                tail_west, tail_east = self.all_gains[k, 2], self.all_gains[k, 3]
                scale = inverse(1.0 - head_west * gain)
                beta, gamma = head_east * scale, tail_west * gain
                self.relation[k, 0], self.relation[k, 1] = scale, beta
                self.relation[k, 2], self.relation[k, 3] = gamma, gain
                gain = tail_east + gamma * beta

    def reply_copy(self, k):
        return self.copy(
            self.reply.at[k], self.sides.at[self.group],
            self.reply_send.at[k], self.reply_recv.at[self.group], k,
        )

    def solve(self):
        @pl.when(self.mine)
        def _():
            self.arrived(self.all_ends, self.end_recv)
            value = jnp.zeros((self.rows, 128), jnp.float32)
            alphas, values = [], []
            for k in range(self.count):
                values.append(value)
                scale, gamma = self.relation[k, 0], self.relation[k, 2]
                head_west, tail_west = self.all_gains[k, 0], self.all_gains[k, 2]
                alpha = (self.all_ends[k, 0] + head_west * value) * scale
                value = (self.all_ends[k, 1] + tail_west * value) + gamma * alpha
                alphas.append(alpha)
            after = jnp.zeros((self.rows, 128), jnp.float32)
            for k in reversed(range(self.count)):
                self.reply[k, 1] = after
                after = alphas[k] + self.relation[k, 1] * after
                self.reply[k, 0] = values[k] + self.relation[k, 3] * after
            for d in range(1, self.count):
                self.reply_copy(lax.rem(self.me + d, self.count)).start()
            self.sides[self.group] = self.reply[self.me]

    def result(self):
        for o in range(self.owners):

            @pl.when(self.me != o * self.stride)
            def _():
                self.copy(
                    self.sides.at[o], self.sides.at[o], self.reply_recv.at[o], self.reply_recv.at[o],
                    o * self.stride,
                ).wait_recv()

        whole = (self.owners * self.rows, 128)
        return self.sides[:, 0].reshape(whole), self.sides[:, 1].reshape(whole)

    def drain(self):
        for o in range(self.owners):

            @pl.when(self.me != o * self.stride)
            def _():
                self.to_owner(o, self.gains, self.all_gains, self.gain_send, self.gain_recv).wait_send()
                self.to_owner(o, self.ends, self.all_ends, self.end_send, self.end_recv).wait_send()

        @pl.when(self.mine)
        def _():
            for d in range(1, self.count):
                self.reply_copy(lax.rem(self.me + d, self.count)).wait_send()


def reduced_scratch(count, rows):
    owners = min(count, rows // ROWS)
    part = rows // owners
    dma = pltpu.SemaphoreType.DMA
    return [
        pltpu.VMEM((4, rows, 128), jnp.float32),
        pltpu.VMEM((2, rows, 128), jnp.float32),
        pltpu.VMEM((count, 4, part, 128), jnp.float32),
        pltpu.VMEM((count, 2, part, 128), jnp.float32),
        pltpu.VMEM((count, 4, part, 128), jnp.float32),
        pltpu.VMEM((count, 2, part, 128), jnp.float32),
        pltpu.VMEM((owners, 2, part, 128), jnp.float32),
        dma((owners,)), dma((count,)), dma((owners,)), dma((count,)), dma((count,)), dma((owners,)),
    ]


def kernel(X, Y, h_in, c_in, q_in, out, *scratch):
    Z = 128
    chunks = X * Y // 128
    (stage_x, stage_y, halo_x, halo_y, halo_send, halo_recv, force, link_x, link_y, link_z) = scratch[:10]
    fwd_x, bwd_x, near_x, far_x, value_x, fwd_y, bwd_y, near_y, far_y, value_y = scratch[10:20]
    first, up_z, piv_z, lag_z, lead_z, val_z, low_z, h, c, q, load_sem = scratch[20:31]
    along_x = Reduced("gx", Y, scratch[31:44])
    along_y = Reduced("gy", X, scratch[44:57])
    nx, ny, me_x, me_y = along_x.count, along_y.count, along_x.me, along_y.me

    part = X * Y // PARTS
    loads = [
        pltpu.make_async_copy(src.at[pl.ds(m * part, part)], dst.at[pl.ds(m * part, part)], load_sem.at[k, m])
        for k, (src, dst) in enumerate(((h_in, h), (c_in, c), (q_in, q)))
        for m in range(PARTS)
    ]
    for load in loads:
        load.start()
    barrier = pltpu.get_barrier_semaphore()
    for d in range(1, nx):
        pl.semaphore_signal(barrier, inc=1, device_id={"gx": lax.rem(me_x + d, nx)}, device_id_type=MESH)
    for d in range(1, ny):
        pl.semaphore_signal(barrier, inc=1, device_id={"gy": lax.rem(me_y + d, ny)}, device_id_type=MESH)

    for load in loads[: 2 * PARTS]:
        load.wait()

    def column(j):
        return pl.ds(j, X, stride=Y)

    for side, (i, j) in enumerate(((0, 0), (X - 1, Y - 1))):
        stage_x[side, 0], stage_x[side, 1] = h[plane(i, Y)], c[plane(i, Y)]
        stage_y[side, 0], stage_y[side, 1] = h[column(j), :], c[column(j), :]

    for load in loads[2 * PARTS :]:
        load.wait()

    def along_first(i, carry):
        head, cond, flux = carry
        stores = []
        for u in range(4):
            here, ahead = plane(i + u, Y), plane(jnp.minimum(i + u + 1, X - 1), Y)
            head_next, cond_next = h[ahead], c[ahead]
            east = link(COEF_X, cond, cond_next)
            flux_next = east * (head_next - head)
            stores += [(link_x, plane(i + u + 1, Y), east), (force, here, 2.0 * (flux_next - flux) + q[here])]
            head, cond, flux = head_next, cond_next, flux_next
        for ref, at, value in stores:
            ref[at] = value
        return head, cond, flux

    blocks(0, X, 4, along_first, (h[plane(0, Y)], c[plane(0, Y)], jnp.zeros((Y, 128), jnp.float32)))

    pl.semaphore_wait(barrier, nx - 1 + ny - 1)

    halos = []
    for a, (axis, me, count, stage, halo) in enumerate(
        (("gx", me_x, nx, stage_x, halo_x), ("gy", me_y, ny, stage_y, halo_y))
    ):
        for side in (0, 1):
            to = me - 1 if side == 0 else me + 1
            inside = me > 0 if side == 0 else me < count - 1
            send = pltpu.make_async_remote_copy(
                src_ref=stage.at[side], dst_ref=halo.at[1 - side],
                send_sem=halo_send.at[2 * a + side], recv_sem=halo_recv.at[2 * a + 1 - side],
                device_id={axis: to}, device_id_type=MESH,
            )
            take = pltpu.make_async_remote_copy(
                src_ref=stage.at[side], dst_ref=halo.at[side],
                send_sem=halo_send.at[2 * a + side], recv_sem=halo_recv.at[2 * a + side],
                device_id={axis: to}, device_id_type=MESH,
            )
            halos.append((inside, send, take))

            @pl.when(inside)
            def _():
                send.start()

            @pl.when(jnp.logical_not(inside))
            def _():
                halo[side] = jnp.zeros((2,) + halo.shape[2:], jnp.float32)

    inner = lax.broadcasted_iota(jnp.int32, (X, 128), 1) < Z - 1

    def depth_and_second(j, carry):
        head, cond, flux = carry
        stores = []
        for u in range(4):
            ahead = jnp.minimum(j + u + 1, Y - 1)
            head_next, cond_next = h[column(ahead), :], c[column(ahead), :]
            old = force[column(j + u), :]
            up = jnp.where(inner, link(COEF_Z, cond, pltpu.roll(cond, Z - 1, 1)), 0.0)
            rise = up * (pltpu.roll(head, Z - 1, 1) - head)
            north = link(COEF_Y, cond, cond_next)
            flux_next = north * (head_next - head)
            total = old + 2.0 * ((rise - pltpu.roll(rise, 1, 1)) + (flux_next - flux))
            stores.append((link_z, plane(j + u, X), up))
            stores.append((link_y, plane(j + u + 1, X), north))
            stores.append((force, column(j + u), total))
            head, cond, flux = head_next, cond_next, flux_next
        for ref, at, value in stores:
            ref[at, :] = value
        return head, cond, flux

    blocks(0, Y, 4, depth_and_second, (h[column(0), :], c[column(0), :], jnp.zeros((X, 128), jnp.float32)))

    for inside, _, take in halos:

        @pl.when(inside)
        def _():
            take.wait_recv()

    low = link(COEF_X, halo_x[0, 1], c[plane(0, Y)])
    high = link(COEF_X, halo_x[1, 1], c[plane(X - 1, Y)])
    link_x[plane(0, Y)], link_x[plane(X, Y)] = low, high
    force[plane(0, Y)] += 2.0 * (low * (halo_x[0, 0] - h[plane(0, Y)]))
    force[plane(X - 1, Y)] += 2.0 * (high * (halo_x[1, 0] - h[plane(X - 1, Y)]))
    low = link(COEF_Y, halo_y[0, 1], c[column(0), :])
    high = link(COEF_Y, halo_y[1, 1], c[column(Y - 1), :])
    link_y[plane(0, X)], link_y[plane(Y, X)] = low, high
    force[column(0), :] += 2.0 * (low * (halo_y[0, 0] - h[column(0), :]))
    force[column(Y - 1), :] += 2.0 * (high * (halo_y[1, 0] - h[column(Y - 1), :]))

    segment_x = (link_x, X, Y, fwd_x, bwd_x, near_x, far_x, along_x.gains)
    factor_segment(*segment_x, factor_segment(*segment_x))
    along_x.send_gains()
    sweep_values(force, link_x, X, Y, fwd_x, bwd_x, value_x, along_x.ends)
    along_x.send_ends()

    segment_y = (link_y, Y, X, fwd_y, bwd_y, near_y, far_y, along_y.gains)
    along_x.factor()
    halfway = factor_segment(*segment_y)
    along_x.solve()
    factor_segment(*segment_y, halfway)
    along_y.send_gains()

    before, after = along_x.result()

    def store_first(block, lows, highs):
        for u in range(4):
            i = block * 4 + u
            first[pl.ds(i, Y, stride=X), :] = lows[u]
            first[pl.ds(X - 1 - i, Y, stride=X), :] = highs[u]

    back_substitute(before, after, X, Y, near_x, far_x, value_x, 4, store_first)

    sweep_values(first, link_y, Y, X, fwd_y, bwd_y, value_y, along_y.ends)
    along_y.send_ends()
    along_y.factor()

    def turn_links(k, carry):
        for u in range(2):
            up_z[pl.ds(chunks + k + u, Z, stride=chunks), :] = link_z[plane(k + u, 128)].T
        return carry

    ones, zeros = (jnp.full((chunks, 128), v, jnp.float32) for v in (1.0, 0.0))
    up_z[plane(0, chunks)] = zeros
    blocks(0, chunks, 2, turn_links, 0)
    half = Z // 2

    def factor_z(i, carry):
        states, stores = [], []
        for s, (first_cell, way) in zip(carry, ((i, 1), (Z - 1 - i, -1))):
            edge = first_cell + (way < 0)
            beside = [up_z[plane(edge + way * u, chunks)] for u in range(9)]
            parts, s = pivots(beside, s)
            for u, p in enumerate(parts):
                at = plane(first_cell + way * u, chunks)
                stores += [(piv_z, at, p), (lag_z, at, beside[u] * p), (lead_z, at, beside[u + 1] * p)]
            states.append(s)
        for ref, at, value in stores:
            ref[at] = value
        return tuple(states)

    carry = blocks(0, half // 2, 8, factor_z, (ones, ones))
    along_y.solve()
    s_f, s_b = blocks(half // 2, half, 8, factor_z, carry)
    middle = inverse(s_f + s_b * lead_z[plane(half - 1, chunks)])
    before, after = along_y.result()
    per_chunk = 128 // X

    def store_second(block, lows, highs):
        val_z[pl.ds(block, Z, stride=chunks), :] = jnp.concatenate(lows, 0).T
        val_z[pl.ds(chunks - 1 - block, Z, stride=chunks), :] = jnp.concatenate(highs[::-1], 0).T

    back_substitute(before, after, Y, X, near_y, far_y, value_y, per_chunk, store_second)

    def sweep_z(i, carry):
        y_f, y_b = carry
        stores = []
        for u in range(8):
            here, there = plane(i + u, chunks), plane(Z - 1 - i - u, chunks)
            y_f = val_z[here] * piv_z[here] + lag_z[here] * y_f
            y_b = val_z[there] * piv_z[there] + lag_z[there] * y_b
            stores += [(here, y_f), (there, y_b)]
        for at, y in stores:
            low_z[at] = y
        return y_f, y_b

    y_f, y_b = blocks(0, half, 8, sweep_z, (zeros, zeros))
    below = (y_f + lead_z[plane(half - 1, chunks)] * y_b) * middle
    above = y_b + lead_z[plane(half, chunks)] * below

    def back_z(i, carry):
        low, high = carry
        stores = []
        for u in range(8):
            stores += [(plane(half - 1 - i - u, chunks), low), (plane(half + i + u, chunks), high)]
            nearer = plane(jnp.maximum(half - 2 - i - u, 0), chunks)
            farther = plane(jnp.minimum(half + 1 + i + u, Z - 1), chunks)
            low = low_z[nearer] + lead_z[nearer] * low
            high = low_z[farther] + lead_z[farther] * high
        for at, value in stores:
            out[at] = value
        return low, high

    blocks(0, half, 8, back_z, (below, above))

    for inside, send, _ in halos:

        @pl.when(inside)
        def _():
            send.wait_send()

    along_x.drain()
    along_y.drain()

def finish(X, Y, delta, h, out):
    chunks, per_chunk = X * Y // 128, 128 // X

    def write(k, carry):
        stores = []
        for u in range(2):
            lines = delta[pl.ds(k + u, 128, stride=chunks), :].T
            for part in range(per_chunk):
                at = pl.ds((k + u) * per_chunk + part, X, stride=Y)
                stores.append((at, h[at, :] + lines[part * X : (part + 1) * X]))
        for at, value in stores:
            out[at, :] = value
        return carry

    blocks(0, chunks, 2, write, 0)


def per_device(water_head, conductivity, recharge):
    X, Y, Z = water_head.shape
    nx, ny = lax.axis_size("gx"), lax.axis_size("gy")

    def vmem(*shape):
        return pltpu.VMEM(shape, jnp.float32)

    cells = X * Y
    chunks = cells // 128
    scratch = [
        vmem(2, 2, Y, Z), vmem(2, 2, X, Z), vmem(2, 2, Y, Z), vmem(2, 2, X, Z),
        pltpu.SemaphoreType.DMA((4,)), pltpu.SemaphoreType.DMA((4,)),
        vmem(cells, Z), vmem(cells + Y, Z), vmem(cells + X, Z), vmem(cells, Z),
    ]
    scratch += [vmem(cells, Z) for _ in range(11)] + [vmem(cells + chunks, Z)] + [vmem(cells, Z) for _ in range(8)] + [pltpu.SemaphoreType.DMA((3, PARTS))]
    scratch += reduced_scratch(nx, Y) + reduced_scratch(ny, X)
    flat = [array.reshape(cells, Z) for array in (water_head, conductivity, recharge)]
    delta = pl.pallas_call(
        functools.partial(kernel, X, Y),
        out_shape=jax.ShapeDtypeStruct((cells, Z), jnp.float32),
        in_specs=[pl.BlockSpec(memory_space=pl.ANY)] * 3,
        out_specs=pl.BlockSpec(memory_space=pltpu.VMEM),
        scratch_shapes=scratch,
        compiler_params=pltpu.CompilerParams(
            collective_id=0, has_side_effects=True, vmem_limit_bytes=56 * 2**20
        ),
    )(*flat)
    result = pl.pallas_call(
        functools.partial(finish, X, Y),
        out_shape=jax.ShapeDtypeStruct((cells, Z), jnp.float32),
        in_specs=[pl.BlockSpec(memory_space=pltpu.VMEM)] * 2,
        out_specs=pl.BlockSpec(memory_space=pltpu.VMEM),
        compiler_params=pltpu.CompilerParams(vmem_limit_bytes=16 * 2**20),
    )(delta, flat[0])
    return result.reshape(X, Y, Z)


def solution(mesh):
    placed = (P("gx", "gy", None), P("gx", "gy", None), P("gx", "gy", None))
    return jax.shard_map(
        per_device, mesh=mesh, in_specs=placed, out_specs=P("gx", "gy", None), check_vma=False
    )
```

```python
import functools

import jax
import jax.numpy as jnp
from jax import lax
from jax.experimental import pallas as pl
from jax.experimental.pallas import tpu as pltpu
from jax.sharding import PartitionSpec as P

COEF_Z = 8
COEF_X = 5120
COEF_Y = 5120
ROWS = 8
PARTS = 4
MESH = pl.DeviceIdType.MESH


def inverse(x):
    return pl.reciprocal(x, approx=True, full_range=False)


def link(coef, one_side, other_side):
    return (coef * one_side * other_side) * inverse(one_side + other_side)


def blocks(start, stop, size, body, carry):
    return lax.fori_loop(start // size, stop // size, lambda block, carry: body(block * size, carry), carry)


def plane(i, size):
    start = i * size
    return pl.ds(start if isinstance(i, int) else pl.multiple_of(start, size), size)


def pivots(links, share):
    result = []
    for behind, ahead in zip(links[:-1], links[1:]):
        if not result:
            top = 1.0 + behind * share
            bottom = top + ahead
            scale = inverse(bottom)
            result.append(scale)
        else:
            top = bottom + behind * top
            below, bottom = bottom, top + ahead * bottom
            scale = inverse(bottom)
            result.append(below * scale)
    return result, top * scale


def factor_segment(links, cells, rows, fwd_p, bwd_p, near, far, gains, carry=None):
    size = 4

    def body(keep, i, carry):
        states, stores = [], []
        for (s, g), (p_ref, first, way) in zip(carry, ((fwd_p, i, 1), (bwd_p, cells - 1 - i, -1))):
            edge = first + (way < 0)
            beside = [links[plane(edge + way * u, rows)] for u in range(size + 1)]
            parts, s = pivots(beside, s)
            for u, p in enumerate(parts):
                at = plane(first + way * u, rows)
                g = g * (beside[u] * p)
                stores.append((p_ref, at, p))
                if keep:
                    stores += [(near, at, beside[u + 1] * p), (far, at, g)]
            states.append((s, g))
        for ref, at, value in stores:
            ref[at] = value
        return tuple(states)

    half = cells // 2
    if carry is None:
        ones = jnp.ones((rows, 128), jnp.float32)
        return blocks(0, half, size, functools.partial(body, False), ((ones, ones), (ones, ones)))
    (_, g_f), (_, g_b) = blocks(half, cells, size, functools.partial(body, True), carry)
    for k, value in enumerate((near[plane(0, rows)], g_b, g_f, near[plane(cells - 1, rows)])):
        gains.put(k, value)


def sweep_values(rhs, links, cells, rows, fwd_p, bwd_p, value, ends, at=0):
    size = 4

    def body(keep, i, carry):
        y_f, y_b = carry
        stores = []
        for u in range(size):
            j = cells - 1 - i - u
            here, there = plane(i + u, rows), plane(j, rows)
            p_f, p_b = fwd_p[here], bwd_p[there]
            y_f = rhs[here] * p_f + (links[here] * p_f) * y_f
            y_b = rhs[there] * p_b + (links[plane(j + 1, rows)] * p_b) * y_b
            stores += [(here, y_f), (there, y_b)]
        if keep:
            for at, y in stores:
                value[at] = y
        return y_f, y_b

    half = cells // 2
    zeros = jnp.zeros((rows, 128), jnp.float32)
    carry = blocks(0, half, size, functools.partial(body, False), (zeros, zeros))
    y_f, y_b = blocks(half, cells, size, functools.partial(body, True), carry)
    ends.put(at, y_b)
    ends.put(at + 1, y_f)


def back_substitute(before, after, cells, rows, near, far, value, unroll, store):
    def lap(block, carry):
        low, high = carry
        lows, highs = [], []
        for u in range(unroll):
            i = block * unroll + u
            here, there = plane(i, rows), plane(cells - 1 - i, rows)
            low = (value[here] + far[here] * after) + near[here] * low
            high = (value[there] + far[there] * before) + near[there] * high
            lows.append(low)
            highs.append(high)
        store(block, lows, highs)
        return low, high

    lax.fori_loop(0, cells // 2 // unroll, lap, (before, after))


def remote(src, dst, send, recv, axis, to):
    return pltpu.make_async_remote_copy(
        src_ref=src, dst_ref=dst, send_sem=send, recv_sem=recv, device_id={axis: to}, device_id_type=MESH
    )


class Parcel:
    def __init__(self, system, refs):
        self.system = system
        self.stage, self.everyone, self.send_sem, self.recv_sem = refs

    def put(self, k, value):
        rows = self.system.rows
        for o in range(self.system.owners):
            self.stage[o, k] = value[o * rows : (o + 1) * rows]

    def copy(self, o):
        own = self.system
        return remote(
            self.stage.at[o], self.everyone.at[own.me], self.send_sem.at[o], self.recv_sem.at[own.me],
            own.axis, o * own.stride,
        )

    def send(self):
        own = self.system
        for o in range(own.owners):

            @pl.when(own.me != o * own.stride)
            def _():
                self.copy(o).start()

        @pl.when(own.mine)
        def _():
            self.everyone[own.me] = self.stage[own.group]

    def arrived(self):
        own = self.system
        for d in range(1, own.count):
            k = lax.rem(own.me + d, own.count)
            part = self.everyone.at[k]
            remote(part, part, self.recv_sem.at[k], self.recv_sem.at[k], own.axis, k).wait_recv()

    def drain(self):
        for o in range(self.system.owners):

            @pl.when(self.system.me != o * self.system.stride)
            def _():
                self.copy(o).wait_send()


class Reduced:
    def __init__(self, axis, rows, merged, refs):
        self.axis, self.count, self.me = axis, lax.axis_size(axis), lax.axis_index(axis)
        self.owners, self.rows = groups(self.count, rows)
        self.stride = self.count // self.owners
        self.mine = lax.rem(self.me, self.stride) == 0
        self.group = self.me // self.stride
        self.merged = merged
        self.gains = Parcel(self, refs[:4])
        self.ends = self.gains if merged else Parcel(self, refs[4:8])
        refs = refs[4 if merged else 8 :]
        (self.relation, self.reply, self.replies, self.sides) = refs[:4]
        (self.reply_send, self.reply_recv, self.forward_send, self.forward_recv) = refs[4:]
        self.shift = 4 if merged else 0

    def factor(self):
        @pl.when(self.mine)
        def _():
            self.gains.arrived()
            gain = jnp.zeros((self.rows, 128), jnp.float32)
            for k in range(self.count):
                head_west, head_east, tail_west, tail_east = (self.gains.everyone[k, v] for v in range(4))
                scale = inverse(1.0 - head_west * gain)
                beta, gamma = head_east * scale, tail_west * gain
                self.relation[k, 0], self.relation[k, 1] = scale, beta
                self.relation[k, 2], self.relation[k, 3] = gamma, gain
                gain = tail_east + gamma * beta

    def reply_copy(self, o):
        return remote(
            self.reply.at[pl.ds(o * self.stride, self.stride)], self.replies.at[self.group],
            self.reply_send.at[o], self.reply_recv.at[self.group], self.axis, o * self.stride,
        )

    def forward_copy(self, member):
        return remote(
            self.replies.at[:, member], self.sides, self.forward_send.at[member], self.forward_recv,
            self.axis, self.group * self.stride + member,
        )

    def solve(self):
        @pl.when(self.mine)
        def _():
            if not self.merged:
                self.ends.arrived()
            value = jnp.zeros((self.rows, 128), jnp.float32)
            alphas, values = [], []
            for k in range(self.count):
                values.append(value)
                scale, gamma = self.relation[k, 0], self.relation[k, 2]
                head_west, tail_west = self.gains.everyone[k, 0], self.gains.everyone[k, 2]
                alpha = (self.ends.everyone[k, self.shift] + head_west * value) * scale
                value = (self.ends.everyone[k, self.shift + 1] + tail_west * value) + gamma * alpha
                alphas.append(alpha)
            after = jnp.zeros((self.rows, 128), jnp.float32)
            for k in reversed(range(self.count)):
                self.reply[k, 1] = after
                after = alphas[k] + self.relation[k, 1] * after
                self.reply[k, 0] = values[k] + self.relation[k, 3] * after
            for d in range(1, self.owners):
                self.reply_copy(lax.rem(self.group + d, self.owners)).start()
            self.replies[self.group] = self.reply[pl.ds(self.me, self.stride)]

    def result(self):
        @pl.when(self.mine)
        def _():
            for d in range(1, self.owners):
                o = lax.rem(self.group + d, self.owners)
                part = self.replies.at[o]
                remote(
                    part, part, self.reply_recv.at[o], self.reply_recv.at[o], self.axis, o * self.stride
                ).wait_recv()
            for member in range(1, self.stride):
                self.forward_copy(member).start()
            self.sides[...] = self.replies[:, 0]

        if self.stride > 1:

            @pl.when(jnp.logical_not(self.mine))
            def _():
                remote(
                    self.sides, self.sides, self.forward_recv, self.forward_recv,
                    self.axis, self.group * self.stride,
                ).wait_recv()

        whole = (self.owners * self.rows, 128)
        return self.sides[:, 0].reshape(whole), self.sides[:, 1].reshape(whole)

    def drain(self):
        @pl.when(self.mine)
        def _():
            for d in range(1, self.owners):
                self.reply_copy(lax.rem(self.group + d, self.owners)).wait_send()
            for member in range(1, self.stride):
                self.forward_copy(member).wait_send()


def groups(count, rows):
    owners = min(count, rows // ROWS)
    return owners, rows // owners


def reduced_scratch(count, rows, merged):
    owners, part = groups(count, rows)
    dma = pltpu.SemaphoreType.DMA

    def vmem(*shape):
        return pltpu.VMEM(shape + (part, 128), jnp.float32)

    scratch = []
    for values in (6,) if merged else (4, 2):
        scratch += [vmem(owners, values), vmem(count, values), dma((owners,)), dma((count,))]
    return scratch + [
        vmem(count, 4), vmem(count, 2), vmem(owners, count // owners, 2), vmem(owners, 2),
        dma((owners,)), dma((owners,)), dma((count // owners,)), dma,
    ]


def kernel(X, Y, h_in, c_in, q_in, out, *scratch):
    Z = 128
    chunks = X * Y // 128
    (stage_x, stage_y, halo_x, halo_y, halo_send, halo_recv, force, link_x, link_y, link_z) = scratch[:10]
    fwd_x, bwd_x, near_x, far_x, value_x, fwd_y, bwd_y, near_y, far_y, value_y = scratch[10:20]
    first, up_z, piv_z, lag_z, lead_z, val_z, low_z, h, c, q, load_sem = scratch[20:31]
    along_x = Reduced("gx", Y, True, scratch[31:43])
    along_y = Reduced("gy", X, False, scratch[43:59])
    nx, ny, me_x, me_y = along_x.count, along_y.count, along_x.me, along_y.me

    part = X * Y // PARTS
    loads = [
        pltpu.make_async_copy(src.at[pl.ds(m * part, part)], dst.at[pl.ds(m * part, part)], load_sem.at[k, m])
        for k, (src, dst) in enumerate(((h_in, h), (c_in, c), (q_in, q)))
        for m in range(PARTS)
    ]
    for load in loads:
        load.start()
    barrier = pltpu.get_barrier_semaphore()
    for d in range(1, nx):
        pl.semaphore_signal(barrier, inc=1, device_id={"gx": lax.rem(me_x + d, nx)}, device_id_type=MESH)
    for d in range(1, ny):
        pl.semaphore_signal(barrier, inc=1, device_id={"gy": lax.rem(me_y + d, ny)}, device_id_type=MESH)

    for load in loads[: 2 * PARTS]:
        load.wait()

    def column(j):
        return pl.ds(j, X, stride=Y)

    for side, (i, j) in enumerate(((0, 0), (X - 1, Y - 1))):
        stage_x[side, 0], stage_x[side, 1] = h[plane(i, Y)], c[plane(i, Y)]
        stage_y[side, 0], stage_y[side, 1] = h[column(j), :], c[column(j), :]

    for load in loads[2 * PARTS :]:
        load.wait()

    def along_first(i, carry):
        head, cond, flux = carry
        stores = []
        for u in range(4):
            here, ahead = plane(i + u, Y), plane(jnp.minimum(i + u + 1, X - 1), Y)
            head_next, cond_next = h[ahead], c[ahead]
            east = link(COEF_X, cond, cond_next)
            flux_next = east * (head_next - head)
            stores += [(link_x, plane(i + u + 1, Y), east), (force, here, 2.0 * (flux_next - flux) + q[here])]
            head, cond, flux = head_next, cond_next, flux_next
        for ref, at, value in stores:
            ref[at] = value
        return head, cond, flux

    blocks(0, X, 4, along_first, (h[plane(0, Y)], c[plane(0, Y)], jnp.zeros((Y, 128), jnp.float32)))

    pl.semaphore_wait(barrier, nx - 1 + ny - 1)

    halos = []
    for a, (axis, me, count, stage, halo) in enumerate(
        (("gx", me_x, nx, stage_x, halo_x), ("gy", me_y, ny, stage_y, halo_y))
    ):
        for side in (0, 1):
            to = me - 1 if side == 0 else me + 1
            inside = me > 0 if side == 0 else me < count - 1
            send = pltpu.make_async_remote_copy(
                src_ref=stage.at[side], dst_ref=halo.at[1 - side],
                send_sem=halo_send.at[2 * a + side], recv_sem=halo_recv.at[2 * a + 1 - side],
                device_id={axis: to}, device_id_type=MESH,
            )
            take = pltpu.make_async_remote_copy(
                src_ref=stage.at[side], dst_ref=halo.at[side],
                send_sem=halo_send.at[2 * a + side], recv_sem=halo_recv.at[2 * a + side],
                device_id={axis: to}, device_id_type=MESH,
            )
            halos.append((inside, send, take))

            @pl.when(inside)
            def _():
                send.start()

            @pl.when(jnp.logical_not(inside))
            def _():
                halo[side] = jnp.zeros((2,) + halo.shape[2:], jnp.float32)

    inner = lax.broadcasted_iota(jnp.int32, (X, 128), 1) < Z - 1

    def depth_and_second(j, carry):
        head, cond, flux = carry
        stores = []
        for u in range(4):
            ahead = jnp.minimum(j + u + 1, Y - 1)
            head_next, cond_next = h[column(ahead), :], c[column(ahead), :]
            old = force[column(j + u), :]
            up = jnp.where(inner, link(COEF_Z, cond, pltpu.roll(cond, Z - 1, 1)), 0.0)
            rise = up * (pltpu.roll(head, Z - 1, 1) - head)
            north = link(COEF_Y, cond, cond_next)
            flux_next = north * (head_next - head)
            total = old + 2.0 * ((rise - pltpu.roll(rise, 1, 1)) + (flux_next - flux))
            stores.append((link_z, plane(j + u, X), up))
            stores.append((link_y, plane(j + u + 1, X), north))
            stores.append((force, column(j + u), total))
            head, cond, flux = head_next, cond_next, flux_next
        for ref, at, value in stores:
            ref[at, :] = value
        return head, cond, flux

    blocks(0, Y, 4, depth_and_second, (h[column(0), :], c[column(0), :], jnp.zeros((X, 128), jnp.float32)))

    for inside, _, take in halos:

        @pl.when(inside)
        def _():
            take.wait_recv()

    low = link(COEF_X, halo_x[0, 1], c[plane(0, Y)])
    high = link(COEF_X, halo_x[1, 1], c[plane(X - 1, Y)])
    link_x[plane(0, Y)], link_x[plane(X, Y)] = low, high
    force[plane(0, Y)] += 2.0 * (low * (halo_x[0, 0] - h[plane(0, Y)]))
    force[plane(X - 1, Y)] += 2.0 * (high * (halo_x[1, 0] - h[plane(X - 1, Y)]))
    low = link(COEF_Y, halo_y[0, 1], c[column(0), :])
    high = link(COEF_Y, halo_y[1, 1], c[column(Y - 1), :])
    link_y[plane(0, X)], link_y[plane(Y, X)] = low, high
    force[column(0), :] += 2.0 * (low * (halo_y[0, 0] - h[column(0), :]))
    force[column(Y - 1), :] += 2.0 * (high * (halo_y[1, 0] - h[column(Y - 1), :]))

    segment_x = (link_x, X, Y, fwd_x, bwd_x, near_x, far_x, along_x.gains)
    factor_segment(*segment_x, factor_segment(*segment_x))
    sweep_values(force, link_x, X, Y, fwd_x, bwd_x, value_x, along_x.gains, 4)
    along_x.gains.send()

    segment_y = (link_y, Y, X, fwd_y, bwd_y, near_y, far_y, along_y.gains)
    factor_segment(*segment_y, factor_segment(*segment_y))
    along_y.gains.send()

    along_x.factor()
    along_x.solve()

    def turn_links(k, carry):
        for u in range(2):
            up_z[pl.ds(chunks + k + u, Z, stride=chunks), :] = link_z[plane(k + u, 128)].T
        return carry

    ones, zeros = (jnp.full((chunks, 128), v, jnp.float32) for v in (1.0, 0.0))
    up_z[plane(0, chunks)] = zeros
    blocks(0, chunks, 2, turn_links, 0)

    before, after = along_x.result()

    def store_first(block, lows, highs):
        for u in range(4):
            i = block * 4 + u
            first[pl.ds(i, Y, stride=X), :] = lows[u]
            first[pl.ds(X - 1 - i, Y, stride=X), :] = highs[u]

    back_substitute(before, after, X, Y, near_x, far_x, value_x, 4, store_first)

    sweep_values(first, link_y, Y, X, fwd_y, bwd_y, value_y, along_y.ends)
    along_y.ends.send()
    along_y.factor()
    along_x.gains.drain()
    along_y.gains.drain()
    along_x.drain()

    half = Z // 2

    def factor_z(i, carry):
        states, stores = [], []
        for s, (first_cell, way) in zip(carry, ((i, 1), (Z - 1 - i, -1))):
            edge = first_cell + (way < 0)
            beside = [up_z[plane(edge + way * u, chunks)] for u in range(9)]
            parts, s = pivots(beside, s)
            for u, p in enumerate(parts):
                at = plane(first_cell + way * u, chunks)
                stores += [(piv_z, at, p), (lag_z, at, beside[u] * p), (lead_z, at, beside[u + 1] * p)]
            states.append(s)
        for ref, at, value in stores:
            ref[at] = value
        return tuple(states)

    carry = blocks(0, half // 2, 8, factor_z, (ones, ones))
    along_y.solve()
    s_f, s_b = blocks(half // 2, half, 8, factor_z, carry)
    along_y.ends.drain()
    for inside, send, _ in halos:

        @pl.when(inside)
        def _():
            send.wait_send()
    middle = inverse(s_f + s_b * lead_z[plane(half - 1, chunks)])
    before, after = along_y.result()
    per_chunk = 128 // X

    def store_second(block, lows, highs):
        val_z[pl.ds(block, Z, stride=chunks), :] = jnp.concatenate(lows, 0).T
        val_z[pl.ds(chunks - 1 - block, Z, stride=chunks), :] = jnp.concatenate(highs[::-1], 0).T

    back_substitute(before, after, Y, X, near_y, far_y, value_y, per_chunk, store_second)

    def sweep_z(i, carry):
        y_f, y_b = carry
        stores = []
        for u in range(8):
            here, there = plane(i + u, chunks), plane(Z - 1 - i - u, chunks)
            y_f = val_z[here] * piv_z[here] + lag_z[here] * y_f
            y_b = val_z[there] * piv_z[there] + lag_z[there] * y_b
            stores += [(here, y_f), (there, y_b)]
        for at, y in stores:
            low_z[at] = y
        return y_f, y_b

    y_f, y_b = blocks(0, half, 8, sweep_z, (zeros, zeros))
    below = (y_f + lead_z[plane(half - 1, chunks)] * y_b) * middle
    above = y_b + lead_z[plane(half, chunks)] * below

    def back_z(i, carry):
        low, high = carry
        stores = []
        for u in range(8):
            stores += [(plane(half - 1 - i - u, chunks), low), (plane(half + i + u, chunks), high)]
            nearer = plane(jnp.maximum(half - 2 - i - u, 0), chunks)
            farther = plane(jnp.minimum(half + 1 + i + u, Z - 1), chunks)
            low = low_z[nearer] + lead_z[nearer] * low
            high = low_z[farther] + lead_z[farther] * high
        for at, value in stores:
            out[at] = value
        return low, high

    blocks(0, half, 8, back_z, (below, above))

    along_y.drain()


def finish(X, Y, delta, h, out):
    chunks, per_chunk = X * Y // 128, 128 // X

    def write(k, carry):
        stores = []
        for u in range(2):
            lines = delta[pl.ds(k + u, 128, stride=chunks), :].T
            for part in range(per_chunk):
                at = pl.ds((k + u) * per_chunk + part, X, stride=Y)
                stores.append((at, h[at, :] + lines[part * X : (part + 1) * X]))
        for at, value in stores:
            out[at, :] = value
        return carry

    blocks(0, chunks, 2, write, 0)


def per_device(water_head, conductivity, recharge):
    X, Y, Z = water_head.shape
    nx, ny = lax.axis_size("gx"), lax.axis_size("gy")

    def vmem(*shape):
        return pltpu.VMEM(shape, jnp.float32)

    cells = X * Y
    chunks = cells // 128
    scratch = [
        vmem(2, 2, Y, Z), vmem(2, 2, X, Z), vmem(2, 2, Y, Z), vmem(2, 2, X, Z),
        pltpu.SemaphoreType.DMA((4,)), pltpu.SemaphoreType.DMA((4,)),
        vmem(cells, Z), vmem(cells + Y, Z), vmem(cells + X, Z), vmem(cells, Z),
    ]
    scratch += [vmem(cells, Z) for _ in range(11)] + [vmem(cells + chunks, Z)] + [vmem(cells, Z) for _ in range(8)] + [pltpu.SemaphoreType.DMA((3, PARTS))]
    scratch += reduced_scratch(nx, Y, True) + reduced_scratch(ny, X, False)
    flat = [array.reshape(cells, Z) for array in (water_head, conductivity, recharge)]
    delta = pl.pallas_call(
        functools.partial(kernel, X, Y),
        out_shape=jax.ShapeDtypeStruct((cells, Z), jnp.float32),
        in_specs=[pl.BlockSpec(memory_space=pl.ANY)] * 3,
        out_specs=pl.BlockSpec(memory_space=pltpu.VMEM),
        scratch_shapes=scratch,
        compiler_params=pltpu.CompilerParams(
            collective_id=0, has_side_effects=True, vmem_limit_bytes=56 * 2**20
        ),
    )(*flat)
    result = pl.pallas_call(
        functools.partial(finish, X, Y),
        out_shape=jax.ShapeDtypeStruct((cells, Z), jnp.float32),
        in_specs=[pl.BlockSpec(memory_space=pltpu.VMEM)] * 2,
        out_specs=pl.BlockSpec(memory_space=pltpu.VMEM),
        compiler_params=pltpu.CompilerParams(vmem_limit_bytes=16 * 2**20),
    )(delta, flat[0])
    return result.reshape(X, Y, Z)


def solution(mesh):
    placed = (P("gx", "gy", None), P("gx", "gy", None), P("gx", "gy", None))
    return jax.shard_map(
        per_device, mesh=mesh, in_specs=placed, out_specs=P("gx", "gy", None), check_vma=False
    )
```

```python
import functools

import jax
import jax.numpy as jnp
from jax import lax
from jax.experimental import pallas as pl
from jax.experimental.pallas import tpu as pltpu
from jax.sharding import PartitionSpec as P

COEF_Z = 8
COEF_X = 5120
COEF_Y = 5120
ROWS = 8
PARTS = 4
MESH = pl.DeviceIdType.MESH


def inverse(x):
    return pl.reciprocal(x, approx=True, full_range=False)


def link(coef, one_side, other_side):
    return (coef * one_side * other_side) * inverse(one_side + other_side)


def blocks(start, stop, size, body, carry):
    return lax.fori_loop(start // size, stop // size, lambda block, carry: body(block * size, carry), carry)


def plane(i, size):
    start = i * size
    return pl.ds(start if isinstance(i, int) else pl.multiple_of(start, size), size)


def pivots(links, share):
    result = []
    for behind, ahead in zip(links[:-1], links[1:]):
        if not result:
            top = 1.0 + behind * share
            bottom = top + ahead
            scale = inverse(bottom)
            result.append(scale)
        else:
            top = bottom + behind * top
            below, bottom = bottom, top + ahead * bottom
            scale = inverse(bottom)
            result.append(below * scale)
    return result, top * scale


def factor_segment(links, cells, rows, fwd_p, bwd_p, near, far, gains, carry=None):
    size = 4

    def body(keep, i, carry):
        states, stores = [], []
        for (s, g), (p_ref, first, way) in zip(carry, ((fwd_p, i, 1), (bwd_p, cells - 1 - i, -1))):
            edge = first + (way < 0)
            beside = [links[plane(edge + way * u, rows)] for u in range(size + 1)]
            parts, s = pivots(beside, s)
            for u, p in enumerate(parts):
                at = plane(first + way * u, rows)
                g = g * (beside[u] * p)
                stores.append((p_ref, at, p))
                if keep:
                    stores += [(near, at, beside[u + 1] * p), (far, at, g)]
            states.append((s, g))
        for ref, at, value in stores:
            ref[at] = value
        return tuple(states)

    half = cells // 2
    if carry is None:
        ones = jnp.ones((rows, 128), jnp.float32)
        return blocks(0, half, size, functools.partial(body, False), ((ones, ones), (ones, ones)))
    (_, g_f), (_, g_b) = blocks(half, cells, size, functools.partial(body, True), carry)
    for k, value in enumerate((near[plane(0, rows)], g_b, g_f, near[plane(cells - 1, rows)])):
        gains.put(k, value)


def sweep_values(rhs, links, cells, rows, fwd_p, bwd_p, value, ends, at=0):
    size = 4

    def body(keep, i, carry):
        y_f, y_b = carry
        stores = []
        for u in range(size):
            j = cells - 1 - i - u
            here, there = plane(i + u, rows), plane(j, rows)
            p_f, p_b = fwd_p[here], bwd_p[there]
            y_f = rhs[here] * p_f + (links[here] * p_f) * y_f
            y_b = rhs[there] * p_b + (links[plane(j + 1, rows)] * p_b) * y_b
            stores += [(here, y_f), (there, y_b)]
        if keep:
            for at, y in stores:
                value[at] = y
        return y_f, y_b

    half = cells // 2
    zeros = jnp.zeros((rows, 128), jnp.float32)
    carry = blocks(0, half, size, functools.partial(body, False), (zeros, zeros))
    y_f, y_b = blocks(half, cells, size, functools.partial(body, True), carry)
    ends.put(at, y_b)
    ends.put(at + 1, y_f)


def back_substitute(before, after, cells, rows, near, far, value, unroll, store):
    def lap(block, carry):
        low, high = carry
        lows, highs = [], []
        for u in range(unroll):
            i = block * unroll + u
            here, there = plane(i, rows), plane(cells - 1 - i, rows)
            low = (value[here] + far[here] * after) + near[here] * low
            high = (value[there] + far[there] * before) + near[there] * high
            lows.append(low)
            highs.append(high)
        store(block, lows, highs)
        return low, high

    lax.fori_loop(0, cells // 2 // unroll, lap, (before, after))


def remote(src, dst, send, recv, axis, to):
    return pltpu.make_async_remote_copy(
        src_ref=src, dst_ref=dst, send_sem=send, recv_sem=recv, device_id={axis: to}, device_id_type=MESH
    )


class Parcel:
    def __init__(self, system, refs):
        self.system = system
        self.stage, self.everyone, self.send_sem, self.recv_sem = refs

    def put(self, k, value):
        rows = self.system.rows
        for o in range(self.system.owners):
            self.stage[o, k] = value[o * rows : (o + 1) * rows]

    def copy(self, o):
        own = self.system
        return remote(
            self.stage.at[o], self.everyone.at[own.me], self.send_sem.at[o], self.recv_sem.at[own.me],
            own.axis, o * own.stride,
        )

    def send(self):
        own = self.system
        for o in range(own.owners):

            @pl.when(own.me != o * own.stride)
            def _():
                self.copy(o).start()

        @pl.when(own.mine)
        def _():
            self.everyone[own.me] = self.stage[own.group]

    def arrived(self):
        own = self.system
        for d in range(1, own.count):
            k = lax.rem(own.me + d, own.count)
            part = self.everyone.at[k]
            remote(part, part, self.recv_sem.at[k], self.recv_sem.at[k], own.axis, k).wait_recv()

    def drain(self):
        for o in range(self.system.owners):

            @pl.when(self.system.me != o * self.system.stride)
            def _():
                self.copy(o).wait_send()


class Reduced:
    def __init__(self, axis, rows, merged, refs):
        self.axis, self.count, self.me = axis, lax.axis_size(axis), lax.axis_index(axis)
        self.owners, self.rows = groups(self.count, rows)
        self.stride = self.count // self.owners
        self.mine = lax.rem(self.me, self.stride) == 0
        self.group = self.me // self.stride
        self.merged = merged
        self.gains = Parcel(self, refs[:4])
        self.ends = self.gains if merged else Parcel(self, refs[4:8])
        refs = refs[4 if merged else 8 :]
        (self.relation, self.reply, self.replies, self.sides) = refs[:4]
        (self.reply_send, self.reply_recv, self.forward_send, self.forward_recv) = refs[4:]
        self.shift = 4 if merged else 0

    def factor(self):
        @pl.when(self.mine)
        def _():
            self.gains.arrived()
            gain = jnp.zeros((self.rows, 128), jnp.float32)
            for k in range(self.count):
                head_west, head_east, tail_west, tail_east = (self.gains.everyone[k, v] for v in range(4))
                scale = inverse(1.0 - head_west * gain)
                beta, gamma = head_east * scale, tail_west * gain
                self.relation[k, 0], self.relation[k, 1] = scale, beta
                self.relation[k, 2], self.relation[k, 3] = gamma, gain
                gain = tail_east + gamma * beta

    def reply_copy(self, o):
        return remote(
            self.reply.at[pl.ds(o * self.stride, self.stride)], self.replies.at[self.group],
            self.reply_send.at[o], self.reply_recv.at[self.group], self.axis, o * self.stride,
        )

    def forward_copy(self, member):
        return remote(
            self.replies.at[:, member], self.sides, self.forward_send.at[member], self.forward_recv,
            self.axis, self.group * self.stride + member,
        )

    def solve(self):
        @pl.when(self.mine)
        def _():
            if not self.merged:
                self.ends.arrived()
            value = jnp.zeros((self.rows, 128), jnp.float32)
            alphas, values = [], []
            for k in range(self.count):
                values.append(value)
                scale, gamma = self.relation[k, 0], self.relation[k, 2]
                head_west, tail_west = self.gains.everyone[k, 0], self.gains.everyone[k, 2]
                alpha = (self.ends.everyone[k, self.shift] + head_west * value) * scale
                value = (self.ends.everyone[k, self.shift + 1] + tail_west * value) + gamma * alpha
                alphas.append(alpha)
            after = jnp.zeros((self.rows, 128), jnp.float32)
            for k in reversed(range(self.count)):
                self.reply[k, 1] = after
                after = alphas[k] + self.relation[k, 1] * after
                self.reply[k, 0] = values[k] + self.relation[k, 3] * after
            for d in range(1, self.owners):
                self.reply_copy(lax.rem(self.group + d, self.owners)).start()
            self.replies[self.group] = self.reply[pl.ds(self.me, self.stride)]

    def result(self):
        @pl.when(self.mine)
        def _():
            for d in range(1, self.owners):
                o = lax.rem(self.group + d, self.owners)
                part = self.replies.at[o]
                remote(
                    part, part, self.reply_recv.at[o], self.reply_recv.at[o], self.axis, o * self.stride
                ).wait_recv()
            for member in range(1, self.stride):
                self.forward_copy(member).start()
            self.sides[...] = self.replies[:, 0]

        if self.stride > 1:

            @pl.when(jnp.logical_not(self.mine))
            def _():
                remote(
                    self.sides, self.sides, self.forward_recv, self.forward_recv,
                    self.axis, self.group * self.stride,
                ).wait_recv()

        whole = (self.owners * self.rows, 128)
        return self.sides[:, 0].reshape(whole), self.sides[:, 1].reshape(whole)

    def drain(self):
        @pl.when(self.mine)
        def _():
            for d in range(1, self.owners):
                self.reply_copy(lax.rem(self.group + d, self.owners)).wait_send()
            for member in range(1, self.stride):
                self.forward_copy(member).wait_send()


class Everywhere:
    def __init__(self, axis, refs):
        self.axis, self.count, self.me = axis, lax.axis_size(axis), lax.axis_index(axis)
        self.relation = refs[8]
        self.gains, self.ends = (Broadcast(self, refs[4 * k : 4 * k + 4]) for k in range(2))

    def factor(self):
        self.gains.arrived()
        gain = jnp.zeros(self.relation.shape[2:], jnp.float32)
        for k in range(self.count):
            head_west, head_east, tail_west, tail_east = (self.gains.everyone[k, v] for v in range(4))
            scale = inverse(1.0 - head_west * gain)
            beta, gamma = head_east * scale, tail_west * gain
            self.relation[k, 0], self.relation[k, 1] = scale, beta
            self.relation[k, 2], self.relation[k, 3] = gamma, gain
            gain = tail_east + gamma * beta

    def solve(self):
        self.ends.arrived()
        zeros = jnp.zeros(self.relation.shape[2:], jnp.float32)
        value, alphas, values = zeros, [], []
        for k in range(self.count):
            values.append(value)
            alpha = (self.ends.everyone[k, 0] + self.gains.everyone[k, 0] * value) * self.relation[k, 0]
            value = (self.ends.everyone[k, 1] + self.gains.everyone[k, 2] * value) + self.relation[k, 2] * alpha
            alphas.append(alpha)
        after, mine_before, mine_after = zeros, zeros, zeros
        for k in reversed(range(self.count)):
            here = self.me == k
            mine_after = jnp.where(here, after, mine_after)
            after = alphas[k] + self.relation[k, 1] * after
            mine_before = jnp.where(here, values[k] + self.relation[k, 3] * after, mine_before)
        return mine_before, mine_after


class Broadcast:
    def __init__(self, system, refs):
        self.system = system
        self.stage, self.everyone, self.send_sem, self.recv_sem = refs

    def put(self, k, value):
        self.stage[k] = value

    def copies(self):
        own = self.system
        for d in range(1, own.count):
            to = lax.rem(own.me + d, own.count)
            yield remote(
                self.stage, self.everyone.at[own.me], self.send_sem.at[to], self.recv_sem.at[own.me], own.axis, to
            )

    def send(self):
        for copy in self.copies():
            copy.start()
        self.everyone[self.system.me] = self.stage[...]

    def arrived(self):
        own = self.system
        for d in range(1, own.count):
            k = lax.rem(own.me + d, own.count)
            part = self.everyone.at[k]
            remote(part, part, self.recv_sem.at[k], self.recv_sem.at[k], own.axis, k).wait_recv()

    def drain(self):
        for copy in self.copies():
            copy.wait_send()


def everywhere_scratch(count, rows):
    dma = pltpu.SemaphoreType.DMA((count,))

    def vmem(*shape):
        return pltpu.VMEM(shape + (rows, 128), jnp.float32)

    return [vmem(4), vmem(count, 4), dma, dma, vmem(2), vmem(count, 2), dma, dma, vmem(count, 4)]


def groups(count, rows):
    owners = min(count, rows // ROWS)
    return owners, rows // owners


def reduced_scratch(count, rows, merged):
    owners, part = groups(count, rows)
    dma = pltpu.SemaphoreType.DMA

    def vmem(*shape):
        return pltpu.VMEM(shape + (part, 128), jnp.float32)

    scratch = []
    for values in (6,) if merged else (4, 2):
        scratch += [vmem(owners, values), vmem(count, values), dma((owners,)), dma((count,))]
    return scratch + [
        vmem(count, 4), vmem(count, 2), vmem(owners, count // owners, 2), vmem(owners, 2),
        dma((owners,)), dma((owners,)), dma((count // owners,)), dma,
    ]


def kernel(X, Y, h_in, c_in, q_in, out, *scratch):
    Z = 128
    chunks = X * Y // 128
    (stage_x, stage_y, halo_x, halo_y, halo_send, halo_recv, force, link_x, link_y, link_z) = scratch[:10]
    fwd_x, bwd_x, near_x, far_x, value_x, fwd_y, bwd_y, near_y, far_y, value_y = scratch[10:20]
    first, up_z, piv_z, lag_z, lead_z, val_z, low_z, h, c, q, load_sem = scratch[20:31]
    along_x = Reduced("gx", Y, False, scratch[31:47])
    along_y = Everywhere("gy", scratch[47:56])
    nx, ny, me_x, me_y = along_x.count, along_y.count, along_x.me, along_y.me

    part = X * Y // PARTS
    loads = [
        pltpu.make_async_copy(src.at[pl.ds(m * part, part)], dst.at[pl.ds(m * part, part)], load_sem.at[k, m])
        for k, (src, dst) in enumerate(((h_in, h), (c_in, c), (q_in, q)))
        for m in range(PARTS)
    ]
    for load in loads:
        load.start()
    barrier = pltpu.get_barrier_semaphore()
    for d in range(1, nx):
        pl.semaphore_signal(barrier, inc=1, device_id={"gx": lax.rem(me_x + d, nx)}, device_id_type=MESH)
    for d in range(1, ny):
        pl.semaphore_signal(barrier, inc=1, device_id={"gy": lax.rem(me_y + d, ny)}, device_id_type=MESH)

    for load in loads[: 2 * PARTS]:
        load.wait()

    def column(j):
        return pl.ds(j, X, stride=Y)

    for side, (i, j) in enumerate(((0, 0), (X - 1, Y - 1))):
        stage_x[side, 0], stage_x[side, 1] = h[plane(i, Y)], c[plane(i, Y)]
        stage_y[side, 0], stage_y[side, 1] = h[column(j), :], c[column(j), :]

    for load in loads[2 * PARTS :]:
        load.wait()

    def along_first(i, carry):
        head, cond, flux = carry
        stores = []
        for u in range(4):
            here, ahead = plane(i + u, Y), plane(jnp.minimum(i + u + 1, X - 1), Y)
            head_next, cond_next = h[ahead], c[ahead]
            east = link(COEF_X, cond, cond_next)
            flux_next = east * (head_next - head)
            stores += [(link_x, plane(i + u + 1, Y), east), (force, here, 2.0 * (flux_next - flux) + q[here])]
            head, cond, flux = head_next, cond_next, flux_next
        for ref, at, value in stores:
            ref[at] = value
        return head, cond, flux

    blocks(0, X, 4, along_first, (h[plane(0, Y)], c[plane(0, Y)], jnp.zeros((Y, 128), jnp.float32)))

    pl.semaphore_wait(barrier, nx - 1 + ny - 1)

    halos = []
    for a, (axis, me, count, stage, halo) in enumerate(
        (("gx", me_x, nx, stage_x, halo_x), ("gy", me_y, ny, stage_y, halo_y))
    ):
        for side in (0, 1):
            to = me - 1 if side == 0 else me + 1
            inside = me > 0 if side == 0 else me < count - 1
            send = pltpu.make_async_remote_copy(
                src_ref=stage.at[side], dst_ref=halo.at[1 - side],
                send_sem=halo_send.at[2 * a + side], recv_sem=halo_recv.at[2 * a + 1 - side],
                device_id={axis: to}, device_id_type=MESH,
            )
            take = pltpu.make_async_remote_copy(
                src_ref=stage.at[side], dst_ref=halo.at[side],
                send_sem=halo_send.at[2 * a + side], recv_sem=halo_recv.at[2 * a + side],
                device_id={axis: to}, device_id_type=MESH,
            )
            halos.append((inside, send, take))

            @pl.when(inside)
            def _():
                send.start()

            @pl.when(jnp.logical_not(inside))
            def _():
                halo[side] = jnp.zeros((2,) + halo.shape[2:], jnp.float32)

    inner = lax.broadcasted_iota(jnp.int32, (X, 128), 1) < Z - 1

    def depth_and_second(j, carry):
        head, cond, flux = carry
        stores = []
        for u in range(4):
            ahead = jnp.minimum(j + u + 1, Y - 1)
            head_next, cond_next = h[column(ahead), :], c[column(ahead), :]
            old = force[column(j + u), :]
            up = jnp.where(inner, link(COEF_Z, cond, pltpu.roll(cond, Z - 1, 1)), 0.0)
            rise = up * (pltpu.roll(head, Z - 1, 1) - head)
            north = link(COEF_Y, cond, cond_next)
            flux_next = north * (head_next - head)
            total = old + 2.0 * ((rise - pltpu.roll(rise, 1, 1)) + (flux_next - flux))
            stores.append((link_z, plane(j + u, X), up))
            stores.append((link_y, plane(j + u + 1, X), north))
            stores.append((force, column(j + u), total))
            head, cond, flux = head_next, cond_next, flux_next
        for ref, at, value in stores:
            ref[at, :] = value
        return head, cond, flux

    blocks(0, Y, 4, depth_and_second, (h[column(0), :], c[column(0), :], jnp.zeros((X, 128), jnp.float32)))

    for inside, _, take in halos:

        @pl.when(inside)
        def _():
            take.wait_recv()

    low = link(COEF_X, halo_x[0, 1], c[plane(0, Y)])
    high = link(COEF_X, halo_x[1, 1], c[plane(X - 1, Y)])
    link_x[plane(0, Y)], link_x[plane(X, Y)] = low, high
    force[plane(0, Y)] += 2.0 * (low * (halo_x[0, 0] - h[plane(0, Y)]))
    force[plane(X - 1, Y)] += 2.0 * (high * (halo_x[1, 0] - h[plane(X - 1, Y)]))
    low = link(COEF_Y, halo_y[0, 1], c[column(0), :])
    high = link(COEF_Y, halo_y[1, 1], c[column(Y - 1), :])
    link_y[plane(0, X)], link_y[plane(Y, X)] = low, high
    force[column(0), :] += 2.0 * (low * (halo_y[0, 0] - h[column(0), :]))
    force[column(Y - 1), :] += 2.0 * (high * (halo_y[1, 0] - h[column(Y - 1), :]))

    segment_x = (link_x, X, Y, fwd_x, bwd_x, near_x, far_x, along_x.gains)
    factor_segment(*segment_x, factor_segment(*segment_x))
    along_x.gains.send()
    sweep_values(force, link_x, X, Y, fwd_x, bwd_x, value_x, along_x.ends)
    along_x.ends.send()

    segment_y = (link_y, Y, X, fwd_y, bwd_y, near_y, far_y, along_y.gains)
    along_x.factor()
    halfway = factor_segment(*segment_y)
    along_x.solve()
    factor_segment(*segment_y, halfway)
    along_y.gains.send()

    before, after = along_x.result()

    def store_first(block, lows, highs):
        for u in range(4):
            i = block * 4 + u
            first[pl.ds(i, Y, stride=X), :] = lows[u]
            first[pl.ds(X - 1 - i, Y, stride=X), :] = highs[u]

    back_substitute(before, after, X, Y, near_x, far_x, value_x, 4, store_first)

    sweep_values(first, link_y, Y, X, fwd_y, bwd_y, value_y, along_y.ends)
    along_y.ends.send()
    along_y.factor()

    def turn_links(k, carry):
        for u in range(2):
            up_z[pl.ds(chunks + k + u, Z, stride=chunks), :] = link_z[plane(k + u, 128)].T
        return carry

    ones, zeros = (jnp.full((chunks, 128), v, jnp.float32) for v in (1.0, 0.0))
    up_z[plane(0, chunks)] = zeros
    blocks(0, chunks, 2, turn_links, 0)

    half = Z // 2

    def factor_z(i, carry):
        states, stores = [], []
        for s, (first_cell, way) in zip(carry, ((i, 1), (Z - 1 - i, -1))):
            edge = first_cell + (way < 0)
            beside = [up_z[plane(edge + way * u, chunks)] for u in range(9)]
            parts, s = pivots(beside, s)
            for u, p in enumerate(parts):
                at = plane(first_cell + way * u, chunks)
                stores += [(piv_z, at, p), (lag_z, at, beside[u] * p), (lead_z, at, beside[u + 1] * p)]
            states.append(s)
        for ref, at, value in stores:
            ref[at] = value
        return tuple(states)

    s_f, s_b = blocks(0, half, 8, factor_z, (ones, ones))
    middle = inverse(s_f + s_b * lead_z[plane(half - 1, chunks)])

    for system in (along_x, along_y):
        system.gains.drain()
    along_x.ends.drain()
    along_x.drain()
    for inside, send, _ in halos:

        @pl.when(inside)
        def _():
            send.wait_send()

    before, after = along_y.solve()
    per_chunk = 128 // X

    def store_second(block, lows, highs):
        val_z[pl.ds(block, Z, stride=chunks), :] = jnp.concatenate(lows, 0).T
        val_z[pl.ds(chunks - 1 - block, Z, stride=chunks), :] = jnp.concatenate(highs[::-1], 0).T

    back_substitute(before, after, Y, X, near_y, far_y, value_y, per_chunk, store_second)

    def sweep_z(i, carry):
        y_f, y_b = carry
        stores = []
        for u in range(8):
            here, there = plane(i + u, chunks), plane(Z - 1 - i - u, chunks)
            y_f = val_z[here] * piv_z[here] + lag_z[here] * y_f
            y_b = val_z[there] * piv_z[there] + lag_z[there] * y_b
            stores += [(here, y_f), (there, y_b)]
        for at, y in stores:
            low_z[at] = y
        return y_f, y_b

    y_f, y_b = blocks(0, half, 8, sweep_z, (zeros, zeros))
    below = (y_f + lead_z[plane(half - 1, chunks)] * y_b) * middle
    above = y_b + lead_z[plane(half, chunks)] * below

    def back_z(i, carry):
        low, high = carry
        stores = []
        for u in range(8):
            stores += [(plane(half - 1 - i - u, chunks), low), (plane(half + i + u, chunks), high)]
            nearer = plane(jnp.maximum(half - 2 - i - u, 0), chunks)
            farther = plane(jnp.minimum(half + 1 + i + u, Z - 1), chunks)
            low = low_z[nearer] + lead_z[nearer] * low
            high = low_z[farther] + lead_z[farther] * high
        for at, value in stores:
            out[at] = value
        return low, high

    blocks(0, half, 8, back_z, (below, above))

    along_y.ends.drain()


def finish(X, Y, delta, h, out):
    chunks, per_chunk = X * Y // 128, 128 // X

    def write(k, carry):
        stores = []
        for u in range(2):
            lines = delta[pl.ds(k + u, 128, stride=chunks), :].T
            for part in range(per_chunk):
                at = pl.ds((k + u) * per_chunk + part, X, stride=Y)
                stores.append((at, h[at, :] + lines[part * X : (part + 1) * X]))
        for at, value in stores:
            out[at, :] = value
        return carry

    blocks(0, chunks, 2, write, 0)


def per_device(water_head, conductivity, recharge):
    X, Y, Z = water_head.shape
    nx, ny = lax.axis_size("gx"), lax.axis_size("gy")

    def vmem(*shape):
        return pltpu.VMEM(shape, jnp.float32)

    cells = X * Y
    chunks = cells // 128
    scratch = [
        vmem(2, 2, Y, Z), vmem(2, 2, X, Z), vmem(2, 2, Y, Z), vmem(2, 2, X, Z),
        pltpu.SemaphoreType.DMA((4,)), pltpu.SemaphoreType.DMA((4,)),
        vmem(cells, Z), vmem(cells + Y, Z), vmem(cells + X, Z), vmem(cells, Z),
    ]
    scratch += [vmem(cells, Z) for _ in range(11)] + [vmem(cells + chunks, Z)] + [vmem(cells, Z) for _ in range(8)] + [pltpu.SemaphoreType.DMA((3, PARTS))]
    scratch += reduced_scratch(nx, Y, False) + everywhere_scratch(ny, X)
    flat = [array.reshape(cells, Z) for array in (water_head, conductivity, recharge)]
    delta = pl.pallas_call(
        functools.partial(kernel, X, Y),
        out_shape=jax.ShapeDtypeStruct((cells, Z), jnp.float32),
        in_specs=[pl.BlockSpec(memory_space=pl.ANY)] * 3,
        out_specs=pl.BlockSpec(memory_space=pltpu.VMEM),
        scratch_shapes=scratch,
        compiler_params=pltpu.CompilerParams(
            collective_id=0, has_side_effects=True, vmem_limit_bytes=56 * 2**20
        ),
    )(*flat)
    result = pl.pallas_call(
        functools.partial(finish, X, Y),
        out_shape=jax.ShapeDtypeStruct((cells, Z), jnp.float32),
        in_specs=[pl.BlockSpec(memory_space=pltpu.VMEM)] * 2,
        out_specs=pl.BlockSpec(memory_space=pltpu.VMEM),
        compiler_params=pltpu.CompilerParams(vmem_limit_bytes=16 * 2**20),
    )(delta, flat[0])
    return result.reshape(X, Y, Z)


def solution(mesh):
    placed = (P("gx", "gy", None), P("gx", "gy", None), P("gx", "gy", None))
    return jax.shard_map(
        per_device, mesh=mesh, in_specs=placed, out_specs=P("gx", "gy", None), check_vma=False
    )
```

```python
import functools

import jax
import jax.numpy as jnp
from jax import lax
from jax.experimental import pallas as pl
from jax.experimental.pallas import tpu as pltpu
from jax.sharding import PartitionSpec as P

COEF_Z = 8
COEF_X = 5120
COEF_Y = 5120
ROWS = 8
PARTS = 4
MESH = pl.DeviceIdType.MESH


def inverse(x):
    return pl.reciprocal(x, approx=True, full_range=False)


def link(coef, one_side, other_side):
    return (coef * one_side * other_side) * inverse(one_side + other_side)


def blocks(start, stop, size, body, carry):
    return lax.fori_loop(start // size, stop // size, lambda block, carry: body(block * size, carry), carry)


def plane(i, size):
    start = i * size
    return pl.ds(start if isinstance(i, int) else pl.multiple_of(start, size), size)


def pivots(links, share):
    result = []
    for behind, ahead in zip(links[:-1], links[1:]):
        if not result:
            top = 1.0 + behind * share
            bottom = top + ahead
            scale = inverse(bottom)
            result.append(scale)
        else:
            top = bottom + behind * top
            below, bottom = bottom, top + ahead * bottom
            scale = inverse(bottom)
            result.append(below * scale)
    return result, top * scale


def factor_segment(links, cells, rows, fwd_p, bwd_p, near, far, gains, carry=None):
    size = 4

    def body(keep, i, carry):
        states, stores = [], []
        for (s, g), (p_ref, first, way) in zip(carry, ((fwd_p, i, 1), (bwd_p, cells - 1 - i, -1))):
            edge = first + (way < 0)
            beside = [links[plane(edge + way * u, rows)] for u in range(size + 1)]
            parts, s = pivots(beside, s)
            for u, p in enumerate(parts):
                at = plane(first + way * u, rows)
                g = g * (beside[u] * p)
                stores.append((p_ref, at, p))
                if keep:
                    stores += [(near, at, beside[u + 1] * p), (far, at, g)]
            states.append((s, g))
        for ref, at, value in stores:
            ref[at] = value
        return tuple(states)

    half = cells // 2
    if carry is None:
        ones = jnp.ones((rows, 128), jnp.float32)
        return blocks(0, half, size, functools.partial(body, False), ((ones, ones), (ones, ones)))
    (_, g_f), (_, g_b) = blocks(half, cells, size, functools.partial(body, True), carry)
    for k, value in enumerate((near[plane(0, rows)], g_b, g_f, near[plane(cells - 1, rows)])):
        gains.put(k, value)


def sweep_values(rhs, links, cells, rows, fwd_p, bwd_p, value, ends, at=0):
    size = 4

    def body(keep, i, carry):
        y_f, y_b = carry
        stores = []
        for u in range(size):
            j = cells - 1 - i - u
            here, there = plane(i + u, rows), plane(j, rows)
            p_f, p_b = fwd_p[here], bwd_p[there]
            y_f = rhs[here] * p_f + (links[here] * p_f) * y_f
            y_b = rhs[there] * p_b + (links[plane(j + 1, rows)] * p_b) * y_b
            stores += [(here, y_f), (there, y_b)]
        if keep:
            for at, y in stores:
                value[at] = y
        return y_f, y_b

    half = cells // 2
    zeros = jnp.zeros((rows, 128), jnp.float32)
    carry = blocks(0, half, size, functools.partial(body, False), (zeros, zeros))
    y_f, y_b = blocks(half, cells, size, functools.partial(body, True), carry)
    ends.put(at, y_b)
    ends.put(at + 1, y_f)


def back_substitute(before, after, cells, rows, near, far, value, unroll, store):
    def lap(block, carry):
        low, high = carry
        lows, highs = [], []
        for u in range(unroll):
            i = block * unroll + u
            here, there = plane(i, rows), plane(cells - 1 - i, rows)
            low = (value[here] + far[here] * after) + near[here] * low
            high = (value[there] + far[there] * before) + near[there] * high
            lows.append(low)
            highs.append(high)
        store(block, lows, highs)
        return low, high

    lax.fori_loop(0, cells // 2 // unroll, lap, (before, after))


def remote(src, dst, send, recv, axis, to):
    return pltpu.make_async_remote_copy(
        src_ref=src, dst_ref=dst, send_sem=send, recv_sem=recv, device_id={axis: to}, device_id_type=MESH
    )


class Parcel:
    def __init__(self, system, refs):
        self.system = system
        self.stage, self.everyone, self.send_sem, self.recv_sem = refs

    def put(self, k, value):
        rows = self.system.rows
        for o in range(self.system.owners):
            self.stage[o, k] = value[o * rows : (o + 1) * rows]

    def copy(self, o):
        own = self.system
        return remote(
            self.stage.at[o], self.everyone.at[own.me], self.send_sem.at[o], self.recv_sem.at[own.me],
            own.axis, o * own.stride,
        )

    def send(self):
        own = self.system
        for o in range(own.owners):

            @pl.when(own.me != o * own.stride)
            def _():
                self.copy(o).start()

        @pl.when(own.mine)
        def _():
            self.everyone[own.me] = self.stage[own.group]

    def arrived(self):
        own = self.system
        for d in range(1, own.count):
            k = lax.rem(own.me + d, own.count)
            part = self.everyone.at[k]
            remote(part, part, self.recv_sem.at[k], self.recv_sem.at[k], own.axis, k).wait_recv()

    def drain(self):
        for o in range(self.system.owners):

            @pl.when(self.system.me != o * self.system.stride)
            def _():
                self.copy(o).wait_send()


class Reduced:
    def __init__(self, axis, rows, merged, refs):
        self.axis, self.count, self.me = axis, lax.axis_size(axis), lax.axis_index(axis)
        self.owners, self.rows = groups(self.count, rows)
        self.stride = self.count // self.owners
        self.mine = lax.rem(self.me, self.stride) == 0
        self.group = self.me // self.stride
        self.merged = merged
        self.gains = Parcel(self, refs[:4])
        self.ends = self.gains if merged else Parcel(self, refs[4:8])
        refs = refs[4 if merged else 8 :]
        self.relation, self.reply, self.sides, self.reply_send, self.reply_recv = refs
        self.shift = 4 if merged else 0

    def factor(self):
        @pl.when(self.mine)
        def _():
            self.gains.arrived()
            gain = jnp.zeros((self.rows, 128), jnp.float32)
            for k in range(self.count):
                head_west, head_east, tail_west, tail_east = (self.gains.everyone[k, v] for v in range(4))
                scale = inverse(1.0 - head_west * gain)
                beta, gamma = head_east * scale, tail_west * gain
                self.relation[k, 0], self.relation[k, 1] = scale, beta
                self.relation[k, 2], self.relation[k, 3] = gamma, gain
                gain = tail_east + gamma * beta

    def reply_copies(self):
        for member in range(self.stride):
            for d in range(1 if member == 0 else 0, self.owners):
                k = lax.rem(self.group + d, self.owners) * self.stride + member
                yield remote(
                    self.reply.at[k], self.sides.at[self.group],
                    self.reply_send.at[k], self.reply_recv.at[self.group], self.axis, k,
                )

    def solve(self):
        @pl.when(self.mine)
        def _():
            if not self.merged:
                self.ends.arrived()
            value = jnp.zeros((self.rows, 128), jnp.float32)
            alphas, values = [], []
            for k in range(self.count):
                values.append(value)
                scale, gamma = self.relation[k, 0], self.relation[k, 2]
                head_west, tail_west = self.gains.everyone[k, 0], self.gains.everyone[k, 2]
                alpha = (self.ends.everyone[k, self.shift] + head_west * value) * scale
                value = (self.ends.everyone[k, self.shift + 1] + tail_west * value) + gamma * alpha
                alphas.append(alpha)
            after = jnp.zeros((self.rows, 128), jnp.float32)
            for k in reversed(range(self.count)):
                self.reply[k, 1] = after
                after = alphas[k] + self.relation[k, 1] * after
                self.reply[k, 0] = values[k] + self.relation[k, 3] * after
            for copy in self.reply_copies():
                copy.start()
            self.sides[self.group] = self.reply[self.me]

    def result(self):
        for o in range(self.owners):

            @pl.when(self.me != o * self.stride)
            def _():
                part = self.sides.at[o]
                remote(
                    part, part, self.reply_recv.at[o], self.reply_recv.at[o], self.axis, o * self.stride
                ).wait_recv()

        whole = (self.owners * self.rows, 128)
        return self.sides[:, 0].reshape(whole), self.sides[:, 1].reshape(whole)

    def drain(self):
        @pl.when(self.mine)
        def _():
            for copy in self.reply_copies():
                copy.wait_send()


class Everywhere:
    def __init__(self, axis, refs):
        self.axis, self.count, self.me = axis, lax.axis_size(axis), lax.axis_index(axis)
        self.relation = refs[8]
        self.gains, self.ends = (Broadcast(self, refs[4 * k : 4 * k + 4]) for k in range(2))

    def factor(self):
        self.gains.arrived()
        gain = jnp.zeros(self.relation.shape[2:], jnp.float32)
        for k in range(self.count):
            head_west, head_east, tail_west, tail_east = (self.gains.everyone[k, v] for v in range(4))
            scale = inverse(1.0 - head_west * gain)
            beta, gamma = head_east * scale, tail_west * gain
            self.relation[k, 0], self.relation[k, 1] = scale, beta
            self.relation[k, 2], self.relation[k, 3] = gamma, gain
            gain = tail_east + gamma * beta

    def solve(self):
        self.ends.arrived()
        zeros = jnp.zeros(self.relation.shape[2:], jnp.float32)
        value, alphas, values = zeros, [], []
        for k in range(self.count):
            values.append(value)
            alpha = (self.ends.everyone[k, 0] + self.gains.everyone[k, 0] * value) * self.relation[k, 0]
            value = (self.ends.everyone[k, 1] + self.gains.everyone[k, 2] * value) + self.relation[k, 2] * alpha
            alphas.append(alpha)
        after, mine_before, mine_after = zeros, zeros, zeros
        for k in reversed(range(self.count)):
            here = self.me == k
            mine_after = jnp.where(here, after, mine_after)
            after = alphas[k] + self.relation[k, 1] * after
            mine_before = jnp.where(here, values[k] + self.relation[k, 3] * after, mine_before)
        return mine_before, mine_after


class Broadcast:
    def __init__(self, system, refs):
        self.system = system
        self.stage, self.everyone, self.send_sem, self.recv_sem = refs

    def put(self, k, value):
        self.stage[k] = value

    def copies(self):
        own = self.system
        for d in range(1, own.count):
            to = lax.rem(own.me + d, own.count)
            yield remote(
                self.stage, self.everyone.at[own.me], self.send_sem.at[to], self.recv_sem.at[own.me], own.axis, to
            )

    def send(self):
        for copy in self.copies():
            copy.start()
        self.everyone[self.system.me] = self.stage[...]

    def arrived(self):
        own = self.system
        for d in range(1, own.count):
            k = lax.rem(own.me + d, own.count)
            part = self.everyone.at[k]
            remote(part, part, self.recv_sem.at[k], self.recv_sem.at[k], own.axis, k).wait_recv()

    def drain(self):
        for copy in self.copies():
            copy.wait_send()


def everywhere_scratch(count, rows):
    dma = pltpu.SemaphoreType.DMA((count,))

    def vmem(*shape):
        return pltpu.VMEM(shape + (rows, 128), jnp.float32)

    return [vmem(4), vmem(count, 4), dma, dma, vmem(2), vmem(count, 2), dma, dma, vmem(count, 4)]


def groups(count, rows):
    owners = min(count, rows // ROWS)
    return owners, rows // owners


def reduced_scratch(count, rows, merged):
    owners, part = groups(count, rows)
    dma = pltpu.SemaphoreType.DMA

    def vmem(*shape):
        return pltpu.VMEM(shape + (part, 128), jnp.float32)

    scratch = []
    for values in (6,) if merged else (4, 2):
        scratch += [vmem(owners, values), vmem(count, values), dma((owners,)), dma((count,))]
    return scratch + [
        vmem(count, 4), vmem(count, 2), vmem(owners, 2), dma((count,)), dma((owners,)),
    ]


def kernel(X, Y, h_in, c_in, q_in, out, *scratch):
    Z = 128
    chunks = X * Y // 128
    (stage_x, stage_y, halo_x, halo_y, halo_send, halo_recv, force, link_x, link_y, link_z) = scratch[:10]
    fwd_x, bwd_x, near_x, far_x, value_x, fwd_y, bwd_y, near_y, far_y, value_y = scratch[10:20]
    first, up_z, piv_z, lag_z, lead_z, val_z, low_z, h, c, q, load_sem, delta, delta_sem = scratch[20:33]
    along_x = Reduced("gx", Y, False, scratch[33:46])
    along_y = Everywhere("gy", scratch[46:55])
    nx, ny, me_x, me_y = along_x.count, along_y.count, along_x.me, along_y.me

    part = X * Y // PARTS
    loads = [
        pltpu.make_async_copy(src.at[pl.ds(m * part, part)], dst.at[pl.ds(m * part, part)], load_sem.at[k, m])
        for k, (src, dst) in enumerate(((h_in, h), (c_in, c), (q_in, q)))
        for m in range(PARTS)
    ]
    for load in loads:
        load.start()
    barrier = pltpu.get_barrier_semaphore()
    for d in range(1, nx):
        pl.semaphore_signal(barrier, inc=1, device_id={"gx": lax.rem(me_x + d, nx)}, device_id_type=MESH)
    for d in range(1, ny):
        pl.semaphore_signal(barrier, inc=1, device_id={"gy": lax.rem(me_y + d, ny)}, device_id_type=MESH)

    for load in loads[: 2 * PARTS]:
        load.wait()

    def column(j):
        return pl.ds(j, X, stride=Y)

    for side, (i, j) in enumerate(((0, 0), (X - 1, Y - 1))):
        stage_x[side, 0], stage_x[side, 1] = h[plane(i, Y)], c[plane(i, Y)]
        stage_y[side, 0], stage_y[side, 1] = h[column(j), :], c[column(j), :]

    for load in loads[2 * PARTS :]:
        load.wait()

    def along_first(i, carry):
        head, cond, flux = carry
        stores = []
        for u in range(4):
            here, ahead = plane(i + u, Y), plane(jnp.minimum(i + u + 1, X - 1), Y)
            head_next, cond_next = h[ahead], c[ahead]
            east = link(COEF_X, cond, cond_next)
            flux_next = east * (head_next - head)
            stores += [(link_x, plane(i + u + 1, Y), east), (force, here, 2.0 * (flux_next - flux) + q[here])]
            head, cond, flux = head_next, cond_next, flux_next
        for ref, at, value in stores:
            ref[at] = value
        return head, cond, flux

    blocks(0, X, 4, along_first, (h[plane(0, Y)], c[plane(0, Y)], jnp.zeros((Y, 128), jnp.float32)))

    pl.semaphore_wait(barrier, nx - 1 + ny - 1)

    halos = []
    for a, (axis, me, count, stage, halo) in enumerate(
        (("gx", me_x, nx, stage_x, halo_x), ("gy", me_y, ny, stage_y, halo_y))
    ):
        for side in (0, 1):
            to = me - 1 if side == 0 else me + 1
            inside = me > 0 if side == 0 else me < count - 1
            send = pltpu.make_async_remote_copy(
                src_ref=stage.at[side], dst_ref=halo.at[1 - side],
                send_sem=halo_send.at[2 * a + side], recv_sem=halo_recv.at[2 * a + 1 - side],
                device_id={axis: to}, device_id_type=MESH,
            )
            take = pltpu.make_async_remote_copy(
                src_ref=stage.at[side], dst_ref=halo.at[side],
                send_sem=halo_send.at[2 * a + side], recv_sem=halo_recv.at[2 * a + side],
                device_id={axis: to}, device_id_type=MESH,
            )
            halos.append((inside, send, take))

            @pl.when(inside)
            def _():
                send.start()

            @pl.when(jnp.logical_not(inside))
            def _():
                halo[side] = jnp.zeros((2,) + halo.shape[2:], jnp.float32)

    inner = lax.broadcasted_iota(jnp.int32, (X, 128), 1) < Z - 1

    def depth_and_second(j, carry):
        head, cond, flux = carry
        stores = []
        for u in range(4):
            ahead = jnp.minimum(j + u + 1, Y - 1)
            head_next, cond_next = h[column(ahead), :], c[column(ahead), :]
            old = force[column(j + u), :]
            up = jnp.where(inner, link(COEF_Z, cond, pltpu.roll(cond, Z - 1, 1)), 0.0)
            rise = up * (pltpu.roll(head, Z - 1, 1) - head)
            north = link(COEF_Y, cond, cond_next)
            flux_next = north * (head_next - head)
            total = old + 2.0 * ((rise - pltpu.roll(rise, 1, 1)) + (flux_next - flux))
            stores.append((link_z, plane(j + u, X), up))
            stores.append((link_y, plane(j + u + 1, X), north))
            stores.append((force, column(j + u), total))
            head, cond, flux = head_next, cond_next, flux_next
        for ref, at, value in stores:
            ref[at, :] = value
        return head, cond, flux

    blocks(0, Y, 4, depth_and_second, (h[column(0), :], c[column(0), :], jnp.zeros((X, 128), jnp.float32)))

    for inside, _, take in halos:

        @pl.when(inside)
        def _():
            take.wait_recv()

    low = link(COEF_X, halo_x[0, 1], c[plane(0, Y)])
    high = link(COEF_X, halo_x[1, 1], c[plane(X - 1, Y)])
    link_x[plane(0, Y)], link_x[plane(X, Y)] = low, high
    force[plane(0, Y)] += 2.0 * (low * (halo_x[0, 0] - h[plane(0, Y)]))
    force[plane(X - 1, Y)] += 2.0 * (high * (halo_x[1, 0] - h[plane(X - 1, Y)]))
    low = link(COEF_Y, halo_y[0, 1], c[column(0), :])
    high = link(COEF_Y, halo_y[1, 1], c[column(Y - 1), :])
    link_y[plane(0, X)], link_y[plane(Y, X)] = low, high
    force[column(0), :] += 2.0 * (low * (halo_y[0, 0] - h[column(0), :]))
    force[column(Y - 1), :] += 2.0 * (high * (halo_y[1, 0] - h[column(Y - 1), :]))

    segment_x = (link_x, X, Y, fwd_x, bwd_x, near_x, far_x, along_x.gains)
    factor_segment(*segment_x, factor_segment(*segment_x))
    along_x.gains.send()
    sweep_values(force, link_x, X, Y, fwd_x, bwd_x, value_x, along_x.ends)
    along_x.ends.send()

    segment_y = (link_y, Y, X, fwd_y, bwd_y, near_y, far_y, along_y.gains)
    along_x.factor()
    halfway = factor_segment(*segment_y)
    along_x.solve()
    factor_segment(*segment_y, halfway)
    along_y.gains.send()

    before, after = along_x.result()

    def store_first(block, lows, highs):
        for u in range(4):
            i = block * 4 + u
            first[pl.ds(i, Y, stride=X), :] = lows[u]
            first[pl.ds(X - 1 - i, Y, stride=X), :] = highs[u]

    back_substitute(before, after, X, Y, near_x, far_x, value_x, 4, store_first)

    sweep_values(first, link_y, Y, X, fwd_y, bwd_y, value_y, along_y.ends)
    along_y.ends.send()
    along_y.factor()

    def turn_links(k, carry):
        for u in range(2):
            up_z[pl.ds(chunks + k + u, Z, stride=chunks), :] = link_z[plane(k + u, 128)].T
        return carry

    ones, zeros = (jnp.full((chunks, 128), v, jnp.float32) for v in (1.0, 0.0))
    up_z[plane(0, chunks)] = zeros
    blocks(0, chunks, 2, turn_links, 0)

    half = Z // 2

    def factor_z(i, carry):
        states, stores = [], []
        for s, (first_cell, way) in zip(carry, ((i, 1), (Z - 1 - i, -1))):
            edge = first_cell + (way < 0)
            beside = [up_z[plane(edge + way * u, chunks)] for u in range(9)]
            parts, s = pivots(beside, s)
            for u, p in enumerate(parts):
                at = plane(first_cell + way * u, chunks)
                stores += [(piv_z, at, p), (lag_z, at, beside[u] * p), (lead_z, at, beside[u + 1] * p)]
            states.append(s)
        for ref, at, value in stores:
            ref[at] = value
        return tuple(states)

    s_f, s_b = blocks(0, half, 8, factor_z, (ones, ones))
    middle = inverse(s_f + s_b * lead_z[plane(half - 1, chunks)])

    for system in (along_x, along_y):
        system.gains.drain()
    along_x.ends.drain()
    along_x.drain()
    for inside, send, _ in halos:

        @pl.when(inside)
        def _():
            send.wait_send()

    before, after = along_y.solve()
    per_chunk = 128 // X

    def store_second(block, lows, highs):
        val_z[pl.ds(block, Z, stride=chunks), :] = jnp.concatenate(lows, 0).T
        val_z[pl.ds(chunks - 1 - block, Z, stride=chunks), :] = jnp.concatenate(highs[::-1], 0).T

    back_substitute(before, after, Y, X, near_y, far_y, value_y, per_chunk, store_second)

    def sweep_z(i, carry):
        y_f, y_b = carry
        stores = []
        for u in range(8):
            here, there = plane(i + u, chunks), plane(Z - 1 - i - u, chunks)
            y_f = val_z[here] * piv_z[here] + lag_z[here] * y_f
            y_b = val_z[there] * piv_z[there] + lag_z[there] * y_b
            stores += [(here, y_f), (there, y_b)]
        for at, y in stores:
            low_z[at] = y
        return y_f, y_b

    y_f, y_b = blocks(0, half, 8, sweep_z, (zeros, zeros))
    below = (y_f + lead_z[plane(half - 1, chunks)] * y_b) * middle
    above = y_b + lead_z[plane(half, chunks)] * below

    def back_z(i, carry):
        low, high = carry
        stores = []
        for u in range(8):
            stores += [(plane(half - 1 - i - u, chunks), low), (plane(half + i + u, chunks), high)]
            nearer = plane(jnp.maximum(half - 2 - i - u, 0), chunks)
            farther = plane(jnp.minimum(half + 1 + i + u, Z - 1), chunks)
            low = low_z[nearer] + lead_z[nearer] * low
            high = low_z[farther] + lead_z[farther] * high
        for at, value in stores:
            delta[at] = value
        return low, high

    def give(k, start, stop):
        cells = pl.ds(start * chunks, (stop - start) * chunks)
        return pltpu.make_async_copy(delta.at[cells], out.at[cells], delta_sem.at[k])

    quarter = half // 2
    gives = [give(0, quarter, Z - quarter), give(1, 0, quarter), give(2, Z - quarter, Z)]
    carry = blocks(0, quarter, 8, back_z, (below, above))
    gives[0].start()
    blocks(quarter, half, 8, back_z, carry)
    gives[1].start()
    gives[2].start()

    along_y.ends.drain()
    for copy in gives:
        copy.wait()


def finish(X, Y, delta, h, out):
    chunks, per_chunk = X * Y // 128, 128 // X

    def write(k, carry):
        stores = []
        for u in range(2):
            lines = delta[pl.ds(k + u, 128, stride=chunks), :].T
            for part in range(per_chunk):
                at = pl.ds((k + u) * per_chunk + part, X, stride=Y)
                stores.append((at, h[at, :] + lines[part * X : (part + 1) * X]))
        for at, value in stores:
            out[at, :] = value
        return carry

    blocks(0, chunks, 2, write, 0)


def per_device(water_head, conductivity, recharge):
    X, Y, Z = water_head.shape
    nx, ny = lax.axis_size("gx"), lax.axis_size("gy")

    def vmem(*shape):
        return pltpu.VMEM(shape, jnp.float32)

    cells = X * Y
    chunks = cells // 128
    scratch = [
        vmem(2, 2, Y, Z), vmem(2, 2, X, Z), vmem(2, 2, Y, Z), vmem(2, 2, X, Z),
        pltpu.SemaphoreType.DMA((4,)), pltpu.SemaphoreType.DMA((4,)),
        vmem(cells, Z), vmem(cells + Y, Z), vmem(cells + X, Z), vmem(cells, Z),
    ]
    scratch += [vmem(cells, Z) for _ in range(11)] + [vmem(cells + chunks, Z)] + [vmem(cells, Z) for _ in range(8)] + [pltpu.SemaphoreType.DMA((3, PARTS)), vmem(cells, Z), pltpu.SemaphoreType.DMA((3,))]
    scratch += reduced_scratch(nx, Y, False) + everywhere_scratch(ny, X)
    flat = [array.reshape(cells, Z) for array in (water_head, conductivity, recharge)]
    delta = pl.pallas_call(
        functools.partial(kernel, X, Y),
        out_shape=jax.ShapeDtypeStruct((cells, Z), jnp.float32),
        in_specs=[pl.BlockSpec(memory_space=pl.ANY)] * 3,
        out_specs=pl.BlockSpec(memory_space=pl.ANY),
        scratch_shapes=scratch,
        compiler_params=pltpu.CompilerParams(
            collective_id=0, has_side_effects=True, vmem_limit_bytes=56 * 2**20
        ),
    )(*flat)
    result = pl.pallas_call(
        functools.partial(finish, X, Y),
        out_shape=jax.ShapeDtypeStruct((cells, Z), jnp.float32),
        in_specs=[pl.BlockSpec(memory_space=pltpu.VMEM)] * 2,
        out_specs=pl.BlockSpec(memory_space=pltpu.VMEM),
        compiler_params=pltpu.CompilerParams(vmem_limit_bytes=16 * 2**20),
    )(delta, flat[0])
    return result.reshape(X, Y, Z)


def solution(mesh):
    placed = (P("gx", "gy", None), P("gx", "gy", None), P("gx", "gy", None))
    return jax.shard_map(
        per_device, mesh=mesh, in_specs=placed, out_specs=P("gx", "gy", None), check_vma=False
    )
```

```python
import functools

import jax
import jax.numpy as jnp
from jax import lax
from jax.experimental import pallas as pl
from jax.experimental.pallas import tpu as pltpu
from jax.sharding import PartitionSpec as P

COEF_Z = 8
COEF_X = 5120
COEF_Y = 5120
ROWS = 8
PARTS = 4
MESH = pl.DeviceIdType.MESH


def inverse(x):
    return pl.reciprocal(x, approx=True, full_range=False)


def link(coef, one_side, other_side):
    return (coef * one_side * other_side) * inverse(one_side + other_side)


def blocks(start, stop, size, body, carry):
    return lax.fori_loop(start // size, stop // size, lambda block, carry: body(block * size, carry), carry)


def plane(i, size):
    start = i * size
    return pl.ds(start if isinstance(i, int) else pl.multiple_of(start, size), size)


def pivots(links, share):
    result = []
    for behind, ahead in zip(links[:-1], links[1:]):
        if not result:
            top = 1.0 + behind * share
            bottom = top + ahead
            scale = inverse(bottom)
            result.append(scale)
        else:
            top = bottom + behind * top
            below, bottom = bottom, top + ahead * bottom
            scale = inverse(bottom)
            result.append(below * scale)
    return result, top * scale


def factor_segment(links, cells, rows, fwd_p, bwd_p, near, far, gains, carry=None):
    size = 4

    def body(keep, i, carry):
        states, stores = [], []
        for (s, g), (p_ref, first, way) in zip(carry, ((fwd_p, i, 1), (bwd_p, cells - 1 - i, -1))):
            edge = first + (way < 0)
            beside = [links[plane(edge + way * u, rows)] for u in range(size + 1)]
            parts, s = pivots(beside, s)
            for u, p in enumerate(parts):
                at = plane(first + way * u, rows)
                g = g * (beside[u] * p)
                stores.append((p_ref, at, p))
                if keep:
                    stores += [(near, at, beside[u + 1] * p), (far, at, g)]
            states.append((s, g))
        for ref, at, value in stores:
            ref[at] = value
        return tuple(states)

    half = cells // 2
    if carry is None:
        ones = jnp.ones((rows, 128), jnp.float32)
        return blocks(0, half, size, functools.partial(body, False), ((ones, ones), (ones, ones)))
    (_, g_f), (_, g_b) = blocks(half, cells, size, functools.partial(body, True), carry)
    for k, value in enumerate((near[plane(0, rows)], g_b, g_f, near[plane(cells - 1, rows)])):
        gains.put(k, value)


def sweep_values(rhs, links, cells, rows, fwd_p, bwd_p, value, ends, at=0):
    size = 4

    def body(keep, i, carry):
        y_f, y_b = carry
        stores = []
        for u in range(size):
            j = cells - 1 - i - u
            here, there = plane(i + u, rows), plane(j, rows)
            p_f, p_b = fwd_p[here], bwd_p[there]
            y_f = rhs[here] * p_f + (links[here] * p_f) * y_f
            y_b = rhs[there] * p_b + (links[plane(j + 1, rows)] * p_b) * y_b
            stores += [(here, y_f), (there, y_b)]
        if keep:
            for at, y in stores:
                value[at] = y
        return y_f, y_b

    half = cells // 2
    zeros = jnp.zeros((rows, 128), jnp.float32)
    carry = blocks(0, half, size, functools.partial(body, False), (zeros, zeros))
    y_f, y_b = blocks(half, cells, size, functools.partial(body, True), carry)
    ends.put(at, y_b)
    ends.put(at + 1, y_f)


def back_substitute(before, after, cells, rows, near, far, value, unroll, store):
    def lap(block, carry):
        low, high = carry
        lows, highs = [], []
        for u in range(unroll):
            i = block * unroll + u
            here, there = plane(i, rows), plane(cells - 1 - i, rows)
            low = (value[here] + far[here] * after) + near[here] * low
            high = (value[there] + far[there] * before) + near[there] * high
            lows.append(low)
            highs.append(high)
        store(block, lows, highs)
        return low, high

    lax.fori_loop(0, cells // 2 // unroll, lap, (before, after))


def remote(src, dst, send, recv, axis, to):
    return pltpu.make_async_remote_copy(
        src_ref=src, dst_ref=dst, send_sem=send, recv_sem=recv, device_id={axis: to}, device_id_type=MESH
    )


class Parcel:
    def __init__(self, system, refs):
        self.system = system
        self.stage, self.everyone, self.send_sem, self.recv_sem = refs

    def put(self, k, value):
        rows = self.system.rows
        for o in range(self.system.owners):
            self.stage[o, k] = value[o * rows : (o + 1) * rows]

    def copy(self, o):
        own = self.system
        return remote(
            self.stage.at[o], self.everyone.at[own.me], self.send_sem.at[o], self.recv_sem.at[own.me],
            own.axis, o * own.stride,
        )

    def send(self):
        own = self.system
        for o in range(own.owners):

            @pl.when(own.me != o * own.stride)
            def _():
                self.copy(o).start()

        @pl.when(own.mine)
        def _():
            self.everyone[own.me] = self.stage[own.group]

    def arrived(self):
        own = self.system
        for d in range(1, own.count):
            k = lax.rem(own.me + d, own.count)
            part = self.everyone.at[k]
            remote(part, part, self.recv_sem.at[k], self.recv_sem.at[k], own.axis, k).wait_recv()

    def drain(self):
        for o in range(self.system.owners):

            @pl.when(self.system.me != o * self.system.stride)
            def _():
                self.copy(o).wait_send()


class Reduced:
    def __init__(self, axis, rows, merged, refs):
        self.axis, self.count, self.me = axis, lax.axis_size(axis), lax.axis_index(axis)
        self.owners, self.rows = groups(self.count, rows)
        self.stride = self.count // self.owners
        self.mine = lax.rem(self.me, self.stride) == 0
        self.group = self.me // self.stride
        self.merged = merged
        self.gains = Parcel(self, refs[:4])
        self.ends = self.gains if merged else Parcel(self, refs[4:8])
        refs = refs[4 if merged else 8 :]
        self.relation, self.reply, self.sides, self.reply_send, self.reply_recv = refs
        self.shift = 4 if merged else 0

    def factor(self):
        @pl.when(self.mine)
        def _():
            self.gains.arrived()
            gain = jnp.zeros((self.rows, 128), jnp.float32)
            for k in range(self.count):
                head_west, head_east, tail_west, tail_east = (self.gains.everyone[k, v] for v in range(4))
                scale = inverse(1.0 - head_west * gain)
                beta, gamma = head_east * scale, tail_west * gain
                self.relation[k, 0], self.relation[k, 1] = scale, beta
                self.relation[k, 2], self.relation[k, 3] = gamma, gain
                gain = tail_east + gamma * beta

    def reply_copies(self):
        for member in range(self.stride):
            for d in range(1 if member == 0 else 0, self.owners):
                k = lax.rem(self.group + d, self.owners) * self.stride + member
                yield remote(
                    self.reply.at[k], self.sides.at[self.group],
                    self.reply_send.at[k], self.reply_recv.at[self.group], self.axis, k,
                )

    def solve(self):
        @pl.when(self.mine)
        def _():
            if not self.merged:
                self.ends.arrived()
            value = jnp.zeros((self.rows, 128), jnp.float32)
            alphas, values = [], []
            for k in range(self.count):
                values.append(value)
                scale, gamma = self.relation[k, 0], self.relation[k, 2]
                head_west, tail_west = self.gains.everyone[k, 0], self.gains.everyone[k, 2]
                alpha = (self.ends.everyone[k, self.shift] + head_west * value) * scale
                value = (self.ends.everyone[k, self.shift + 1] + tail_west * value) + gamma * alpha
                alphas.append(alpha)
            after = jnp.zeros((self.rows, 128), jnp.float32)
            for k in reversed(range(self.count)):
                self.reply[k, 1] = after
                after = alphas[k] + self.relation[k, 1] * after
                self.reply[k, 0] = values[k] + self.relation[k, 3] * after
            for copy in self.reply_copies():
                copy.start()
            self.sides[self.group] = self.reply[self.me]

    def result(self):
        for o in range(self.owners):

            @pl.when(self.me != o * self.stride)
            def _():
                part = self.sides.at[o]
                remote(
                    part, part, self.reply_recv.at[o], self.reply_recv.at[o], self.axis, o * self.stride
                ).wait_recv()

        whole = (self.owners * self.rows, 128)
        return self.sides[:, 0].reshape(whole), self.sides[:, 1].reshape(whole)

    def drain(self):
        @pl.when(self.mine)
        def _():
            for copy in self.reply_copies():
                copy.wait_send()


class Everywhere:
    def __init__(self, axis, refs):
        self.axis, self.count, self.me = axis, lax.axis_size(axis), lax.axis_index(axis)
        self.relation = refs[8]
        self.gains, self.ends = (Broadcast(self, refs[4 * k : 4 * k + 4]) for k in range(2))

    def factor(self):
        self.gains.arrived()
        gain = jnp.zeros(self.relation.shape[2:], jnp.float32)
        for k in range(self.count):
            head_west, head_east, tail_west, tail_east = (self.gains.everyone[k, v] for v in range(4))
            scale = inverse(1.0 - head_west * gain)
            beta, gamma = head_east * scale, tail_west * gain
            self.relation[k, 0], self.relation[k, 1] = scale, beta
            self.relation[k, 2], self.relation[k, 3] = gamma, gain
            gain = tail_east + gamma * beta

    def solve(self):
        self.ends.arrived()
        zeros = jnp.zeros(self.relation.shape[2:], jnp.float32)
        value, alphas, values = zeros, [], []
        for k in range(self.count):
            values.append(value)
            alpha = (self.ends.everyone[k, 0] + self.gains.everyone[k, 0] * value) * self.relation[k, 0]
            value = (self.ends.everyone[k, 1] + self.gains.everyone[k, 2] * value) + self.relation[k, 2] * alpha
            alphas.append(alpha)
        after, mine_before, mine_after = zeros, zeros, zeros
        for k in reversed(range(self.count)):
            here = self.me == k
            mine_after = jnp.where(here, after, mine_after)
            after = alphas[k] + self.relation[k, 1] * after
            mine_before = jnp.where(here, values[k] + self.relation[k, 3] * after, mine_before)
        return mine_before, mine_after


class Broadcast:
    def __init__(self, system, refs):
        self.system = system
        self.stage, self.everyone, self.send_sem, self.recv_sem = refs

    def put(self, k, value):
        self.stage[k] = value

    def copies(self):
        own = self.system
        for d in range(1, own.count):
            to = lax.rem(own.me + d, own.count)
            yield remote(
                self.stage, self.everyone.at[own.me], self.send_sem.at[to], self.recv_sem.at[own.me], own.axis, to
            )

    def send(self):
        for copy in self.copies():
            copy.start()
        self.everyone[self.system.me] = self.stage[...]

    def arrived(self):
        own = self.system
        for d in range(1, own.count):
            k = lax.rem(own.me + d, own.count)
            part = self.everyone.at[k]
            remote(part, part, self.recv_sem.at[k], self.recv_sem.at[k], own.axis, k).wait_recv()

    def drain(self):
        for copy in self.copies():
            copy.wait_send()


def everywhere_scratch(count, rows):
    dma = pltpu.SemaphoreType.DMA((count,))

    def vmem(*shape):
        return pltpu.VMEM(shape + (rows, 128), jnp.float32)

    return [vmem(4), vmem(count, 4), dma, dma, vmem(2), vmem(count, 2), dma, dma, vmem(count, 4)]


def groups(count, rows):
    owners = min(count, rows // ROWS)
    return owners, rows // owners


def reduced_scratch(count, rows, merged):
    owners, part = groups(count, rows)
    dma = pltpu.SemaphoreType.DMA

    def vmem(*shape):
        return pltpu.VMEM(shape + (part, 128), jnp.float32)

    scratch = []
    for values in (6,) if merged else (4, 2):
        scratch += [vmem(owners, values), vmem(count, values), dma((owners,)), dma((count,))]
    return scratch + [
        vmem(count, 4), vmem(count, 2), vmem(owners, 2), dma((count,)), dma((owners,)),
    ]


def kernel(X, Y, h_in, c_in, q_in, out, *scratch):
    Z = 128
    chunks = X * Y // 128
    (stage_x, stage_y, halo_x, halo_y, halo_send, halo_recv, force, link_x, link_y, link_z) = scratch[:10]
    fwd_x, bwd_x, near_x, far_x, value_x, fwd_y, bwd_y, near_y, far_y, value_y = scratch[10:20]
    first, up_z, piv_z, lag_z, lead_z, val_z, low_z, h, c, q, load_sem, delta, delta_sem = scratch[20:33]
    along_x = Reduced("gx", Y, False, scratch[33:46])
    along_y = Everywhere("gy", scratch[46:55])
    nx, ny, me_x, me_y = along_x.count, along_y.count, along_x.me, along_y.me

    part = X * Y // PARTS
    loads = [
        pltpu.make_async_copy(src.at[pl.ds(m * part, part)], dst.at[pl.ds(m * part, part)], load_sem.at[k, m])
        for k, (src, dst) in enumerate(((h_in, h), (c_in, c), (q_in, q)))
        for m in range(PARTS)
    ]
    for load in loads:
        load.start()
    barrier = pltpu.get_barrier_semaphore()
    for d in range(1, nx):
        pl.semaphore_signal(barrier, inc=1, device_id={"gx": lax.rem(me_x + d, nx)}, device_id_type=MESH)
    for d in range(1, ny):
        pl.semaphore_signal(barrier, inc=1, device_id={"gy": lax.rem(me_y + d, ny)}, device_id_type=MESH)

    for load in loads[: 2 * PARTS]:
        load.wait()

    def column(j):
        return pl.ds(j, X, stride=Y)

    for side, (i, j) in enumerate(((0, 0), (X - 1, Y - 1))):
        stage_x[side, 0], stage_x[side, 1] = h[plane(i, Y)], c[plane(i, Y)]
        stage_y[side, 0], stage_y[side, 1] = h[column(j), :], c[column(j), :]

    pl.semaphore_wait(barrier, nx - 1 + ny - 1)

    halos = []
    for a, (axis, me, count, stage, halo) in enumerate(
        (("gx", me_x, nx, stage_x, halo_x), ("gy", me_y, ny, stage_y, halo_y))
    ):
        for side in (0, 1):
            to = me - 1 if side == 0 else me + 1
            inside = me > 0 if side == 0 else me < count - 1
            send = pltpu.make_async_remote_copy(
                src_ref=stage.at[side], dst_ref=halo.at[1 - side],
                send_sem=halo_send.at[2 * a + side], recv_sem=halo_recv.at[2 * a + 1 - side],
                device_id={axis: to}, device_id_type=MESH,
            )
            take = pltpu.make_async_remote_copy(
                src_ref=stage.at[side], dst_ref=halo.at[side],
                send_sem=halo_send.at[2 * a + side], recv_sem=halo_recv.at[2 * a + side],
                device_id={axis: to}, device_id_type=MESH,
            )
            halos.append((inside, send, take))

            @pl.when(inside)
            def _():
                send.start()

            @pl.when(jnp.logical_not(inside))
            def _():
                halo[side] = jnp.zeros((2,) + halo.shape[2:], jnp.float32)

    for load in loads[2 * PARTS :]:
        load.wait()

    def along_first(i, carry):
        head, cond, flux = carry
        stores = []
        for u in range(4):
            here, ahead = plane(i + u, Y), plane(jnp.minimum(i + u + 1, X - 1), Y)
            head_next, cond_next = h[ahead], c[ahead]
            east = link(COEF_X, cond, cond_next)
            flux_next = east * (head_next - head)
            stores += [(link_x, plane(i + u + 1, Y), east), (force, here, 2.0 * (flux_next - flux) + q[here])]
            head, cond, flux = head_next, cond_next, flux_next
        for ref, at, value in stores:
            ref[at] = value
        return head, cond, flux

    blocks(0, X, 4, along_first, (h[plane(0, Y)], c[plane(0, Y)], jnp.zeros((Y, 128), jnp.float32)))

    inner = lax.broadcasted_iota(jnp.int32, (X, 128), 1) < Z - 1

    def depth_and_second(j, carry):
        head, cond, flux = carry
        stores = []
        for u in range(4):
            ahead = jnp.minimum(j + u + 1, Y - 1)
            head_next, cond_next = h[column(ahead), :], c[column(ahead), :]
            old = force[column(j + u), :]
            up = jnp.where(inner, link(COEF_Z, cond, pltpu.roll(cond, Z - 1, 1)), 0.0)
            rise = up * (pltpu.roll(head, Z - 1, 1) - head)
            north = link(COEF_Y, cond, cond_next)
            flux_next = north * (head_next - head)
            total = old + 2.0 * ((rise - pltpu.roll(rise, 1, 1)) + (flux_next - flux))
            stores.append((link_z, plane(j + u, X), up))
            stores.append((link_y, plane(j + u + 1, X), north))
            stores.append((force, column(j + u), total))
            head, cond, flux = head_next, cond_next, flux_next
        for ref, at, value in stores:
            ref[at, :] = value
        return head, cond, flux

    blocks(0, Y, 4, depth_and_second, (h[column(0), :], c[column(0), :], jnp.zeros((X, 128), jnp.float32)))

    for inside, _, take in halos:

        @pl.when(inside)
        def _():
            take.wait_recv()

    low = link(COEF_X, halo_x[0, 1], c[plane(0, Y)])
    high = link(COEF_X, halo_x[1, 1], c[plane(X - 1, Y)])
    link_x[plane(0, Y)], link_x[plane(X, Y)] = low, high
    force[plane(0, Y)] += 2.0 * (low * (halo_x[0, 0] - h[plane(0, Y)]))
    force[plane(X - 1, Y)] += 2.0 * (high * (halo_x[1, 0] - h[plane(X - 1, Y)]))
    low = link(COEF_Y, halo_y[0, 1], c[column(0), :])
    high = link(COEF_Y, halo_y[1, 1], c[column(Y - 1), :])
    link_y[plane(0, X)], link_y[plane(Y, X)] = low, high
    force[column(0), :] += 2.0 * (low * (halo_y[0, 0] - h[column(0), :]))
    force[column(Y - 1), :] += 2.0 * (high * (halo_y[1, 0] - h[column(Y - 1), :]))

    segment_x = (link_x, X, Y, fwd_x, bwd_x, near_x, far_x, along_x.gains)
    factor_segment(*segment_x, factor_segment(*segment_x))
    along_x.gains.send()
    sweep_values(force, link_x, X, Y, fwd_x, bwd_x, value_x, along_x.ends)
    along_x.ends.send()

    segment_y = (link_y, Y, X, fwd_y, bwd_y, near_y, far_y, along_y.gains)
    along_x.factor()
    halfway = factor_segment(*segment_y)
    along_x.solve()
    factor_segment(*segment_y, halfway)
    along_y.gains.send()

    before, after = along_x.result()

    def store_first(block, lows, highs):
        for u in range(4):
            i = block * 4 + u
            first[pl.ds(i, Y, stride=X), :] = lows[u]
            first[pl.ds(X - 1 - i, Y, stride=X), :] = highs[u]

    back_substitute(before, after, X, Y, near_x, far_x, value_x, 4, store_first)

    sweep_values(first, link_y, Y, X, fwd_y, bwd_y, value_y, along_y.ends)
    along_y.ends.send()
    along_y.factor()

    def turn_links(k, carry):
        for u in range(2):
            up_z[pl.ds(chunks + k + u, Z, stride=chunks), :] = link_z[plane(k + u, 128)].T
        return carry

    ones, zeros = (jnp.full((chunks, 128), v, jnp.float32) for v in (1.0, 0.0))
    up_z[plane(0, chunks)] = zeros
    blocks(0, chunks, 2, turn_links, 0)

    half = Z // 2

    def factor_z(i, carry):
        states, stores = [], []
        for s, (first_cell, way) in zip(carry, ((i, 1), (Z - 1 - i, -1))):
            edge = first_cell + (way < 0)
            beside = [up_z[plane(edge + way * u, chunks)] for u in range(9)]
            parts, s = pivots(beside, s)
            for u, p in enumerate(parts):
                at = plane(first_cell + way * u, chunks)
                stores += [(piv_z, at, p), (lag_z, at, beside[u] * p), (lead_z, at, beside[u + 1] * p)]
            states.append(s)
        for ref, at, value in stores:
            ref[at] = value
        return tuple(states)

    s_f, s_b = blocks(0, half, 8, factor_z, (ones, ones))
    middle = inverse(s_f + s_b * lead_z[plane(half - 1, chunks)])

    for system in (along_x, along_y):
        system.gains.drain()
    along_x.ends.drain()
    along_x.drain()
    for inside, send, _ in halos:

        @pl.when(inside)
        def _():
            send.wait_send()

    before, after = along_y.solve()
    per_chunk = 128 // X

    def store_second(block, lows, highs):
        val_z[pl.ds(block, Z, stride=chunks), :] = jnp.concatenate(lows, 0).T
        val_z[pl.ds(chunks - 1 - block, Z, stride=chunks), :] = jnp.concatenate(highs[::-1], 0).T

    back_substitute(before, after, Y, X, near_y, far_y, value_y, per_chunk, store_second)

    def sweep_z(i, carry):
        y_f, y_b = carry
        stores = []
        for u in range(8):
            here, there = plane(i + u, chunks), plane(Z - 1 - i - u, chunks)
            y_f = val_z[here] * piv_z[here] + lag_z[here] * y_f
            y_b = val_z[there] * piv_z[there] + lag_z[there] * y_b
            stores += [(here, y_f), (there, y_b)]
        for at, y in stores:
            low_z[at] = y
        return y_f, y_b

    y_f, y_b = blocks(0, half, 8, sweep_z, (zeros, zeros))
    below = (y_f + lead_z[plane(half - 1, chunks)] * y_b) * middle
    above = y_b + lead_z[plane(half, chunks)] * below

    def back_z(i, carry):
        low, high = carry
        stores = []
        for u in range(8):
            stores += [(plane(half - 1 - i - u, chunks), low), (plane(half + i + u, chunks), high)]
            nearer = plane(jnp.maximum(half - 2 - i - u, 0), chunks)
            farther = plane(jnp.minimum(half + 1 + i + u, Z - 1), chunks)
            low = low_z[nearer] + lead_z[nearer] * low
            high = low_z[farther] + lead_z[farther] * high
        for at, value in stores:
            delta[at] = value
        return low, high

    def give(k, start, stop):
        cells = pl.ds(start * chunks, (stop - start) * chunks)
        return pltpu.make_async_copy(delta.at[cells], out.at[cells], delta_sem.at[k])

    quarter = half // 2
    gives = [give(0, quarter, Z - quarter), give(1, 0, quarter), give(2, Z - quarter, Z)]
    carry = blocks(0, quarter, 8, back_z, (below, above))
    gives[0].start()
    blocks(quarter, half, 8, back_z, carry)
    gives[1].start()
    gives[2].start()

    along_y.ends.drain()
    for copy in gives:
        copy.wait()


def finish(X, Y, delta, h, out):
    chunks, per_chunk = X * Y // 128, 128 // X

    def write(k, carry):
        stores = []
        for u in range(2):
            lines = delta[pl.ds(k + u, 128, stride=chunks), :].T
            for part in range(per_chunk):
                at = pl.ds((k + u) * per_chunk + part, X, stride=Y)
                stores.append((at, h[at, :] + lines[part * X : (part + 1) * X]))
        for at, value in stores:
            out[at, :] = value
        return carry

    blocks(0, chunks, 2, write, 0)


def per_device(water_head, conductivity, recharge):
    X, Y, Z = water_head.shape
    nx, ny = lax.axis_size("gx"), lax.axis_size("gy")

    def vmem(*shape):
        return pltpu.VMEM(shape, jnp.float32)

    cells = X * Y
    chunks = cells // 128
    scratch = [
        vmem(2, 2, Y, Z), vmem(2, 2, X, Z), vmem(2, 2, Y, Z), vmem(2, 2, X, Z),
        pltpu.SemaphoreType.DMA((4,)), pltpu.SemaphoreType.DMA((4,)),
        vmem(cells, Z), vmem(cells + Y, Z), vmem(cells + X, Z), vmem(cells, Z),
    ]
    scratch += [vmem(cells, Z) for _ in range(11)] + [vmem(cells + chunks, Z)] + [vmem(cells, Z) for _ in range(8)] + [pltpu.SemaphoreType.DMA((3, PARTS)), vmem(cells, Z), pltpu.SemaphoreType.DMA((3,))]
    scratch += reduced_scratch(nx, Y, False) + everywhere_scratch(ny, X)
    flat = [array.reshape(cells, Z) for array in (water_head, conductivity, recharge)]
    delta = pl.pallas_call(
        functools.partial(kernel, X, Y),
        out_shape=jax.ShapeDtypeStruct((cells, Z), jnp.float32),
        in_specs=[pl.BlockSpec(memory_space=pl.ANY)] * 3,
        out_specs=pl.BlockSpec(memory_space=pl.ANY),
        scratch_shapes=scratch,
        compiler_params=pltpu.CompilerParams(
            collective_id=0, has_side_effects=True, vmem_limit_bytes=56 * 2**20
        ),
    )(*flat)
    result = pl.pallas_call(
        functools.partial(finish, X, Y),
        out_shape=jax.ShapeDtypeStruct((cells, Z), jnp.float32),
        in_specs=[pl.BlockSpec(memory_space=pltpu.VMEM)] * 2,
        out_specs=pl.BlockSpec(memory_space=pltpu.VMEM),
        compiler_params=pltpu.CompilerParams(vmem_limit_bytes=16 * 2**20),
    )(delta, flat[0])
    return result.reshape(X, Y, Z)


def solution(mesh):
    placed = (P("gx", "gy", None), P("gx", "gy", None), P("gx", "gy", None))
    return jax.shard_map(
        per_device, mesh=mesh, in_specs=placed, out_specs=P("gx", "gy", None), check_vma=False
    )
```

```python
import functools

import jax
import jax.numpy as jnp
from jax import lax
from jax.experimental import pallas as pl
from jax.experimental.pallas import tpu as pltpu
from jax.sharding import PartitionSpec as P

COEF_Z = 8
COEF_X = 5120
COEF_Y = 5120
ROWS = 8
PARTS = 4
MESH = pl.DeviceIdType.MESH


def inverse(x):
    return pl.reciprocal(x, approx=True, full_range=False)


def link(coef, one_side, other_side):
    return (coef * one_side * other_side) * inverse(one_side + other_side)


def blocks(start, stop, size, body, carry):
    return lax.fori_loop(start // size, stop // size, lambda block, carry: body(block * size, carry), carry)


def plane(i, size):
    start = i * size
    return pl.ds(start if isinstance(i, int) else pl.multiple_of(start, size), size)


def pivots(links, share):
    result = []
    for behind, ahead in zip(links[:-1], links[1:]):
        if not result:
            top = 1.0 + behind * share
            bottom = top + ahead
            scale = inverse(bottom)
            result.append(scale)
        else:
            top = bottom + behind * top
            below, bottom = bottom, top + ahead * bottom
            scale = inverse(bottom)
            result.append(below * scale)
    return result, top * scale


def factor_segment(links, cells, rows, fwd_p, bwd_p, near, far, gains, carry=None):
    size = 4

    def body(keep, i, carry):
        states, stores = [], []
        for (s, g), (p_ref, first, way) in zip(carry, ((fwd_p, i, 1), (bwd_p, cells - 1 - i, -1))):
            edge = first + (way < 0)
            beside = [links[plane(edge + way * u, rows)] for u in range(size + 1)]
            parts, s = pivots(beside, s)
            for u, p in enumerate(parts):
                at = plane(first + way * u, rows)
                g = g * (beside[u] * p)
                stores.append((p_ref, at, p))
                if keep:
                    stores += [(near, at, beside[u + 1] * p), (far, at, g)]
            states.append((s, g))
        for ref, at, value in stores:
            ref[at] = value
        return tuple(states)

    half = cells // 2
    if carry is None:
        ones = jnp.ones((rows, 128), jnp.float32)
        return blocks(0, half, size, functools.partial(body, False), ((ones, ones), (ones, ones)))
    (_, g_f), (_, g_b) = blocks(half, cells, size, functools.partial(body, True), carry)
    for k, value in enumerate((near[plane(0, rows)], g_b, g_f, near[plane(cells - 1, rows)])):
        gains.put(k, value)


def sweep_values(rhs, links, cells, rows, fwd_p, bwd_p, value, ends, at=0):
    size = 4

    def body(keep, i, carry):
        y_f, y_b = carry
        stores = []
        for u in range(size):
            j = cells - 1 - i - u
            here, there = plane(i + u, rows), plane(j, rows)
            p_f, p_b = fwd_p[here], bwd_p[there]
            y_f = rhs[here] * p_f + (links[here] * p_f) * y_f
            y_b = rhs[there] * p_b + (links[plane(j + 1, rows)] * p_b) * y_b
            stores += [(here, y_f), (there, y_b)]
        if keep:
            for at, y in stores:
                value[at] = y
        return y_f, y_b

    half = cells // 2
    zeros = jnp.zeros((rows, 128), jnp.float32)
    carry = blocks(0, half, size, functools.partial(body, False), (zeros, zeros))
    y_f, y_b = blocks(half, cells, size, functools.partial(body, True), carry)
    ends.put(at, y_b)
    ends.put(at + 1, y_f)


def back_substitute(before, after, cells, rows, near, far, value, unroll, store):
    def lap(block, carry):
        low, high = carry
        lows, highs = [], []
        for u in range(unroll):
            i = block * unroll + u
            here, there = plane(i, rows), plane(cells - 1 - i, rows)
            low = (value[here] + far[here] * after) + near[here] * low
            high = (value[there] + far[there] * before) + near[there] * high
            lows.append(low)
            highs.append(high)
        store(block, lows, highs)
        return low, high

    lax.fori_loop(0, cells // 2 // unroll, lap, (before, after))


def remote(src, dst, send, recv, axis, to):
    return pltpu.make_async_remote_copy(
        src_ref=src, dst_ref=dst, send_sem=send, recv_sem=recv, device_id={axis: to}, device_id_type=MESH
    )


class Parcel:
    def __init__(self, system, refs):
        self.system = system
        self.stage, self.everyone, self.send_sem, self.recv_sem = refs

    def put(self, k, value):
        rows = self.system.rows
        for o in range(self.system.owners):
            self.stage[o, k] = value[o * rows : (o + 1) * rows]

    def copy(self, o):
        own = self.system
        return remote(
            self.stage.at[o], self.everyone.at[own.me], self.send_sem.at[o], self.recv_sem.at[own.me],
            own.axis, o * own.stride,
        )

    def send(self):
        own = self.system
        for o in range(own.owners):

            @pl.when(own.me != o * own.stride)
            def _():
                self.copy(o).start()

        @pl.when(own.mine)
        def _():
            self.everyone[own.me] = self.stage[own.group]

    def arrived(self):
        own = self.system
        for d in range(1, own.count):
            k = lax.rem(own.me + d, own.count)
            part = self.everyone.at[k]
            remote(part, part, self.recv_sem.at[k], self.recv_sem.at[k], own.axis, k).wait_recv()

    def drain(self):
        for o in range(self.system.owners):

            @pl.when(self.system.me != o * self.system.stride)
            def _():
                self.copy(o).wait_send()


class Reduced:
    def __init__(self, axis, rows, merged, refs):
        self.axis, self.count, self.me = axis, lax.axis_size(axis), lax.axis_index(axis)
        self.owners, self.rows = groups(self.count, rows)
        self.stride = self.count // self.owners
        self.mine = lax.rem(self.me, self.stride) == 0
        self.group = self.me // self.stride
        self.merged = merged
        self.gains = Parcel(self, refs[:4])
        self.ends = self.gains if merged else Parcel(self, refs[4:8])
        refs = refs[4 if merged else 8 :]
        self.relation, self.reply, self.sides, self.reply_send, self.reply_recv = refs
        self.shift = 4 if merged else 0

    def factor(self):
        @pl.when(self.mine)
        def _():
            self.gains.arrived()
            gain = jnp.zeros((self.rows, 128), jnp.float32)
            for k in range(self.count):
                head_west, head_east, tail_west, tail_east = (self.gains.everyone[k, v] for v in range(4))
                scale = inverse(1.0 - head_west * gain)
                beta, gamma = head_east * scale, tail_west * gain
                self.relation[k, 0], self.relation[k, 1] = scale, beta
                self.relation[k, 2], self.relation[k, 3] = gamma, gain
                gain = tail_east + gamma * beta

    def reply_copies(self):
        for member in range(self.stride):
            for d in range(1 if member == 0 else 0, self.owners):
                k = lax.rem(self.group + d, self.owners) * self.stride + member
                yield remote(
                    self.reply.at[k], self.sides.at[self.group],
                    self.reply_send.at[k], self.reply_recv.at[self.group], self.axis, k,
                )

    def solve(self):
        @pl.when(self.mine)
        def _():
            if not self.merged:
                self.ends.arrived()
            value = jnp.zeros((self.rows, 128), jnp.float32)
            alphas, values = [], []
            for k in range(self.count):
                values.append(value)
                scale, gamma = self.relation[k, 0], self.relation[k, 2]
                head_west, tail_west = self.gains.everyone[k, 0], self.gains.everyone[k, 2]
                alpha = (self.ends.everyone[k, self.shift] + head_west * value) * scale
                value = (self.ends.everyone[k, self.shift + 1] + tail_west * value) + gamma * alpha
                alphas.append(alpha)
            after = jnp.zeros((self.rows, 128), jnp.float32)
            for k in reversed(range(self.count)):
                self.reply[k, 1] = after
                after = alphas[k] + self.relation[k, 1] * after
                self.reply[k, 0] = values[k] + self.relation[k, 3] * after
            for copy in self.reply_copies():
                copy.start()
            self.sides[self.group] = self.reply[self.me]

    def result(self):
        for o in range(self.owners):

            @pl.when(self.me != o * self.stride)
            def _():
                part = self.sides.at[o]
                remote(
                    part, part, self.reply_recv.at[o], self.reply_recv.at[o], self.axis, o * self.stride
                ).wait_recv()

        whole = (self.owners * self.rows, 128)
        return self.sides[:, 0].reshape(whole), self.sides[:, 1].reshape(whole)

    def drain(self):
        @pl.when(self.mine)
        def _():
            for copy in self.reply_copies():
                copy.wait_send()


class Everywhere:
    def __init__(self, axis, refs):
        self.axis, self.count, self.me = axis, lax.axis_size(axis), lax.axis_index(axis)
        self.relation = refs[8]
        self.gains, self.ends = (Broadcast(self, refs[4 * k : 4 * k + 4]) for k in range(2))

    def factor(self):
        self.gains.arrived()
        gain = jnp.zeros(self.relation.shape[2:], jnp.float32)
        for k in range(self.count):
            head_west, head_east, tail_west, tail_east = (self.gains.everyone[k, v] for v in range(4))
            scale = inverse(1.0 - head_west * gain)
            beta, gamma = head_east * scale, tail_west * gain
            self.relation[k, 0], self.relation[k, 1] = scale, beta
            self.relation[k, 2], self.relation[k, 3] = gamma, gain
            gain = tail_east + gamma * beta

    def solve(self):
        self.ends.arrived()
        zeros = jnp.zeros(self.relation.shape[2:], jnp.float32)
        value, alphas, values = zeros, [], []
        for k in range(self.count):
            values.append(value)
            alpha = (self.ends.everyone[k, 0] + self.gains.everyone[k, 0] * value) * self.relation[k, 0]
            value = (self.ends.everyone[k, 1] + self.gains.everyone[k, 2] * value) + self.relation[k, 2] * alpha
            alphas.append(alpha)
        after, mine_before, mine_after = zeros, zeros, zeros
        for k in reversed(range(self.count)):
            here = self.me == k
            mine_after = jnp.where(here, after, mine_after)
            after = alphas[k] + self.relation[k, 1] * after
            mine_before = jnp.where(here, values[k] + self.relation[k, 3] * after, mine_before)
        return mine_before, mine_after


class Broadcast:
    def __init__(self, system, refs):
        self.system = system
        self.stage, self.everyone, self.send_sem, self.recv_sem = refs

    def put(self, k, value):
        self.stage[k] = value

    def copies(self):
        own = self.system
        for d in range(1, own.count):
            to = lax.rem(own.me + d, own.count)
            yield remote(
                self.stage, self.everyone.at[own.me], self.send_sem.at[to], self.recv_sem.at[own.me], own.axis, to
            )

    def send(self):
        for copy in self.copies():
            copy.start()
        self.everyone[self.system.me] = self.stage[...]

    def arrived(self):
        own = self.system
        for d in range(1, own.count):
            k = lax.rem(own.me + d, own.count)
            part = self.everyone.at[k]
            remote(part, part, self.recv_sem.at[k], self.recv_sem.at[k], own.axis, k).wait_recv()

    def drain(self):
        for copy in self.copies():
            copy.wait_send()


def everywhere_scratch(count, rows):
    dma = pltpu.SemaphoreType.DMA((count,))

    def vmem(*shape):
        return pltpu.VMEM(shape + (rows, 128), jnp.float32)

    return [vmem(4), vmem(count, 4), dma, dma, vmem(2), vmem(count, 2), dma, dma, vmem(count, 4)]


def groups(count, rows):
    owners = min(count, rows // ROWS)
    return owners, rows // owners


def reduced_scratch(count, rows, merged):
    owners, part = groups(count, rows)
    dma = pltpu.SemaphoreType.DMA

    def vmem(*shape):
        return pltpu.VMEM(shape + (part, 128), jnp.float32)

    scratch = []
    for values in (6,) if merged else (4, 2):
        scratch += [vmem(owners, values), vmem(count, values), dma((owners,)), dma((count,))]
    return scratch + [
        vmem(count, 4), vmem(count, 2), vmem(owners, 2), dma((count,)), dma((owners,)),
    ]


def kernel(X, Y, h_in, c_in, q_in, out, *scratch):
    Z = 128
    chunks = X * Y // 128
    (stage_x, stage_y, halo_x, halo_y, halo_send, halo_recv, force, link_x, link_y, link_z) = scratch[:10]
    fwd_x, bwd_x, near_x, far_x, value_x, fwd_y, bwd_y, near_y, far_y, value_y = scratch[10:20]
    first, up_z, piv_z, lag_z, lead_z, val_z, low_z, h, c, q, load_sem, delta, delta_sem = scratch[20:33]
    along_x = Reduced("gx", Y, False, scratch[33:46])
    along_y = Everywhere("gy", scratch[46:55])
    nx, ny, me_x, me_y = along_x.count, along_y.count, along_x.me, along_y.me

    part = X * Y // PARTS
    loads = [
        pltpu.make_async_copy(src.at[pl.ds(m * part, part)], dst.at[pl.ds(m * part, part)], load_sem.at[k, m])
        for k, (src, dst) in enumerate(((h_in, h), (c_in, c), (q_in, q)))
        for m in range(PARTS)
    ]
    for load in loads:
        load.start()
    barrier = pltpu.get_barrier_semaphore()
    for d in range(1, nx):
        pl.semaphore_signal(barrier, inc=1, device_id={"gx": lax.rem(me_x + d, nx)}, device_id_type=MESH)
    for d in range(1, ny):
        pl.semaphore_signal(barrier, inc=1, device_id={"gy": lax.rem(me_y + d, ny)}, device_id_type=MESH)

    for load in loads[: 2 * PARTS]:
        load.wait()

    def column(j):
        return pl.ds(j, X, stride=Y)

    for side, (i, j) in enumerate(((0, 0), (X - 1, Y - 1))):
        stage_x[side, 0], stage_x[side, 1] = h[plane(i, Y)], c[plane(i, Y)]
        stage_y[side, 0], stage_y[side, 1] = h[column(j), :], c[column(j), :]

    for load in loads[2 * PARTS :]:
        load.wait()

    def along_first(i, carry):
        head, cond, flux = carry
        stores = []
        for u in range(4):
            here, ahead = plane(i + u, Y), plane(jnp.minimum(i + u + 1, X - 1), Y)
            head_next, cond_next = h[ahead], c[ahead]
            east = link(COEF_X, cond, cond_next)
            flux_next = east * (head_next - head)
            stores += [(link_x, plane(i + u + 1, Y), east), (force, here, 2.0 * (flux_next - flux) + q[here])]
            head, cond, flux = head_next, cond_next, flux_next
        for ref, at, value in stores:
            ref[at] = value
        return head, cond, flux

    blocks(0, X, 4, along_first, (h[plane(0, Y)], c[plane(0, Y)], jnp.zeros((Y, 128), jnp.float32)))

    pl.semaphore_wait(barrier, nx - 1 + ny - 1)

    halos = []
    for a, (axis, me, count, stage, halo) in enumerate(
        (("gx", me_x, nx, stage_x, halo_x), ("gy", me_y, ny, stage_y, halo_y))
    ):
        for side in (0, 1):
            to = me - 1 if side == 0 else me + 1
            inside = me > 0 if side == 0 else me < count - 1
            send = pltpu.make_async_remote_copy(
                src_ref=stage.at[side], dst_ref=halo.at[1 - side],
                send_sem=halo_send.at[2 * a + side], recv_sem=halo_recv.at[2 * a + 1 - side],
                device_id={axis: to}, device_id_type=MESH,
            )
            take = pltpu.make_async_remote_copy(
                src_ref=stage.at[side], dst_ref=halo.at[side],
                send_sem=halo_send.at[2 * a + side], recv_sem=halo_recv.at[2 * a + side],
                device_id={axis: to}, device_id_type=MESH,
            )
            halos.append((inside, send, take))

            @pl.when(inside)
            def _():
                send.start()

            @pl.when(jnp.logical_not(inside))
            def _():
                halo[side] = jnp.zeros((2,) + halo.shape[2:], jnp.float32)

    inner = lax.broadcasted_iota(jnp.int32, (X, 128), 1) < Z - 1

    def depth_and_second(j, carry):
        head, cond, flux = carry
        stores = []
        for u in range(4):
            ahead = jnp.minimum(j + u + 1, Y - 1)
            head_next, cond_next = h[column(ahead), :], c[column(ahead), :]
            old = force[column(j + u), :]
            up = jnp.where(inner, link(COEF_Z, cond, pltpu.roll(cond, Z - 1, 1)), 0.0)
            rise = up * (pltpu.roll(head, Z - 1, 1) - head)
            north = link(COEF_Y, cond, cond_next)
            flux_next = north * (head_next - head)
            total = old + 2.0 * ((rise - pltpu.roll(rise, 1, 1)) + (flux_next - flux))
            stores.append((link_z, plane(j + u, X), up))
            stores.append((link_y, plane(j + u + 1, X), north))
            stores.append((force, column(j + u), total))
            head, cond, flux = head_next, cond_next, flux_next
        for ref, at, value in stores:
            ref[at, :] = value
        return head, cond, flux

    blocks(0, Y, 4, depth_and_second, (h[column(0), :], c[column(0), :], jnp.zeros((X, 128), jnp.float32)))

    for inside, _, take in halos:

        @pl.when(inside)
        def _():
            take.wait_recv()

    low = link(COEF_X, halo_x[0, 1], c[plane(0, Y)])
    high = link(COEF_X, halo_x[1, 1], c[plane(X - 1, Y)])
    link_x[plane(0, Y)], link_x[plane(X, Y)] = low, high
    force[plane(0, Y)] += 2.0 * (low * (halo_x[0, 0] - h[plane(0, Y)]))
    force[plane(X - 1, Y)] += 2.0 * (high * (halo_x[1, 0] - h[plane(X - 1, Y)]))
    low = link(COEF_Y, halo_y[0, 1], c[column(0), :])
    high = link(COEF_Y, halo_y[1, 1], c[column(Y - 1), :])
    link_y[plane(0, X)], link_y[plane(Y, X)] = low, high
    force[column(0), :] += 2.0 * (low * (halo_y[0, 0] - h[column(0), :]))
    force[column(Y - 1), :] += 2.0 * (high * (halo_y[1, 0] - h[column(Y - 1), :]))

    segment_x = (link_x, X, Y, fwd_x, bwd_x, near_x, far_x, along_x.gains)
    factor_segment(*segment_x, factor_segment(*segment_x))
    along_x.gains.send()
    sweep_values(force, link_x, X, Y, fwd_x, bwd_x, value_x, along_x.ends)
    along_x.ends.send()

    segment_y = (link_y, Y, X, fwd_y, bwd_y, near_y, far_y, along_y.gains)
    halfway = factor_segment(*segment_y)
    along_x.factor()
    along_x.solve()
    factor_segment(*segment_y, halfway)
    along_y.gains.send()

    before, after = along_x.result()

    def store_first(block, lows, highs):
        for u in range(4):
            i = block * 4 + u
            first[pl.ds(i, Y, stride=X), :] = lows[u]
            first[pl.ds(X - 1 - i, Y, stride=X), :] = highs[u]

    back_substitute(before, after, X, Y, near_x, far_x, value_x, 4, store_first)

    sweep_values(first, link_y, Y, X, fwd_y, bwd_y, value_y, along_y.ends)
    along_y.ends.send()
    along_y.factor()

    def turn_links(k, carry):
        for u in range(2):
            up_z[pl.ds(chunks + k + u, Z, stride=chunks), :] = link_z[plane(k + u, 128)].T
        return carry

    ones, zeros = (jnp.full((chunks, 128), v, jnp.float32) for v in (1.0, 0.0))
    up_z[plane(0, chunks)] = zeros
    blocks(0, chunks, 2, turn_links, 0)

    half = Z // 2

    def factor_z(i, carry):
        states, stores = [], []
        for s, (first_cell, way) in zip(carry, ((i, 1), (Z - 1 - i, -1))):
            edge = first_cell + (way < 0)
            beside = [up_z[plane(edge + way * u, chunks)] for u in range(9)]
            parts, s = pivots(beside, s)
            for u, p in enumerate(parts):
                at = plane(first_cell + way * u, chunks)
                stores += [(piv_z, at, p), (lag_z, at, beside[u] * p), (lead_z, at, beside[u + 1] * p)]
            states.append(s)
        for ref, at, value in stores:
            ref[at] = value
        return tuple(states)

    s_f, s_b = blocks(0, half, 8, factor_z, (ones, ones))
    middle = inverse(s_f + s_b * lead_z[plane(half - 1, chunks)])

    for system in (along_x, along_y):
        system.gains.drain()
    along_x.ends.drain()
    along_x.drain()
    for inside, send, _ in halos:

        @pl.when(inside)
        def _():
            send.wait_send()

    before, after = along_y.solve()
    per_chunk = 128 // X

    def store_second(block, lows, highs):
        val_z[pl.ds(block, Z, stride=chunks), :] = jnp.concatenate(lows, 0).T
        val_z[pl.ds(chunks - 1 - block, Z, stride=chunks), :] = jnp.concatenate(highs[::-1], 0).T

    back_substitute(before, after, Y, X, near_y, far_y, value_y, per_chunk, store_second)

    def sweep_z(i, carry):
        y_f, y_b = carry
        stores = []
        for u in range(8):
            here, there = plane(i + u, chunks), plane(Z - 1 - i - u, chunks)
            y_f = val_z[here] * piv_z[here] + lag_z[here] * y_f
            y_b = val_z[there] * piv_z[there] + lag_z[there] * y_b
            stores += [(here, y_f), (there, y_b)]
        for at, y in stores:
            low_z[at] = y
        return y_f, y_b

    y_f, y_b = blocks(0, half, 8, sweep_z, (zeros, zeros))
    below = (y_f + lead_z[plane(half - 1, chunks)] * y_b) * middle
    above = y_b + lead_z[plane(half, chunks)] * below

    def back_z(i, carry):
        low, high = carry
        stores = []
        for u in range(8):
            stores += [(plane(half - 1 - i - u, chunks), low), (plane(half + i + u, chunks), high)]
            nearer = plane(jnp.maximum(half - 2 - i - u, 0), chunks)
            farther = plane(jnp.minimum(half + 1 + i + u, Z - 1), chunks)
            low = low_z[nearer] + lead_z[nearer] * low
            high = low_z[farther] + lead_z[farther] * high
        for at, value in stores:
            delta[at] = value
        return low, high

    def give(k, start, stop):
        cells = pl.ds(start * chunks, (stop - start) * chunks)
        return pltpu.make_async_copy(delta.at[cells], out.at[cells], delta_sem.at[k])

    quarter = half // 2
    gives = [give(0, quarter, Z - quarter), give(1, 0, quarter), give(2, Z - quarter, Z)]
    carry = blocks(0, quarter, 8, back_z, (below, above))
    gives[0].start()
    blocks(quarter, half, 8, back_z, carry)
    gives[1].start()
    gives[2].start()

    along_y.ends.drain()
    for copy in gives:
        copy.wait()


def finish(X, Y, delta, h, out):
    chunks, per_chunk = X * Y // 128, 128 // X

    def write(k, carry):
        stores = []
        for u in range(2):
            lines = delta[pl.ds(k + u, 128, stride=chunks), :].T
            for part in range(per_chunk):
                at = pl.ds((k + u) * per_chunk + part, X, stride=Y)
                stores.append((at, h[at, :] + lines[part * X : (part + 1) * X]))
        for at, value in stores:
            out[at, :] = value
        return carry

    blocks(0, chunks, 2, write, 0)


def per_device(water_head, conductivity, recharge):
    X, Y, Z = water_head.shape
    nx, ny = lax.axis_size("gx"), lax.axis_size("gy")

    def vmem(*shape):
        return pltpu.VMEM(shape, jnp.float32)

    cells = X * Y
    chunks = cells // 128
    scratch = [
        vmem(2, 2, Y, Z), vmem(2, 2, X, Z), vmem(2, 2, Y, Z), vmem(2, 2, X, Z),
        pltpu.SemaphoreType.DMA((4,)), pltpu.SemaphoreType.DMA((4,)),
        vmem(cells, Z), vmem(cells + Y, Z), vmem(cells + X, Z), vmem(cells, Z),
    ]
    scratch += [vmem(cells, Z) for _ in range(11)] + [vmem(cells + chunks, Z)] + [vmem(cells, Z) for _ in range(8)] + [pltpu.SemaphoreType.DMA((3, PARTS)), vmem(cells, Z), pltpu.SemaphoreType.DMA((3,))]
    scratch += reduced_scratch(nx, Y, False) + everywhere_scratch(ny, X)
    flat = [array.reshape(cells, Z) for array in (water_head, conductivity, recharge)]
    delta = pl.pallas_call(
        functools.partial(kernel, X, Y),
        out_shape=jax.ShapeDtypeStruct((cells, Z), jnp.float32),
        in_specs=[pl.BlockSpec(memory_space=pl.ANY)] * 3,
        out_specs=pl.BlockSpec(memory_space=pl.ANY),
        scratch_shapes=scratch,
        compiler_params=pltpu.CompilerParams(
            collective_id=0, has_side_effects=True, vmem_limit_bytes=56 * 2**20
        ),
    )(*flat)
    result = pl.pallas_call(
        functools.partial(finish, X, Y),
        out_shape=jax.ShapeDtypeStruct((cells, Z), jnp.float32),
        in_specs=[pl.BlockSpec(memory_space=pltpu.VMEM)] * 2,
        out_specs=pl.BlockSpec(memory_space=pltpu.VMEM),
        compiler_params=pltpu.CompilerParams(vmem_limit_bytes=16 * 2**20),
    )(delta, flat[0])
    return result.reshape(X, Y, Z)


def solution(mesh):
    placed = (P("gx", "gy", None), P("gx", "gy", None), P("gx", "gy", None))
    return jax.shard_map(
        per_device, mesh=mesh, in_specs=placed, out_specs=P("gx", "gy", None), check_vma=False
    )
```
